32 devices in a mesh: owner: 8 (over z, core), tensor: 4 (over y, x).
Axes of the slice: x: 2, y: 2, z: 4, core: 2. Of those that a mesh axis runs over, the one named last changes fastest.
Arguments:
- mixer_input: bfloat16 [8192, 2, 8192], P('owner', None, 'tensor'), may hold values from -6 to 6
- step_raw: float32 [8192, 128], P('owner', 'tensor'), may hold values from -7 to 5
- decay_rate: float32 [128], P('tensor'), may hold values from 0.005 to 0.5
- skip_gain: float32 [128], P('tensor'), may hold values from 0.5 to 2
- state_proj: bfloat16 [8192, 2, 4, 256], P('owner'), may hold values from -1.5 to 1.5
- queries: bfloat16 [8192, 4096], P('owner', 'tensor'), may hold values from -256 to 256
- suffix_kv: bfloat16 [8192, 2, 4, 128], P('owner'), may hold values from -6 to 6
- state_pool: bfloat16 [32, 128, 64, 256], P('owner', 'tensor'), may hold values from -1.5 to 1.5
- page_pool: bfloat16 [128, 128, 2, 4, 128], P('owner'), may hold values from -6 to 6
- norm_gain: float32 [8192], P('tensor'), may hold values from 0.1 to 1.9
- hit_owner: int32 [32, 1], replicated, may hold values from 0 to 7; in each aligned block of 4 rows (0 to 3, 4 to 7, ...) at most 2 rows name the same one
- hit_slot: int32 [32], replicated, may hold values from 0 to 3
- page_owner: int32 [32, 16, 1], replicated, may hold values from 0 to 7; in each aligned block of 64 rows (0 to 63, 64 to 127, ..., all dimensions but the last counted through in order) at most 12 rows name the same one
- page_slot: int32 [32, 16], replicated, may hold values from 0 to 15
- prefix_len: int32 [32], replicated, may hold values from 256 to 2048, as said below
- suffix_len: int32 [32], replicated, may hold values from 64 to 256, as said below
Outputs:
- mamba_out: bfloat16 [8192, 8192], P('owner', 'tensor')
- attn_out: bfloat16 [8192, 4096], P('owner', 'tensor')
The draws below stay inside these ranges and needn't reach their ends.
Inputs may be any that keep to these rules, and one draw needn't show every extreme that they name: `hit_owner`: the 4 requests on one index of owner name one owner at most 2 times, and some index reaches it. `page_owner`: of the 64 list entries of the requests on one index of owner, at most 12 name one owner, and some index reaches it. `prefix_len`: a multiple of 256; request 0 has 2048. `suffix_len`: request 0 has 256.
All inputs are finite; a program needn't handle non-finite values.
Results may differ from the reference program's by a relative error of at most 0.0045.
Values may be sent and summed in bfloat16 or wider, within the bound.
No kernel may reach another device: no remote copies, remote signals or barrier semaphores. Data moves between devices by JAX's collectives and lax.ppermute only.
A program may use at most 256 MiB of HBM per device.

```python
import math
import jax
import jax.numpy as jnp
import numpy as np
from jax import lax

SSM_HEAD_TOTAL = 128
MHDIM = 64
STATE = 256
GROUPS = 4
QHEADS = 32
KVHEADS = 4
HD = 128
PAGE = 128
SPAN = 128
CKPT = 256
SUF = 256
PREFIX_MAX = 2048
REQ_DEV = 4
SLOTS_DEV = 4
PAGES_DEV = 16
CAP_S = 2
MAXP = 16
CAP_P = 12
REQS = 32
TRAILING_PLACES = 8192
SLOTS = 32
PAGES = 128
N_OWNER = 8


def draw_queries(key, part):
    start_shift = jnp.clip(jax.random.normal(key, (TRAILING_PLACES, QHEADS * HD), jnp.float32), -4.0, 4.0)
    return start_shift.astype(jnp.bfloat16)


def draw_step_raw(key, part):
    first_key, tiebreak_order = jax.random.split(key)
    start_shift = jnp.clip(jax.random.normal(first_key, (TRAILING_PLACES, SSM_HEAD_TOTAL), jnp.float32), -3.0, 3.0) - 2.5
    batch_lines = jax.random.randint(tiebreak_order, (TRAILING_PLACES, SSM_HEAD_TOTAL), 0, 48) == 0
    return (start_shift + jnp.where(batch_lines, 4.5, 0.0)).astype(jnp.float32)


def draw_prefix_len(key, part):
    counts = jax.random.randint(key, (REQS,), 1, PREFIX_MAX // CKPT + 1)
    counts = counts.at[0].set(PREFIX_MAX // CKPT)
    return (counts * CKPT).astype(jnp.int32)


def draw_suffix_len(key, part):
    lengths = jax.random.randint(key, (REQS,), SUF // 4, SUF + 1)
    lengths = lengths.at[0].set(SUF)
    return lengths.astype(jnp.int32)


def plant(values, own_key, low, high):
    longest = values.shape.index(max(values.shape))
    spots = []
    for shift in (0, 1):
        where = [jax.random.randint(jax.random.fold_in(own_key, axis), (), 0, length) for axis, length in enumerate(values.shape)]
        where[longest] = (where[longest] + shift) % values.shape[longest]
        spots.append(tuple(where))
    return values.at[spots[0]].set(low).at[spots[1]].set(high)


def shard_levels(key, shape, cuts, low, largest):
    def one(dim, blocks):
        draws = jax.random.uniform(jax.random.fold_in(jax.random.fold_in(key, 6), dim), (blocks,), jnp.float32, low / len(cuts), largest / len(cuts))
        return jnp.repeat(jnp.exp(draws), shape[dim] // blocks).reshape((-1,) + (1,) * (len(shape) - dim - 1))

    gain = one(*cuts[0])
    for cut in cuts[1:]:
        gain = gain * one(*cut)
    return gain


def shared_out(key, own, number, rows, count, top, bound, slope):
    sequence = jax.random.permutation(key, count)
    heavy_load, common = shares(count, rows * top, bound, slope, True), shares(count, rows * top, bound, slope, False)
    places = jnp.arange(count)

    def named(sizes, rotation):
        used = int((sizes > 0).sum())
        fixed = max(1, used // 4)
        shifted = fixed + (places - fixed + rotation * (used - fixed)) % max(1, count - fixed)
        return jnp.zeros((count,), jnp.int32).at[sequence[jnp.where(places < fixed, places, shifted)]].set(jnp.asarray(sizes, jnp.int32))

    sizes = jnp.where(number % 4 == 0, named(heavy_load, number // 4), named(common, number - number // 4 - 1))
    mixed = jax.random.permutation(jax.random.fold_in(own, 3), count)
    giver, receiver = mixed[0:count // 2 * 2:2], mixed[1:count // 2 * 2:2]
    margin = jnp.minimum(sizes[giver] - 1, bound - sizes[receiver]) // 2
    margin = jnp.where((giver == sequence[0]) | (receiver == sequence[0]) | (sizes[receiver] == 0), 0, jnp.maximum(margin, 0))
    shifted = jax.random.randint(jax.random.fold_in(own, 4), (count // 2,), 0, 1 << 20) % (margin + 1)
    sizes = sizes.at[giver].add(-shifted).at[receiver].add(shifted)
    labels = jnp.searchsorted(jnp.cumsum(sizes), jnp.arange(rows * top), side="right").astype(jnp.int32)
    table = labels.reshape(top, rows).T
    table = table[jax.random.permutation(jax.random.fold_in(own, 1), rows)]
    rotation = jax.random.randint(jax.random.fold_in(own, 2), (rows, 1), 0, top)
    return jnp.take_along_axis(table, (jnp.arange(top)[None, :] + rotation) % top, axis=1)


def shares(count, total, most, slope, full):
    weights = [(1 << 20) // math.isqrt(grade ** slope) + 1 for grade in range(1, count + 1)]
    largest = most if full else min(most, max(-(-total // count), total * weights[0] // sum(weights)))
    least = 1 if total - largest >= count - 1 else 0
    given, spare = [largest] + [least] * (count - 1), total - largest - least * (count - 1)
    while spare > 0:
        candidates = [i for i in range(1, count) if given[i] < largest] or [i for i in range(1, count) if given[i] < most]
        whole, left = sum([weights[i] for i in candidates]), spare
        for i in candidates:
            extra = min(most - given[i], max(1, left * weights[i] // whole), spare)
            given[i] = given[i] + extra
            spare = spare - extra
    return np.array(given)


def noise(own_key, shape, deviation, bound, cuts=(), kind=jnp.bfloat16):
    level = shard_levels(own_key, shape, cuts, -0.22, 0.18) if cuts else 1.0
    values = jax.random.normal(own_key, shape, jnp.float32) * deviation * level
    return jnp.minimum(jnp.maximum(values, -bound), bound).astype(kind)


def setup_inputs(seed: int = 0) -> dict:
    splits = jax.random.split(jax.random.key(seed), 17)
    mixer_input = noise(splits[0], (TRAILING_PLACES, 2, SSM_HEAD_TOTAL * MHDIM), 1.0, 6.0, ((0, 8), (2, 4)))
    step_raw = draw_step_raw(jax.random.fold_in(splits[16], 71), 0)
    decay_rate = jnp.clip(jnp.exp(math.log(0.5) - 4.6051702 * jax.random.uniform(splits[2], (SSM_HEAD_TOTAL,), jnp.float32) ** shard_levels(splits[2], (SSM_HEAD_TOTAL,), ((0, 4),), -0.2, 0.2)), 0.005, 0.5)
    skip_gain = jnp.clip(0.5 + 1.5 * jax.random.uniform(splits[3], (SSM_HEAD_TOTAL,), jnp.float32) ** shard_levels(splits[3], (SSM_HEAD_TOTAL,), ((0, 4),), -0.2, 0.2), 0.5, 2.0)
    state_proj = noise(splits[4], (TRAILING_PLACES, 2, GROUPS, STATE), 0.25, 1.5, ((0, 8),))
    queries = draw_queries(jax.random.fold_in(splits[16], 71), 0)
    suffix_kv = noise(splits[6], (TRAILING_PLACES, 2, KVHEADS, HD), 1.0, 6.0, ((0, 8),))
    state_pool = noise(splits[7], (SLOTS, SSM_HEAD_TOTAL, MHDIM, STATE), 0.25, 1.5, ((0, 8), (1, 4)))
    page_pool = noise(splits[8], (PAGES, PAGE, 2, KVHEADS, HD), 1.0, 6.0, ((0, 8),))
    norm_gain = jnp.clip(1.0 + 0.18 * jax.random.normal(splits[9], (SSM_HEAD_TOTAL * MHDIM,), jnp.float32), 0.1, 1.9)
    hit_owner_keys = jax.random.split(jax.random.fold_in(splits[10], 1), REQS // REQ_DEV)
    hit_owner_turns = jax.random.permutation(jax.random.fold_in(splits[10], 3), REQS // REQ_DEV)
    hit_owner = jax.vmap(lambda own, number: shared_out(jax.random.fold_in(splits[10], 2), own, number, REQ_DEV, N_OWNER, 1, CAP_S, 2))(hit_owner_keys, hit_owner_turns).reshape((REQS, 1))
    hit_slot = plant(jax.random.randint(splits[11], (REQS,), 0, SLOTS_DEV), jax.random.fold_in(splits[11], 1), 0, SLOTS_DEV - 1).astype(jnp.int32)
    page_owner_keys = jax.random.split(jax.random.fold_in(splits[12], 1), REQS * MAXP // (REQ_DEV * MAXP))
    page_owner_turns = jax.random.permutation(jax.random.fold_in(splits[12], 3), REQS * MAXP // (REQ_DEV * MAXP))
    page_owner = jax.vmap(lambda own, number: shared_out(jax.random.fold_in(splits[12], 2), own, number, REQ_DEV * MAXP, N_OWNER, 1, CAP_P, 2))(page_owner_keys, page_owner_turns).reshape((REQS, MAXP, 1))
    page_slot = plant(jax.random.randint(splits[13], (REQS, MAXP), 0, PAGES_DEV), jax.random.fold_in(splits[13], 1), 0, PAGES_DEV - 1).astype(jnp.int32)
    prefix_len = draw_prefix_len(jax.random.fold_in(splits[16], 71), 0)
    suffix_len = draw_suffix_len(jax.random.fold_in(splits[16], 71), 0)
    return {"mixer_input": mixer_input, "step_raw": step_raw, "decay_rate": decay_rate, "skip_gain": skip_gain, "state_proj": state_proj, "queries": queries, "suffix_kv": suffix_kv, "state_pool": state_pool, "page_pool": page_pool, "norm_gain": norm_gain, "hit_owner": hit_owner, "hit_slot": hit_slot, "page_owner": page_owner, "page_slot": page_slot, "prefix_len": prefix_len, "suffix_len": suffix_len}


EPSILON = 1e-05
NEG_FILL = -1e+30

def half(value):
    return lax.optimization_barrier(value.astype(jnp.bfloat16)).astype(jnp.float32)

def mixer_core(x_heads, z_heads, rate_raw, decay_groups, skip_groups, b_rows, c_rows, start_state):
    seq_len, group_count, head_count, head_width = x_heads.shape
    blocks = seq_len // SPAN
    step_rate = jax.nn.softplus(rate_raw)
    keep_log = -step_rate * decay_groups[None]
    x_block = x_heads.reshape(blocks, SPAN, group_count, head_count, head_width).astype(jnp.float32)
    rate_block = step_rate.reshape(blocks, SPAN, group_count, head_count)
    cum_block = jnp.cumsum(keep_log.reshape(blocks, SPAN, group_count, head_count), axis=1)
    b_block = b_rows.reshape(blocks, SPAN, group_count, -1).astype(jnp.float32)
    c_block = c_rows.reshape(blocks, SPAN, group_count, -1).astype(jnp.float32)
    intersection = jnp.einsum('cign,cjgn->cgij', c_block, b_block)
    cum_moved = jnp.transpose(cum_block, (0, 2, 3, 1))
    rate_moved = jnp.transpose(rate_block, (0, 2, 3, 1))
    lower = jnp.arange(SPAN)[:, None] >= jnp.arange(SPAN)[None, :]
    fade = jnp.exp(jnp.where(lower, cum_moved[..., :, None] - cum_moved[..., None, :], NEG_FILL))
    weights = half(intersection[:, :, None] * fade * rate_moved[..., None, :])
    inner = jnp.einsum('cghij,cjghp->cighp', weights, x_block)
    cum_end = cum_block[:, -1]
    tail = jnp.exp(cum_end[:, None] - cum_block) * rate_block
    scaled = half(tail[..., None] * x_block)
    block_state = jnp.einsum('cjghp,cjgn->cghpn', scaled, b_block)
    carry = start_state.astype(jnp.float32)
    begins = []
    for block_index in range(blocks):
        begins.append(carry)
        carry = jnp.exp(cum_end[block_index])[..., None, None] * carry + block_state[block_index]
    begin_half = half(jnp.stack(begins))
    carried = jnp.einsum('cign,cghpn->cighp', c_block, begin_half)
    summed = inner + jnp.exp(cum_block)[..., None] * carried + skip_groups[None, None, :, :, None] * x_block
    gate = jax.nn.silu(z_heads.astype(jnp.float32)).reshape(blocks, SPAN, group_count, head_count, head_width)
    return (summed * gate).reshape(seq_len, group_count, head_count, head_width)

def attend(query, key_pre, value_pre, key_suf, value_suf, prefix_count):
    softmax_scale = 1.0 / math.sqrt(HD)
    query_wide = query.astype(jnp.float32)
    score_pre = jnp.einsum('qhd,md->hqm', query_wide, key_pre.astype(jnp.float32)) * softmax_scale
    score_suf = jnp.einsum('qhd,kd->hqk', query_wide, key_suf.astype(jnp.float32)) * softmax_scale
    pre_live = jnp.arange(key_pre.shape[0]) < prefix_count
    causal = jnp.arange(SUF)[:, None] >= jnp.arange(SUF)[None, :]
    score_pre = jnp.where(pre_live[None, None, :], score_pre, NEG_FILL)
    score_suf = jnp.where(causal[None], score_suf, NEG_FILL)
    row_max = jnp.maximum(lax.optimization_barrier(jnp.max(score_pre, axis=2)), lax.optimization_barrier(jnp.max(score_suf, axis=2)))
    weight_pre = jnp.exp(score_pre - row_max[..., None])
    weight_suf = jnp.exp(score_suf - row_max[..., None])
    denominator = lax.optimization_barrier(jnp.sum(weight_pre, axis=2)) + lax.optimization_barrier(jnp.sum(weight_suf, axis=2))
    mixed = jnp.einsum('hqm,md->qhd', half(weight_pre), value_pre.astype(jnp.float32))
    mixed = mixed + jnp.einsum('hqk,kd->qhd', half(weight_suf), value_suf.astype(jnp.float32))
    return mixed / jnp.transpose(denominator)[:, :, None]

def reference(mixer_input, step_raw, decay_rate, skip_gain, state_proj, queries, suffix_kv, state_pool, page_pool, norm_gain, hit_owner, hit_slot, page_owner, page_slot, prefix_len, suffix_len):
    per_group = SSM_HEAD_TOTAL // GROUPS
    per_kv = QHEADS // KVHEADS
    decay_groups = decay_rate.reshape(GROUPS, per_group)
    skip_groups = skip_gain.reshape(GROUPS, per_group)
    gain_groups = norm_gain.reshape(GROUPS, per_group, MHDIM)
    positions = jnp.arange(SUF)

    def one_request(request):
        first_row = (request * SUF).astype(jnp.int32)
        rows_input = lax.dynamic_slice_in_dim(mixer_input, first_row, SUF, 0)
        x_heads = rows_input[:, 0].reshape(SUF, GROUPS, per_group, MHDIM)
        z_heads = rows_input[:, 1].reshape(SUF, GROUPS, per_group, MHDIM)
        rate_raw = lax.dynamic_slice_in_dim(step_raw, first_row, SUF, 0).reshape(SUF, GROUPS, per_group)
        line_targets = lax.dynamic_slice_in_dim(state_proj, first_row, SUF, 0)
        start_index = (hit_owner[request, 0] * SLOTS_DEV + hit_slot[request]).astype(jnp.int32)
        start_state = lax.dynamic_index_in_dim(state_pool, start_index, 0, keepdims=False)
        start_state = start_state.reshape(GROUPS, per_group, MHDIM, STATE)
        gated = mixer_core(x_heads, z_heads, rate_raw, decay_groups, skip_groups, line_targets[:, 0], line_targets[:, 1], start_state)
        square = lax.optimization_barrier(jnp.sum(gated * gated, axis=(2, 3))) / (per_group * MHDIM)
        rescaled_input = gated * lax.rsqrt(square + EPSILON)[:, :, None, None] * gain_groups[None]
        active = positions < suffix_len[request]
        mamba_rows = jnp.where(active[:, None], rescaled_input.reshape(SUF, SSM_HEAD_TOTAL * MHDIM), 0.0).astype(jnp.bfloat16)
        page_index = (page_owner[request, :, 0] * PAGES_DEV + page_slot[request]).astype(jnp.int32)
        prefix_kv = jnp.take(page_pool, page_index, axis=0).reshape(MAXP * PAGE, 2, KVHEADS, HD)
        rows_kv = lax.dynamic_slice_in_dim(suffix_kv, first_row, SUF, 0)
        query = lax.dynamic_slice_in_dim(queries, first_row, SUF, 0).reshape(SUF, KVHEADS, per_kv, HD)
        mixed = jax.vmap(attend, in_axes=(1, 1, 1, 1, 1, None), out_axes=1)(query, prefix_kv[:, 0], prefix_kv[:, 1], rows_kv[:, 0], rows_kv[:, 1], prefix_len[request])
        attn_rows = jnp.where(active[:, None], mixed.reshape(SUF, QHEADS * HD), 0.0).astype(jnp.bfloat16)
        return (mamba_rows, attn_rows)
    mamba_all, attn_all = lax.map(one_request, jnp.arange(REQS, dtype=jnp.int32))
    return (mamba_all.reshape(TRAILING_PLACES, SSM_HEAD_TOTAL * MHDIM), attn_all.reshape(TRAILING_PLACES, QHEADS * HD))
```

```python
import functools
import math

import jax
import jax.numpy as jnp
import numpy as np
from jax import lax
from jax.experimental import pallas as pl
from jax.experimental.pallas import tpu as pltpu
from jax.sharding import PartitionSpec as P

SSM_HEAD_TOTAL = 128
MHDIM = 64
STATE = 256
GROUPS = 4
QHEADS = 32
KVHEADS = 4
HD = 128
PAGE = 128
SPAN = 128
SUF = 256
MAXP = 16
SLOTS_DEV = 4
PAGES_DEV = 16

EPSILON = 1e-05
NEG_FILL = -1e30
LAG = 2
FIXED_STEPS = 7
VMEM = 48 * 1024 * 1024

NT = (((1,), (1,)), ((), ()))
TN = (((0,), (0,)), ((), ()))


def mm(a, b, dims=(((1,), (0,)), ((), ()))):
    return lax.dot_general(a, b, dims, preferred_element_type=jnp.float32)


def route_kernel(chips, per_chip, reqs_per_chip, cap, ids_ref, here_ref, out_ref, need_ref, tab_ref):
    states = chips * per_chip
    here = here_ref[0]

    def clear(s, carry):
        need_ref[s] = 0
        return carry

    lax.fori_loop(0, states, clear, 0)

    def mark(r, carry):
        s = ids_ref[r]
        need_ref[s] = need_ref[s] | (1 << (r // reqs_per_chip))
        return carry

    lax.fori_loop(0, chips * reqs_per_chip, mark, 0)

    steps = jnp.int32(0)
    lengths = []
    for up in (True, False):
        side = []
        for place in range(chips - 1):
            chip = place if up else chips - 1 - place
            base = ((0 if up else chips) + chip) * cap
            before = base - cap if up else base + cap

            def wanted(s, chip=chip, up=up):
                if up:
                    return (need_ref[s] >> (chip + 1)) != 0
                return (need_ref[s] & ((1 << chip) - 1)) != 0

            def own(i, t, chip=chip, base=base, wanted=wanted):
                s = chip * per_chip + i
                tab_ref[base + t] = s
                return t + wanted(s).astype(jnp.int32)

            t = lax.fori_loop(0, per_chip, own, jnp.int32(0))
            if place:

                def forward(j, t, base=base, before=before, wanted=wanted):
                    s = tab_ref[before + j]
                    take = (s < states) & wanted(jnp.minimum(s, states - 1))
                    later = jnp.where(take, jnp.maximum(t, j + LAG), t)

                    def gap(i, carry):
                        tab_ref[base + i] = states
                        return carry

                    lax.fori_loop(t, later, gap, 0)
                    tab_ref[base + later] = s
                    return later + take.astype(jnp.int32)

                t = lax.fori_loop(0, side[-1], forward, t)
            side.append(t)
            steps = jnp.maximum(steps, t)
        lengths.append(side)

    def length_of(side, place):
        total = jnp.int32(0)
        for i, length in enumerate(side):
            total = jnp.where(place == i, length, total)
        return total

    down_place = chips - 1 - here
    bounds = (
        (length_of(lengths[0], here), here * cap),
        (length_of(lengths[0], here - 1), (here - 1) * cap),
        (length_of(lengths[1], down_place), (chips + here) * cap),
        (length_of(lengths[1], down_place - 1), (chips + here + 1) * cap),
    )
    for row, (length, base) in enumerate(bounds):

        def put(t, carry, row=row, length=length, base=base):
            spot = jnp.clip(base + t, 0, 2 * chips * cap - 1)
            out_ref[row * cap + t] = jnp.where(t < length, tab_ref[spot], states)
            return carry

        lax.fori_loop(0, cap, put, 0)
    out_ref[4 * cap] = steps


def route(state_ids, chip, chips, per_chip, reqs_per_chip):
    cap = chips * per_chip + LAG * chips + 8
    smem = pl.BlockSpec(memory_space=pltpu.SMEM)
    table = pl.pallas_call(
        functools.partial(route_kernel, chips, per_chip, reqs_per_chip, cap),
        out_shape=jax.ShapeDtypeStruct((4 * cap + 8,), jnp.int32),
        in_specs=[smem, smem],
        out_specs=smem,
        scratch_shapes=[
            pltpu.SMEM((chips * per_chip,), jnp.int32),
            pltpu.SMEM((2 * chips * cap,), jnp.int32),
        ],
        name="route_states",
    )(state_ids, chip.reshape(1))
    return table, cap


def mamba_pre_kernel(
    heads,
    mix_ref,
    b_ref,
    c_ref,
    cum_col_ref,
    rate_col_ref,
    cum_row_ref,
    rate_row_ref,
    skip_ref,
    spread_ref,
    split_ref,
    _pre_in,
    _z_in,
    _e_in,
    pre_ref,
    z_ref,
    e_ref,
    bs_ref,
    end_ref,
):
    block = pl.program_id(1)
    width = heads * MHDIM
    both = mm(split_ref[...], mix_ref[...])
    z_ref[...] = both[SPAN:].astype(jnp.bfloat16)
    x = both[:SPAN]
    x_half = x.astype(jnp.bfloat16)
    b = b_ref[...]
    c = c_ref[...]
    cross = mm(c, b, NT)
    row = lax.broadcasted_iota(jnp.int32, (SPAN, SPAN), 0)
    lane = lax.broadcasted_iota(jnp.int32, (SPAN, SPAN), 1)
    lower = row >= lane
    left = lane < MHDIM
    cum = cum_col_ref[...]

    def three_way(value):
        high = value.astype(jnp.bfloat16)
        rest = value - high.astype(jnp.float32)
        middle = rest.astype(jnp.bfloat16)
        low = (rest - middle.astype(jnp.float32)).astype(jnp.bfloat16)
        high, middle, low = (v.astype(jnp.float32) for v in (high, middle, low))
        kept = jnp.where(
            lane < heads,
            high,
            jnp.where(lane < 2 * heads, middle, jnp.where(lane < 3 * heads, low, 0.0)),
        )
        return kept.astype(jnp.bfloat16)

    def weights(h):
        fall = cum[:, h : h + 1] - cum_row_ref[h : h + 1, :]
        fade = jnp.exp(jnp.where(lower, fall, NEG_FILL))
        return (cross * fade * rate_row_ref[h : h + 1, :]).astype(jnp.bfloat16)

    for pair in range(heads // 2):
        cols = slice(pair * 2 * MHDIM, (pair + 1) * 2 * MHDIM)
        xp = x_half[:, cols]
        zero = jnp.zeros_like(xp)
        stacked = jnp.concatenate([jnp.where(left, xp, zero), jnp.where(left, zero, xp)], axis=0)
        w = jnp.concatenate([weights(2 * pair), weights(2 * pair + 1)], axis=1)
        pre_ref[:, cols] = mm(w, stacked) + skip_ref[:, cols] * x[:, cols]

    @pl.when(block == 0)
    def _():
        end = cum[SPAN - 1 : SPAN, :]
        tail = jnp.exp(end - cum) * rate_col_ref[...]
        scaled = (mm(three_way(tail), spread_ref[...]) * x).astype(jnp.bfloat16)
        bs_ref[...] = mm(scaled, b, TN).astype(jnp.bfloat16)
        end_ref[...] = jnp.broadcast_to(end, end_ref.shape)
        e_ref[...] = three_way(jnp.exp(cum))

    @pl.when(block == 1)
    def _():
        e_half = three_way(jnp.exp(cum))
        carried = mm(c, bs_ref[...], NT)
        pre_ref[...] += mm(e_half, spread_ref[...]) * carried
        e_ref[...] = three_way(jnp.exp(cum + end_ref[0:1, :]))


def mamba_pre(heads, first, count, mixed, b_rows, c_rows, cum_col, rate_col, cum_row, rate_row, skip, spread, split, carry):
    width = heads * MHDIM
    rows = b_rows.shape[0]

    def at(r, k):
        return ((first + r) * 2 + k, 0)

    def fixed(r, k):
        return (0, 0)

    blocks = count * 2
    outs = [
        jax.ShapeDtypeStruct((rows, width), jnp.float32),
        jax.ShapeDtypeStruct((rows, width), jnp.bfloat16),
        jax.ShapeDtypeStruct((rows, 128), jnp.bfloat16),
    ]
    out_specs = [
        pl.BlockSpec((SPAN, width), at),
        pl.BlockSpec((SPAN, width), at),
        pl.BlockSpec((SPAN, 128), at),
    ]
    if carry is None:
        carry = tuple(jnp.zeros((16, 128), jnp.float32) for _ in outs)
        aliases = {}
    else:
        aliases = {10: 0, 11: 1, 12: 2}
    anywhere = pl.BlockSpec(memory_space=pl.ANY)
    return pl.pallas_call(
        functools.partial(mamba_pre_kernel, heads),
        grid=(count, 2),
        out_shape=outs,
        in_specs=[
            pl.BlockSpec((2 * SPAN, width), at),
            pl.BlockSpec((SPAN, STATE), at),
            pl.BlockSpec((SPAN, STATE), at),
            pl.BlockSpec((SPAN, 128), at),
            pl.BlockSpec((SPAN, 128), at),
            pl.BlockSpec((heads, SPAN), lambda r, k: (0, (first + r) * 2 + k)),
            pl.BlockSpec((heads, SPAN), lambda r, k: (0, (first + r) * 2 + k)),
            pl.BlockSpec((1, width), fixed),
            pl.BlockSpec((128, width), fixed),
            pl.BlockSpec((2 * SPAN, 2 * SPAN), fixed),
            anywhere,
            anywhere,
            anywhere,
        ],
        out_specs=out_specs,
        scratch_shapes=[
            pltpu.VMEM((width, STATE), jnp.bfloat16),
            pltpu.VMEM((8, 128), jnp.float32),
        ],
        input_output_aliases=aliases,
        compiler_params=pltpu.CompilerParams(vmem_limit_bytes=VMEM),
        cost_estimate=pl.CostEstimate(
            flops=blocks * heads * 40 * SPAN * SPAN * MHDIM,
            bytes_accessed=blocks * SPAN * width * 10,
            transcendentals=blocks * heads * SPAN * SPAN,
        ),
        name="mamba_pre",
    )(mixed, b_rows, c_rows, cum_col, rate_col, cum_row, rate_row, skip, spread, split, *carry)


def mamba_post_kernel(
    heads,
    whole_group,
    ids_ref,
    live_ref,
    core_ref,
    c_ref,
    mine_ref,
    other_ref,
    pre_ref,
    z_ref,
    e_ref,
    spread_ref,
    gain_ref,
    out_ref,
    *rest,
):
    r = pl.program_id(0)
    half = heads * MHDIM // 2
    gated_ref = rest[-1]
    c = c_ref[...]
    e = e_ref[...]
    square = jnp.zeros((SUF, 1), jnp.float32)
    for which, state_ref in enumerate((mine_ref, other_ref)):
        core = core_ref[0] if which == 0 else 1 - core_ref[0]
        cols = pl.ds(pl.multiple_of(core * half, 128), half)
        carried = mm(c, state_ref[0], NT)
        summed = pre_ref[:, cols] + mm(e, spread_ref[:, cols]) * carried
        z = z_ref[:, cols].astype(jnp.float32)
        gated = summed * (z / (1.0 + jnp.exp(-z)))
        gated_ref[:, cols] = gated
        square += jnp.sum(gated * gated, axis=1, keepdims=True)
    if whole_group:
        norm = lax.rsqrt(square / (heads * MHDIM) + EPSILON)
        live = lax.broadcasted_iota(jnp.int32, (SUF, 1), 0) < live_ref[r]
        value = gated_ref[...] * norm * gain_ref[...]
        out_ref[...] = jnp.where(live, value, 0.0).astype(out_ref.dtype)
    else:
        out_ref[...] = gated_ref[...]
        rest[0][...] = jnp.broadcast_to(square, (SUF, 128))


def mamba_post(heads, whole_group, ids, live, core, c_rows, store, other, pre, z, e3, spread, gain):
    width = heads * MHDIM
    half = width // 2
    rows = c_rows.shape[0]
    count = rows // SUF

    def at(r, *_):
        return (r, 0)

    def fixed(r, *_):
        return (0, 0)

    out_shape = [jax.ShapeDtypeStruct((rows, width), jnp.bfloat16 if whole_group else jnp.float32)]
    out_specs = [pl.BlockSpec((SUF, width), at)]
    if not whole_group:
        out_shape.append(jax.ShapeDtypeStruct((rows, 128), jnp.float32))
        out_specs.append(pl.BlockSpec((SUF, 128), at))
    return pl.pallas_call(
        functools.partial(mamba_post_kernel, heads, whole_group),
        grid_spec=pltpu.PrefetchScalarGridSpec(
            num_scalar_prefetch=3,
            grid=(count,),
            in_specs=[
                pl.BlockSpec((SUF, STATE), at),
                pl.BlockSpec((1, half, STATE), lambda r, ids, live, core: (ids[r], 0, 0)),
                pl.BlockSpec((1, half, STATE), lambda r, *_: (r, 0, 0)),
                pl.BlockSpec((SUF, width), at),
                pl.BlockSpec((SUF, width), at),
                pl.BlockSpec((SUF, 128), at),
                pl.BlockSpec((128, width), fixed),
                pl.BlockSpec((1, width), fixed),
            ],
            out_specs=out_specs,
            scratch_shapes=[pltpu.VMEM((SUF, width), jnp.float32)],
        ),
        out_shape=out_shape,
        compiler_params=pltpu.CompilerParams(vmem_limit_bytes=VMEM),
        cost_estimate=pl.CostEstimate(
            flops=2 * rows * width * STATE,
            bytes_accessed=rows * width * 12,
            transcendentals=rows * width,
        ),
        name="mamba_post",
    )(ids, live, core, c_rows, store, other, pre, z, e3, spread, gain)


def attend_kernel(
    first, pages_ref, prefix_ref, live_ref, q_ref, ks_ref, vs_ref, pool_ref, _out_in, out_ref, kv_ref, s_ref, sem
):
    r = pl.program_id(0)
    head = pl.program_id(1)
    request = first + r
    scale = math.log2(math.e) / math.sqrt(HD)
    pairs = prefix_ref[request] // (2 * PAGE)

    @pl.when(head == 0)
    def _():
        def begin(p, carry):
            for kv in range(2):
                pltpu.make_async_copy(
                    pool_ref.at[pages_ref[request * MAXP + p], kv],
                    kv_ref.at[kv, pl.ds(pl.multiple_of(p * PAGE, PAGE), PAGE)],
                    sem,
                ).start()
            return carry

        def finish(p, carry):
            for kv in range(2):
                pltpu.make_async_copy(
                    pool_ref.at[pages_ref[request * MAXP + p], kv],
                    kv_ref.at[kv, pl.ds(pl.multiple_of(p * PAGE, PAGE), PAGE)],
                    sem,
                ).wait()
            return carry

        lax.fori_loop(0, 2 * pairs, begin, 0)
        lax.fori_loop(0, 2 * pairs, finish, 0)

    q = q_ref[...]
    row = lax.broadcasted_iota(jnp.int32, (SUF, SUF), 0)
    lane = lax.broadcasted_iota(jnp.int32, (SUF, SUF), 1)
    own = jnp.where(row >= lane, mm(q, ks_ref[...], NT), NEG_FILL)
    top = jnp.maximum(own[:, :HD], own[:, HD:])

    def scores(i, top):
        at = pl.ds(pl.multiple_of(i * 2 * PAGE, 2 * PAGE), 2 * PAGE)
        s = mm(q, kv_ref[0, at], NT)
        s_ref[i] = s
        return jnp.maximum(top, jnp.maximum(s[:, :HD], s[:, HD:]))

    top = lax.fori_loop(0, pairs, scores, top)
    top = jnp.max(top, axis=1, keepdims=True)
    probs = jnp.exp2((own - top) * scale)
    total = probs[:, :HD] + probs[:, HD:]
    mixed = mm(probs.astype(jnp.bfloat16), vs_ref[...])

    def values(i, carry):
        total, mixed = carry
        at = pl.ds(pl.multiple_of(i * 2 * PAGE, 2 * PAGE), 2 * PAGE)
        probs = jnp.exp2((s_ref[i] - top) * scale)
        total = total + (probs[:, :HD] + probs[:, HD:])
        return total, mixed + mm(probs.astype(jnp.bfloat16), kv_ref[1, at])

    total, mixed = lax.fori_loop(0, pairs, values, (total, mixed))
    total = jnp.sum(total, axis=1, keepdims=True)
    live = lax.broadcasted_iota(jnp.int32, (SUF, 1), 0) < live_ref[request]
    out_ref[...] = jnp.where(live, mixed / total, 0.0).astype(out_ref.dtype)


def attention(qheads, first, count, pages, prefix, live, queries, keys, values, pool, carry):
    rows = queries.shape[0]
    most = MAXP * PAGE // SUF
    if carry is None:
        carry = jnp.zeros((16, 128), jnp.bfloat16)
        aliases = {}
    else:
        aliases = {7: 0}
    anywhere = pl.BlockSpec(memory_space=pl.ANY)
    return pl.pallas_call(
        functools.partial(attend_kernel, first),
        grid_spec=pltpu.PrefetchScalarGridSpec(
            num_scalar_prefetch=3,
            grid=(count, qheads),
            in_specs=[
                pl.BlockSpec((SUF, HD), lambda r, h, *_: (first + r, h)),
                pl.BlockSpec((SUF, HD), lambda r, h, *_: (first + r, 0)),
                pl.BlockSpec((SUF, HD), lambda r, h, *_: (first + r, 0)),
                anywhere,
                anywhere,
            ],
            out_specs=pl.BlockSpec((SUF, HD), lambda r, h, *_: (first + r, h)),
            scratch_shapes=[
                pltpu.VMEM((2, MAXP * PAGE, HD), jnp.bfloat16),
                pltpu.VMEM((most, SUF, 2 * PAGE), jnp.float32),
                pltpu.SemaphoreType.DMA,
            ],
        ),
        out_shape=jax.ShapeDtypeStruct(queries.shape, jnp.bfloat16),
        input_output_aliases=aliases,
        compiler_params=pltpu.CompilerParams(vmem_limit_bytes=VMEM),
        cost_estimate=pl.CostEstimate(
            flops=count * qheads * SUF * (MAXP * PAGE + SUF) * HD * 4,
            bytes_accessed=count * (SUF * qheads * HD * 4 + MAXP * PAGE * HD * 4),
            transcendentals=count * qheads * SUF * (MAXP * PAGE + SUF),
        ),
        name="attention",
    )(pages, prefix, live, queries, keys, values, pool, carry)


def body(
    mixer_input,
    step_raw,
    decay_rate,
    skip_gain,
    state_proj,
    queries,
    suffix_kv,
    state_pool,
    page_pool,
    norm_gain,
    hit_owner,
    hit_slot,
    page_owner,
    page_slot,
    prefix_len,
    suffix_len,
):
    owners = lax.axis_size("owner")
    owner = lax.axis_index("owner")
    column = lax.axis_index("tensor")
    rows = mixer_input.shape[0]
    count = rows // SUF
    heads = decay_rate.shape[0]
    width = heads * MHDIM
    qheads = queries.shape[1] // HD
    per_group = SSM_HEAD_TOTAL // GROUPS
    group = column * heads // per_group
    kv_index = column * qheads // (QHEADS // KVHEADS)
    whole_group = heads == per_group
    chips = owners // 2
    chip = owner // 2
    core = owner % 2
    first = owner * count
    per_chip = 2 * SLOTS_DEV
    states = owners * SLOTS_DEV
    half_heads = heads // 2

    up = [(o, o + 2) for o in range(owners - 2)]
    down = [(o + 2, o) for o in range(owners - 2)]
    swap = [(o, o ^ 1) for o in range(owners)]

    own_pages = lax.dynamic_index_in_dim(page_pool, kv_index, 3, keepdims=False)
    own_pages = jnp.transpose(own_pages, (0, 2, 1, 3))
    pool = jnp.zeros((owners + 1,) + own_pages.shape, jnp.bfloat16)

    def keep_pages(pool, piece, index, valid):
        spot = jnp.where(valid, index, owners)
        return lax.dynamic_update_index_in_dim(pool, piece, spot, 0)

    pieces = [(own_pages, owner, owner >= 0)]
    going_up, going_down = own_pages, own_pages
    for hop in range(1, chips):
        going_up = lax.ppermute(going_up, "owner", [p for p in up if p[0] // 2 >= hop - 1])
        going_down = lax.ppermute(going_down, "owner", [p for p in down if p[0] // 2 <= chips - hop])
        pieces.append((going_up, owner - 2 * hop, chip >= hop))
        pieces.append((going_down, owner + 2 * hop, chip + hop < chips))

    state_ids = (hit_owner[:, 0] * SLOTS_DEV + hit_slot).astype(jnp.int32)
    table, cap = route(state_ids, chip.astype(jnp.int32), chips, per_chip, 2 * count)

    shape = (SLOTS_DEV, half_heads, MHDIM, STATE)
    mine = lax.dynamic_slice_in_dim(state_pool, core * half_heads, half_heads, 1)
    theirs = lax.dynamic_slice_in_dim(state_pool, (1 - core) * half_heads, half_heads, 1)
    arrived = lax.ppermute(theirs, "owner", swap)
    store = jnp.zeros((states + 1, half_heads * MHDIM, STATE), jnp.bfloat16)
    store = lax.dynamic_update_slice_in_dim(
        store, mine.reshape(SLOTS_DEV, -1, STATE), owner * SLOTS_DEV, 0
    )
    store = lax.dynamic_update_slice_in_dim(
        store, arrived.reshape(SLOTS_DEV, -1, STATE), (owner + 1 - 2 * core) * SLOTS_DEV, 0
    )

    def send(store, t):
        above = lax.ppermute(
            lax.dynamic_index_in_dim(store, table[t], 0, keepdims=False), "owner", up
        )
        below = lax.ppermute(
            lax.dynamic_index_in_dim(store, table[2 * cap + t], 0, keepdims=False), "owner", down
        )
        return above, below

    def keep(store, got, t):
        store = lax.dynamic_update_index_in_dim(store, got[0], table[cap + t], 0)
        return lax.dynamic_update_index_in_dim(store, got[1], table[3 * cap + t], 0)

    waiting = None
    for t in range(FIXED_STEPS):
        got = send(store, t)
        if waiting is not None:
            store = keep(store, waiting, t - 1)
        waiting = got
    store = keep(store, waiting, FIXED_STEPS - 1)

    rate = jax.nn.softplus(step_raw.T)
    fall = (-rate * decay_rate[:, None]).reshape(heads, rows // SPAN, SPAN)
    cum_row = jnp.cumsum(fall, axis=2).reshape(heads, rows)
    copies = 128 // heads
    cum_col = jnp.tile(cum_row.T, (1, copies))
    rate_col = jnp.tile(rate.T, (1, copies))
    skip = jnp.repeat(skip_gain, MHDIM)[None, :]
    spread_np = np.zeros((128, width), np.float32)
    for h in range(heads):
        for k in range(3):
            spread_np[k * heads + h, h * MHDIM : (h + 1) * MHDIM] = 1.0
    spread = jnp.asarray(spread_np, jnp.bfloat16)
    split_np = np.zeros((2 * SPAN, 2 * SPAN), np.float32)
    for i in range(SPAN):
        split_np[i, 2 * i] = 1.0
        split_np[SPAN + i, 2 * i + 1] = 1.0
    split = jnp.asarray(split_np, jnp.bfloat16)
    mixed = mixer_input.reshape(2 * rows, width)
    maps = lax.dynamic_index_in_dim(state_proj, group, 2, keepdims=False)
    b_rows, c_rows = maps[:, 0], maps[:, 1]
    made = None
    for r in range(0, count, 2):
        made = mamba_pre(
            heads, r, 2, mixed, b_rows, c_rows, cum_col, rate_col, cum_row, rate, skip, spread, split, made
        )
    pre, z, e3 = made

    for piece, index, valid in pieces:
        pool = keep_pages(pool, piece, index, valid)
        other = lax.ppermute(piece, "owner", swap)
        pool = keep_pages(pool, other, index + 1 - 2 * core, valid)
    pool = pool.reshape((owners + 1) * PAGES_DEV, 2, PAGE, HD)
    page_ids = (page_owner[:, :, 0] * PAGES_DEV + page_slot).astype(jnp.int32)
    my_pages = lax.dynamic_slice_in_dim(page_ids, first, count, 0).reshape(-1)
    my_prefix = lax.dynamic_slice_in_dim(prefix_len, first, count, 0)
    my_suffix = lax.dynamic_slice_in_dim(suffix_len, first, count, 0)
    suffix = lax.dynamic_index_in_dim(suffix_kv, kv_index, 2, keepdims=False)
    attn_out = None
    for r in range(count):
        attn_out = attention(
            qheads, r, 1, my_pages, my_prefix, my_suffix, queries, suffix[:, 0], suffix[:, 1], pool, attn_out
        )

    def more(t, store):
        return keep(store, send(store, t), t)

    store = lax.fori_loop(FIXED_STEPS, table[4 * cap], more, store)

    my_ids = lax.dynamic_slice_in_dim(state_ids, first, count, 0)
    their_ids = lax.dynamic_slice_in_dim(state_ids, first + (1 - 2 * core) * count, count, 0)
    partner = jnp.take(store, their_ids, axis=0, mode="clip")
    other = lax.ppermute(partner, "owner", swap)
    result = mamba_post(
        heads,
        whole_group,
        my_ids,
        my_suffix,
        core.astype(jnp.int32).reshape(1),
        c_rows,
        store,
        other,
        pre,
        z,
        e3,
        spread,
        norm_gain[None, :],
    )
    if whole_group:
        return (result[0], attn_out)
    gated, partial_sum = result
    partial_sum = partial_sum[:, 0]
    spread_sum = jnp.where(jnp.arange(GROUPS)[:, None] == group, partial_sum[None, :], 0.0)
    totals = lax.psum(spread_sum, "tensor")
    square = lax.dynamic_index_in_dim(totals, group, 0, keepdims=False) / (per_group * MHDIM)
    active = (jnp.arange(SUF)[None, :] < my_suffix[:, None]).reshape(-1)
    scaled = gated * lax.rsqrt(square + EPSILON)[:, None] * norm_gain[None, :]
    return (jnp.where(active[:, None], scaled, 0.0).astype(jnp.bfloat16), attn_out)


def solution(mesh):
    return jax.shard_map(
        body,
        mesh=mesh,
        in_specs=(
            P("owner", None, "tensor"),
            P("owner", "tensor"),
            P("tensor"),
            P("tensor"),
            P("owner", None, None, None),
            P("owner", "tensor"),
            P("owner", None, None, None),
            P("owner", "tensor"),
            P("owner", None, None, None, None),
            P("tensor"),
            P(),
            P(),
            P(),
            P(),
            P(),
            P(),
        ),
        out_specs=(P("owner", "tensor"), P("owner", "tensor")),
        check_vma=False,
    )
```

```python
import functools
import math

import jax
import jax.numpy as jnp
import numpy as np
from jax import lax
from jax.experimental import pallas as pl
from jax.experimental.pallas import tpu as pltpu
from jax.sharding import PartitionSpec as P

SSM_HEAD_TOTAL = 128
MHDIM = 64
STATE = 256
GROUPS = 4
QHEADS = 32
KVHEADS = 4
HD = 128
PAGE = 128
SPAN = 128
SUF = 256
MAXP = 16
SLOTS_DEV = 4
PAGES_DEV = 16

EPSILON = 1e-05
NEG_FILL = -1e30
LAG = 2
FIXED_STEPS = 8
VMEM = 48 * 1024 * 1024

NT = (((1,), (1,)), ((), ()))
TN = (((0,), (0,)), ((), ()))


def mm(a, b, dims=(((1,), (0,)), ((), ()))):
    return lax.dot_general(a, b, dims, preferred_element_type=jnp.float32)


def route_kernel(chips, per_chip, reqs_per_chip, cap, ids_ref, here_ref, out_ref, need_ref, tab_ref):
    states = chips * per_chip
    chip_here = here_ref[0] // 2
    core_here = here_ref[0] % 2

    def clear(s, carry):
        need_ref[s] = 0
        return carry

    lax.fori_loop(0, states, clear, 0)

    def mark(r, carry):
        s = ids_ref[r]
        need_ref[s] = need_ref[s] | (1 << (r // reqs_per_chip))
        return carry

    lax.fori_loop(0, chips * reqs_per_chip, mark, 0)

    def put(base, length, row):
        def one(t, carry):
            spot = jnp.clip(base + t, 0, 2 * chips * cap - 1)
            out_ref[row * cap + t] = jnp.where(t < length, tab_ref[spot], states)
            return carry

        lax.fori_loop(0, cap, one, 0)

    steps = jnp.int32(0)
    for up in (True, False):
        before = jnp.int32(0)
        sent = jnp.int32(0)
        came = jnp.int32(0)
        for place in range(chips - 1):
            chip = place if up else chips - 1 - place
            base = ((0 if up else chips) + place) * cap

            def wanted(s, chip=chip, up=up):
                if up:
                    return (need_ref[s] >> (chip + 1)) != 0
                return (need_ref[s] & ((1 << chip) - 1)) != 0

            def own(i, t, chip=chip, base=base, wanted=wanted):
                s = chip * per_chip + i
                tab_ref[base + t] = s
                return t + wanted(s).astype(jnp.int32)

            t = lax.fori_loop(0, per_chip, own, jnp.int32(0))
            if place:

                def forward(j, t, base=base, wanted=wanted):
                    s = tab_ref[base - cap + j]
                    take = (s < states) & wanted(jnp.minimum(s, states - 1))
                    later = jnp.where(take, jnp.maximum(t, j + LAG), t)

                    def gap(i, carry):
                        tab_ref[base + i] = states
                        return carry

                    lax.fori_loop(t, later, gap, 0)
                    tab_ref[base + later] = s
                    return later + take.astype(jnp.int32)

                t = lax.fori_loop(0, before, forward, t)
            before = t
            sent = jnp.where(chip_here == chip, t, sent)
            came = jnp.where(chip_here == (chip + 1 if up else chip - 1), t, came)
            steps = jnp.maximum(steps, t)
        here = chip_here if up else chips - 1 - chip_here
        side = 0 if up else chips

        @pl.when(core_here == (0 if up else 1))
        def _(here=here, side=side, sent=sent, came=came):
            put((side + here) * cap, sent, 0)
            put((side + here - 1) * cap, came, 1)

    out_ref[2 * cap] = steps


def route(state_ids, owner, chips, per_chip, reqs_per_chip):
    cap = chips * per_chip + LAG * chips + 8
    smem = pl.BlockSpec(memory_space=pltpu.SMEM)
    table = pl.pallas_call(
        functools.partial(route_kernel, chips, per_chip, reqs_per_chip, cap),
        out_shape=jax.ShapeDtypeStruct((2 * cap + 8,), jnp.int32),
        in_specs=[smem, smem],
        out_specs=smem,
        scratch_shapes=[
            pltpu.SMEM((chips * per_chip,), jnp.int32),
            pltpu.SMEM((2 * chips * cap,), jnp.int32),
        ],
        name="route_states",
    )(state_ids, owner.reshape(1))
    return table, cap


def start_from(state, owner, pool_ref, near_ref, others, dst, sem):
    place = state // SLOTS_DEV
    slot = state % SLOTS_DEV
    in_pool = place == owner
    in_near = place == (owner ^ 1)

    @pl.when(in_pool)
    def _():
        pltpu.make_async_copy(pool_ref.at[slot], dst, sem).start()

    @pl.when(in_near)
    def _():
        pltpu.make_async_copy(near_ref.at[slot], dst, sem).start()

    for holds, ref in others:

        @pl.when(jnp.logical_not(in_pool | in_near) & holds)
        def _(ref=ref):
            pltpu.make_async_copy(ref, dst, sem).start()


ANYWHERE = pl.BlockSpec(memory_space=pl.ANY)


def first_kernel(cap, states, here_ref, table_ref, pool_ref, near_ref, *rest):
    sends, sem = rest[:-1], rest[-1]
    for t, send in enumerate(sends):
        state = table_ref[t]

        @pl.when(state < states)
        def _(state=state, send=send, t=t):
            start_from(state, here_ref[0], pool_ref, near_ref, (), send, sem.at[t])
            pltpu.make_async_copy(pool_ref.at[0], send, sem.at[t]).wait()


def first_sends(cap, states, here, table, pool, near):
    item = jax.ShapeDtypeStruct(pool.shape[1:], pool.dtype)
    return pl.pallas_call(
        functools.partial(first_kernel, cap, states),
        grid_spec=pltpu.PrefetchScalarGridSpec(
            num_scalar_prefetch=2,
            grid=(1,),
            in_specs=[ANYWHERE, ANYWHERE],
            out_specs=[ANYWHERE] * LAG,
            scratch_shapes=[pltpu.SemaphoreType.DMA((LAG,))],
        ),
        out_shape=[item] * LAG,
        name="first_sends",
    )(here, table, pool, near)


def turn_kernel(
    cap, states, sending, here_ref, table_ref, step_ref, pool_ref, near_ref, got_ref, _store_in, store_ref, *rest
):
    sem = rest[-1]
    step = step_ref[0]
    came = table_ref[cap + step - LAG]

    @pl.when(came < states)
    def _():
        pltpu.make_async_copy(got_ref, store_ref.at[came], sem.at[0]).start()

    if sending:
        send_ref = rest[0]
        state = table_ref[step]

        @pl.when(state < states)
        def _():
            spot = jnp.minimum(state, states - 1)
            start_from(
                state,
                here_ref[0],
                pool_ref,
                near_ref,
                ((state == came, got_ref), (state != came, store_ref.at[spot])),
                send_ref,
                sem.at[1],
            )
            pltpu.make_async_copy(got_ref, send_ref, sem.at[1]).wait()

    @pl.when(came < states)
    def _():
        pltpu.make_async_copy(got_ref, store_ref.at[came], sem.at[0]).wait()


def turn(cap, states, sending, here, table, step, pool, near, got, store):
    item = jax.ShapeDtypeStruct(pool.shape[1:], pool.dtype)
    kept = jax.ShapeDtypeStruct((states + 1,) + pool.shape[1:], pool.dtype)
    aliases = {} if store is None else {6: 0}
    if store is None:
        store = jnp.zeros((16, 128), jnp.float32)
    return pl.pallas_call(
        functools.partial(turn_kernel, cap, states, sending),
        grid_spec=pltpu.PrefetchScalarGridSpec(
            num_scalar_prefetch=3,
            grid=(1,),
            in_specs=[ANYWHERE] * 4,
            out_specs=[ANYWHERE] * (1 + sending),
            scratch_shapes=[pltpu.SemaphoreType.DMA((2,))],
        ),
        out_shape=[kept, item][: 1 + sending],
        input_output_aliases=aliases,
        name="turn_states",
    )(here, table, step, pool, near, got, store)


def take_kernel(states, here_ref, table_ref, step_ref, pool_ref, near_ref, store_ref, send_ref, sem):
    state = table_ref[step_ref[0]]

    @pl.when(state < states)
    def _():
        spot = jnp.minimum(state, states - 1)
        start_from(state, here_ref[0], pool_ref, near_ref, ((state < states, store_ref.at[spot]),), send_ref, sem)
        pltpu.make_async_copy(pool_ref.at[0], send_ref, sem).wait()


def take_out(states, here, table, step, pool, near, store):
    return pl.pallas_call(
        functools.partial(take_kernel, states),
        grid_spec=pltpu.PrefetchScalarGridSpec(
            num_scalar_prefetch=3,
            grid=(1,),
            in_specs=[ANYWHERE] * 3,
            out_specs=ANYWHERE,
            scratch_shapes=[pltpu.SemaphoreType.DMA],
        ),
        out_shape=jax.ShapeDtypeStruct(pool.shape[1:], pool.dtype),
        name="take_state",
    )(here, table, step, pool, near, store)


def pick_kernel(count, here_ref, ids_ref, store_ref, out_ref, sem):
    owner = here_ref[0]
    chip = owner // 2
    core = owner % 2
    for r in range(count):
        state = ids_ref[(owner ^ 1) * count + r]
        place = state // (2 * SLOTS_DEV)
        held = jnp.where(core == 0, place < chip, place > chip)

        @pl.when(held)
        def _(state=state, r=r):
            pltpu.make_async_copy(store_ref.at[state], out_ref.at[r], sem.at[r]).start()

    for r in range(count):
        state = ids_ref[(owner ^ 1) * count + r]
        place = state // (2 * SLOTS_DEV)
        held = jnp.where(core == 0, place < chip, place > chip)

        @pl.when(held)
        def _(state=state, r=r):
            pltpu.make_async_copy(store_ref.at[state], out_ref.at[r], sem.at[r]).wait()


def pick(count, here, ids, store):
    return pl.pallas_call(
        functools.partial(pick_kernel, count),
        grid_spec=pltpu.PrefetchScalarGridSpec(
            num_scalar_prefetch=2,
            grid=(1,),
            in_specs=[ANYWHERE],
            out_specs=ANYWHERE,
            scratch_shapes=[pltpu.SemaphoreType.DMA((count,))],
        ),
        out_shape=jax.ShapeDtypeStruct((count,) + store.shape[1:], store.dtype),
        name="pick_states",
    )(here, ids, store)


def mamba_pre_kernel(
    heads,
    live_ref,
    first_ref,
    mix_ref,
    b_ref,
    c_ref,
    step_ref,
    decay_ref,
    skip_ref,
    spread_ref,
    split_ref,
    _pre_in,
    _z_in,
    _e_in,
    pre_ref,
    z_ref,
    e_ref,
    bs_ref,
    end_ref,
):
    block = pl.program_id(1)
    request = first_ref[0] + pl.program_id(0)
    copies = SPAN // heads
    row = lax.broadcasted_iota(jnp.int32, (SPAN, SPAN), 0)
    lane = lax.broadcasted_iota(jnp.int32, (SPAN, SPAN), 1)
    lower = row >= lane
    left = lane < MHDIM

    def three_way(value):
        high = value.astype(jnp.bfloat16)
        rest = value - high.astype(jnp.float32)
        middle = rest.astype(jnp.bfloat16)
        low = (rest - middle.astype(jnp.float32)).astype(jnp.bfloat16)
        high, middle, low = (v.astype(jnp.float32) for v in (high, middle, low))
        kept = jnp.where(
            lane < heads,
            high,
            jnp.where(lane < 2 * heads, middle, jnp.where(lane < 3 * heads, low, 0.0)),
        )
        return kept.astype(jnp.bfloat16)

    @pl.when((block == 0) | (live_ref[request] > SPAN))
    def _():
        raw = step_ref[...]
        rate_row = jnp.maximum(raw, 0.0) + jnp.log1p(jnp.exp(-jnp.abs(raw)))
        upper = jnp.where(row <= lane, 1.0, 0.0)
        cum_row = lax.dot_general(
            -rate_row * decay_ref[...],
            upper,
            (((1,), (0,)), ((), ())),
            precision=lax.Precision.HIGHEST,
            preferred_element_type=jnp.float32,
        )
        cum = jnp.concatenate([cum_row] * copies, axis=0).T
        rate_col = jnp.concatenate([rate_row] * copies, axis=0).T

        both = mm(split_ref[...], mix_ref[...])
        z_ref[...] = both[SPAN:].astype(jnp.bfloat16)
        x = both[:SPAN]
        x_half = x.astype(jnp.bfloat16)
        b = b_ref[...]
        c = c_ref[...]
        cross = mm(c, b, NT)

        def weights(h):
            fall = cum[:, h : h + 1] - cum_row[h : h + 1, :]
            fade = jnp.exp(jnp.where(lower, fall, NEG_FILL))
            return (cross * fade * rate_row[h : h + 1, :]).astype(jnp.bfloat16)

        for pair in range(heads // 2):
            cols = slice(pair * 2 * MHDIM, (pair + 1) * 2 * MHDIM)
            xp = x_half[:, cols]
            zero = jnp.zeros_like(xp)
            stacked = jnp.concatenate([jnp.where(left, xp, zero), jnp.where(left, zero, xp)], axis=0)
            w = jnp.concatenate([weights(2 * pair), weights(2 * pair + 1)], axis=1)
            pre_ref[:, cols] = mm(w, stacked) + skip_ref[:, cols] * x[:, cols]

        @pl.when(block == 0)
        def _():
            end = cum[SPAN - 1 : SPAN, :]
            tail = jnp.exp(end - cum) * rate_col
            scaled = (mm(three_way(tail), spread_ref[...]) * x).astype(jnp.bfloat16)
            bs_ref[...] = mm(scaled, b, TN).astype(jnp.bfloat16)
            end_ref[...] = jnp.broadcast_to(end, end_ref.shape)
            e_ref[...] = three_way(jnp.exp(cum))

        @pl.when(block == 1)
        def _():
            e_half = three_way(jnp.exp(cum))
            carried = mm(c, bs_ref[...], NT)
            pre_ref[...] += mm(e_half, spread_ref[...]) * carried
            e_ref[...] = three_way(jnp.exp(cum + end_ref[0:1, :]))


def mamba_pre(heads, first, count, live, here, mixed, b_rows, c_rows, step_row, decay, skip, spread, split, carry):
    width = heads * MHDIM
    rows = b_rows.shape[0]

    def at(r, k, *_):
        return ((first + r) * 2 + k, 0)

    def fixed(r, k, *_):
        return (0, 0)

    blocks = count * 2
    outs = [
        jax.ShapeDtypeStruct((rows, width), jnp.float32),
        jax.ShapeDtypeStruct((rows, width), jnp.bfloat16),
        jax.ShapeDtypeStruct((rows, 128), jnp.bfloat16),
    ]
    if carry is None:
        carry = tuple(jnp.zeros((16, 128), jnp.float32) for _ in outs)
        aliases = {}
    else:
        aliases = {10: 0, 11: 1, 12: 2}
    return pl.pallas_call(
        functools.partial(mamba_pre_kernel, heads),
        grid_spec=pltpu.PrefetchScalarGridSpec(
            num_scalar_prefetch=2,
            grid=(count, 2),
            in_specs=[
                pl.BlockSpec((2 * SPAN, width), at),
                pl.BlockSpec((SPAN, STATE), at),
                pl.BlockSpec((SPAN, STATE), at),
                pl.BlockSpec((heads, SPAN), lambda r, k, *_: (0, (first + r) * 2 + k)),
                pl.BlockSpec((heads, SPAN), fixed),
                pl.BlockSpec((1, width), fixed),
                pl.BlockSpec((128, width), fixed),
                pl.BlockSpec((2 * SPAN, 2 * SPAN), fixed),
                ANYWHERE,
                ANYWHERE,
                ANYWHERE,
            ],
            out_specs=[
                pl.BlockSpec((SPAN, width), at),
                pl.BlockSpec((SPAN, width), at),
                pl.BlockSpec((SPAN, 128), at),
            ],
            scratch_shapes=[
                pltpu.VMEM((width, STATE), jnp.bfloat16),
                pltpu.VMEM((8, 128), jnp.float32),
            ],
        ),
        out_shape=outs,
        input_output_aliases=aliases,
        compiler_params=pltpu.CompilerParams(vmem_limit_bytes=VMEM),
        cost_estimate=pl.CostEstimate(
            flops=blocks * heads * 40 * SPAN * SPAN * MHDIM,
            bytes_accessed=blocks * SPAN * width * 10,
            transcendentals=blocks * heads * SPAN * SPAN,
        ),
        name="mamba_pre",
    )(live, here + first, mixed, b_rows, c_rows, step_row, decay, skip, spread, split, *carry)


def mamba_post_kernel(
    heads,
    whole_group,
    count,
    here_ref,
    ids_ref,
    live_ref,
    pool_ref,
    near_ref,
    store_ref,
    other_ref,
    c_ref,
    pre_ref,
    z_ref,
    e_ref,
    spread_ref,
    gain_ref,
    out_ref,
    *rest,
):
    r = pl.program_id(0)
    width = heads * MHDIM
    state_ref, sem = rest[-2:]
    owner = here_ref[0]
    chip = owner // 2
    core = owner % 2

    def fetch(r):
        state = ids_ref[owner * count + r]
        place = state // (2 * SLOTS_DEV)
        mine = jnp.where(core == 0, place < chip, place > chip)
        slot = r % 2
        start_from(
            state,
            owner,
            pool_ref,
            near_ref,
            ((mine, store_ref.at[state]), (jnp.logical_not(mine), other_ref.at[r])),
            state_ref.at[slot],
            sem.at[slot],
        )

    @pl.when(r == 0)
    def _():
        fetch(r)

    @pl.when(r + 1 < count)
    def _():
        fetch(r + 1)

    pltpu.make_async_copy(pool_ref.at[0], state_ref.at[r % 2], sem.at[r % 2]).wait()
    c = c_ref[...]
    e = e_ref[...]
    carried = mm(c, state_ref[r % 2], NT)
    summed = pre_ref[...] + mm(e, spread_ref[...]) * carried
    z = z_ref[...].astype(jnp.float32)
    gated = summed * (z / (1.0 + jnp.exp(-z)))
    square = jnp.sum(gated * gated, axis=1, keepdims=True)
    if whole_group:
        norm = lax.rsqrt(square / width + EPSILON)
        live = lax.broadcasted_iota(jnp.int32, (SUF, 1), 0) < live_ref[owner * count + r]
        out_ref[...] = jnp.where(live, gated * norm * gain_ref[...], 0.0).astype(out_ref.dtype)
    else:
        out_ref[...] = gated
        rest[0][...] = jnp.broadcast_to(square, (SUF, 128))


def mamba_post(heads, whole_group, here, ids, live, pool, near, store, other, c_rows, pre, z, e3, spread, gain):
    width = heads * MHDIM
    rows = c_rows.shape[0]
    count = rows // SUF

    def at(r, *_):
        return (r, 0)

    def fixed(r, *_):
        return (0, 0)

    out_shape = [jax.ShapeDtypeStruct((rows, width), jnp.bfloat16 if whole_group else jnp.float32)]
    out_specs = [pl.BlockSpec((SUF, width), at)]
    if not whole_group:
        out_shape.append(jax.ShapeDtypeStruct((rows, 128), jnp.float32))
        out_specs.append(pl.BlockSpec((SUF, 128), at))
    return pl.pallas_call(
        functools.partial(mamba_post_kernel, heads, whole_group, count),
        grid_spec=pltpu.PrefetchScalarGridSpec(
            num_scalar_prefetch=3,
            grid=(count,),
            in_specs=[
                ANYWHERE,
                ANYWHERE,
                ANYWHERE,
                ANYWHERE,
                pl.BlockSpec((SUF, STATE), at),
                pl.BlockSpec((SUF, width), at),
                pl.BlockSpec((SUF, width), at),
                pl.BlockSpec((SUF, 128), at),
                pl.BlockSpec((128, width), fixed),
                pl.BlockSpec((1, width), fixed),
            ],
            out_specs=out_specs,
            scratch_shapes=[
                pltpu.VMEM((2, width, STATE), jnp.bfloat16),
                pltpu.SemaphoreType.DMA((2,)),
            ],
        ),
        out_shape=out_shape,
        compiler_params=pltpu.CompilerParams(vmem_limit_bytes=VMEM),
        cost_estimate=pl.CostEstimate(
            flops=2 * rows * width * STATE,
            bytes_accessed=rows * width * 12,
            transcendentals=rows * width,
        ),
        name="mamba_post",
    )(here, ids, live, pool, near, store, other, c_rows, pre, z, e3, spread, gain)


def attend_kernel(
    qheads,
    first_ref,
    pages_ref,
    prefix_ref,
    live_ref,
    q_ref,
    ks_ref,
    vs_ref,
    pool_ref,
    _out_in,
    out_ref,
    kv_ref,
    s_ref,
    top_ref,
    total_ref,
    mixed_ref,
    sem,
):
    half = pl.program_id(1)
    request = first_ref[0] + pl.program_id(0)
    scale = math.log2(math.e) / math.sqrt(HD)
    pairs = prefix_ref[request] // (2 * PAGE)

    @pl.when(half == 0)
    def _():
        def copy(p, kv):
            return pltpu.make_async_copy(
                pool_ref.at[pages_ref[request * MAXP + p], kv],
                kv_ref.at[kv, pl.ds(pl.multiple_of(p * PAGE, PAGE), PAGE)],
                sem,
            )

        def begin(p, carry):
            copy(p, 0).start()
            copy(p, 1).start()
            return carry

        def finish(p, carry):
            copy(p, 0).wait()
            copy(p, 1).wait()
            return carry

        lax.fori_loop(0, 2 * pairs, begin, 0)
        lax.fori_loop(0, 2 * pairs, finish, 0)

    start = half * SPAN
    live = live_ref[request]

    def columns(h):
        return slice(h * HD, (h + 1) * HD)

    def fold(s):
        return jnp.maximum(s[:, :HD], s[:, HD:])

    @pl.when(start < live)
    def _():
        row = lax.broadcasted_iota(jnp.int32, (SPAN, SUF), 0) + start
        lane = lax.broadcasted_iota(jnp.int32, (SPAN, SUF), 1)
        causal = row >= lane
        for h in range(qheads):
            s = jnp.where(causal, mm(q_ref[:, columns(h)], ks_ref[...], NT), NEG_FILL)
            s_ref[0, h] = s
            top_ref[h] = fold(s)

        def scores(i, carry):
            keys = kv_ref[0, pl.ds(pl.multiple_of(i * 2 * PAGE, 2 * PAGE), 2 * PAGE)]
            for h in range(qheads):
                s = mm(q_ref[:, columns(h)], keys, NT)
                s_ref[i + 1, h] = s
                top_ref[h] = jnp.maximum(top_ref[h], fold(s))
            return carry

        lax.fori_loop(0, pairs, scores, 0)

        def weigh(h, s, values):
            probs = jnp.exp2((s - jnp.concatenate([top_ref[h]] * 2, axis=1)) * scale)
            return probs[:, :HD] + probs[:, HD:], mm(probs.astype(jnp.bfloat16), values)

        for h in range(qheads):
            top_ref[h] = jnp.broadcast_to(jnp.max(top_ref[h], axis=1, keepdims=True), (SPAN, HD))
        for h in range(qheads):
            total_ref[h], mixed_ref[h] = weigh(h, s_ref[0, h], vs_ref[...])

        def values(i, carry):
            rows = kv_ref[1, pl.ds(pl.multiple_of(i * 2 * PAGE, 2 * PAGE), 2 * PAGE)]
            for h in range(qheads):
                total, mixed = weigh(h, s_ref[i + 1, h], rows)
                total_ref[h] += total
                mixed_ref[h] += mixed
            return carry

        lax.fori_loop(0, pairs, values, 0)
        keep = lax.broadcasted_iota(jnp.int32, (SPAN, 1), 0) + start < live
        for h in range(qheads):
            total = jnp.sum(total_ref[h], axis=1, keepdims=True)
            out_ref[:, columns(h)] = jnp.where(keep, mixed_ref[h] / total, 0.0).astype(out_ref.dtype)

    @pl.when(start >= live)
    def _():
        out_ref[...] = jnp.zeros_like(out_ref)


def attention(qheads, first, count, here, pages, prefix, live, queries, keys, values, pool, carry):
    most = MAXP // 2 + 1
    width = qheads * HD
    if carry is None:
        carry = jnp.zeros((16, 128), jnp.bfloat16)
        aliases = {}
    else:
        aliases = {8: 0}

    def at(r, k, *_):
        return ((first + r) * 2 + k, 0)

    return pl.pallas_call(
        functools.partial(attend_kernel, qheads),
        grid_spec=pltpu.PrefetchScalarGridSpec(
            num_scalar_prefetch=4,
            grid=(count, 2),
            in_specs=[
                pl.BlockSpec((SPAN, width), at),
                pl.BlockSpec((SUF, HD), lambda r, k, *_: (first + r, 0)),
                pl.BlockSpec((SUF, HD), lambda r, k, *_: (first + r, 0)),
                ANYWHERE,
                ANYWHERE,
            ],
            out_specs=pl.BlockSpec((SPAN, width), at),
            scratch_shapes=[
                pltpu.VMEM((2, MAXP * PAGE, HD), jnp.bfloat16),
                pltpu.VMEM((most, qheads, SPAN, 2 * PAGE), jnp.float32),
                pltpu.VMEM((qheads, SPAN, HD), jnp.float32),
                pltpu.VMEM((qheads, SPAN, HD), jnp.float32),
                pltpu.VMEM((qheads, SPAN, HD), jnp.float32),
                pltpu.SemaphoreType.DMA,
            ],
        ),
        out_shape=jax.ShapeDtypeStruct(queries.shape, jnp.bfloat16),
        input_output_aliases=aliases,
        compiler_params=pltpu.CompilerParams(vmem_limit_bytes=VMEM),
        cost_estimate=pl.CostEstimate(
            flops=count * qheads * SUF * (MAXP * PAGE + SUF) * HD * 4,
            bytes_accessed=count * (SUF * qheads * HD * 4 + MAXP * PAGE * HD * 4),
            transcendentals=count * qheads * SUF * (MAXP * PAGE + SUF),
        ),
        name="attention",
    )(here + first, pages, prefix, live, queries, keys, values, pool, carry)


def after(value, *others):
    return lax.optimization_barrier((value,) + others)[0]


def body(
    mixer_input,
    step_raw,
    decay_rate,
    skip_gain,
    state_proj,
    queries,
    suffix_kv,
    state_pool,
    page_pool,
    norm_gain,
    hit_owner,
    hit_slot,
    page_owner,
    page_slot,
    prefix_len,
    suffix_len,
):
    owners = lax.axis_size("owner")
    owner = lax.axis_index("owner").astype(jnp.int32)
    column = lax.axis_index("tensor")
    rows = mixer_input.shape[0]
    count = rows // SUF
    heads = decay_rate.shape[0]
    width = heads * MHDIM
    qheads = queries.shape[1] // HD
    per_group = SSM_HEAD_TOTAL // GROUPS
    group = column * heads // per_group
    kv_index = column * qheads // (QHEADS // KVHEADS)
    whole_group = heads == per_group
    chips = owners // 2
    per_chip = 2 * SLOTS_DEV
    states = owners * SLOTS_DEV
    here = owner.reshape(1)
    first = (owner * count).reshape(1)
    swap = [(o, o ^ 1) for o in range(owners)]
    line = [(o, o + 2) for o in range(0, owners - 2, 2)] + [(o, o - 2) for o in range(3, owners, 2)]

    def head_of(array, index, axis):
        return lax.dynamic_index_in_dim(array, index, axis, keepdims=False)

    pool = state_pool.reshape(SLOTS_DEV, width, STATE)
    near = lax.ppermute(pool, "owner", swap)
    own_pages = jnp.transpose(head_of(page_pool, kv_index, 3), (0, 2, 1, 3))
    pages = lax.all_gather(own_pages, "owner", axis=0, tiled=True)

    state_ids = (hit_owner[:, 0] * SLOTS_DEV + hit_slot).astype(jnp.int32)
    table, cap = route(state_ids, owner, chips, per_chip, 2 * count)

    def send(item):
        return lax.ppermute(item, "owner", line)

    sends = first_sends(cap, states, here, table, pool, near)

    spread_np = np.zeros((128, width), np.float32)
    for h in range(heads):
        for k in range(3):
            spread_np[k * heads + h, h * MHDIM : (h + 1) * MHDIM] = 1.0
    spread = jnp.asarray(spread_np, jnp.bfloat16)
    split_np = np.zeros((2 * SPAN, 2 * SPAN), np.float32)
    for i in range(SPAN):
        split_np[i, 2 * i] = 1.0
        split_np[SPAN + i, 2 * i + 1] = 1.0
    split = jnp.asarray(split_np, jnp.bfloat16)
    skip = jnp.repeat(skip_gain, MHDIM)[None, :]
    decay = jnp.broadcast_to(decay_rate[:, None], (heads, SPAN))
    step_row = step_raw.T
    page_ids = (page_owner[:, :, 0] * PAGES_DEV + page_slot).astype(jnp.int32).reshape(-1)
    made = {}

    def shape_inputs(tie):
        made["mixed"] = after(mixer_input, tie).reshape(2 * rows, width)
        maps = head_of(after(state_proj, tie), group, 2)
        made["b"], made["c"] = maps[:, 0], maps[:, 1]
        suffix = head_of(after(suffix_kv, tie), kv_index, 2)
        made["k"], made["v"] = suffix[:, 0], suffix[:, 1]
        return made["mixed"]

    def pre_part(r):
        def run(tie):
            made["pre"] = mamba_pre(
                heads,
                r,
                2,
                suffix_len,
                after(first, tie),
                made["mixed"],
                made["b"],
                made["c"],
                step_row,
                decay,
                skip,
                spread,
                split,
                made.get("pre"),
            )
            return made["pre"][2]

        return run

    def attention_part(r):
        def run(tie):
            made["attn"] = attention(
                qheads,
                r,
                1,
                after(first, tie),
                page_ids,
                prefix_len,
                suffix_len,
                queries,
                made["k"],
                made["v"],
                pages,
                made.get("attn"),
            )
            return made["attn"]

        return run

    chunks = [shape_inputs] + [pre_part(r) for r in range(0, count, 2)] + [attention_part(r) for r in range(count)]

    flying = [send(item) for item in sends]
    store = None
    tie = sends[-1]
    steps = FIXED_STEPS
    for step in range(LAG, steps):
        done = None
        if chunks:
            done = chunks.pop(0)(tie)
        got = flying.pop(0)
        if done is not None:
            got = after(got, done)
        store, item = turn(
            cap, states, True, here, table, jnp.full((1,), step, jnp.int32), pool, near, got, store
        )
        flying.append(send(item))
        tie = item
    for step in range(steps, steps + LAG):
        if chunks:
            done = chunks.pop(0)(tie)
            flying[0] = after(flying[0], done)
        (store,) = turn(
            cap, states, False, here, table, jnp.full((1,), step, jnp.int32), pool, near, flying.pop(0), store
        )
        tie = store
    while chunks:
        done = chunks.pop(0)(tie)

    def late(step, store):
        item = take_out(states, here, table, step.reshape(1), pool, near, store)
        (store,) = turn(
            cap, states, False, here, table, (step + LAG).reshape(1), pool, near, send(item), store
        )
        return store

    store = lax.fori_loop(steps, table[2 * cap], late, store)

    other = lax.ppermute(pick(count, here, state_ids, store), "owner", swap)
    result = mamba_post(
        heads, whole_group, here, state_ids, suffix_len, pool, near, store, other, made["c"], *made["pre"], spread, norm_gain[None, :]
    )
    if whole_group:
        return (result[0], made["attn"])
    gated, partial_sum = result
    partial_sum = partial_sum[:, 0]
    spread_sum = jnp.where(jnp.arange(GROUPS)[:, None] == group, partial_sum[None, :], 0.0)
    totals = lax.psum(spread_sum, "tensor")
    square = lax.dynamic_index_in_dim(totals, group, 0, keepdims=False) / (per_group * MHDIM)
    my_suffix = lax.dynamic_slice_in_dim(suffix_len, first[0], count, 0)
    active = (jnp.arange(SUF)[None, :] < my_suffix[:, None]).reshape(-1)
    scaled = gated * lax.rsqrt(square + EPSILON)[:, None] * norm_gain[None, :]
    return (jnp.where(active[:, None], scaled, 0.0).astype(jnp.bfloat16), made["attn"])


def solution(mesh):
    return jax.shard_map(
        body,
        mesh=mesh,
        in_specs=(
            P("owner", None, "tensor"),
            P("owner", "tensor"),
            P("tensor"),
            P("tensor"),
            P("owner", None, None, None),
            P("owner", "tensor"),
            P("owner", None, None, None),
            P("owner", "tensor"),
            P("owner", None, None, None, None),
            P("tensor"),
            P(),
            P(),
            P(),
            P(),
            P(),
            P(),
        ),
        out_specs=(P("owner", "tensor"), P("owner", "tensor")),
        check_vma=False,
    )
```

```python
import functools
import math

import jax
import jax.numpy as jnp
import numpy as np
from jax import lax
from jax.experimental import pallas as pl
from jax.experimental.pallas import tpu as pltpu
from jax.sharding import PartitionSpec as P

SSM_HEAD_TOTAL = 128
MHDIM = 64
STATE = 256
GROUPS = 4
QHEADS = 32
KVHEADS = 4
HD = 128
PAGE = 128
SPAN = 128
SUF = 256
MAXP = 16
SLOTS_DEV = 4
PAGES_DEV = 16

EPSILON = 1e-05
NEG_FILL = -1e30
LAG = 2
FIXED_STEPS = 8
VMEM = 48 * 1024 * 1024
SMALL_VMEM = 58 * 1024 * 1024

NT = (((1,), (1,)), ((), ()))
TN = (((0,), (0,)), ((), ()))


def mm(a, b, dims=(((1,), (0,)), ((), ()))):
    return lax.dot_general(a, b, dims, preferred_element_type=jnp.float32)


def route_kernel(chips, per_chip, reqs_per_chip, cap, ids_ref, here_ref, out_ref, need_ref, tab_ref):
    states = chips * per_chip
    chip_here = here_ref[0] // 2
    core_here = here_ref[0] % 2

    def clear(s, carry):
        need_ref[s] = 0
        return carry

    lax.fori_loop(0, states, clear, 0)

    def mark(r, carry):
        s = ids_ref[r]
        need_ref[s] = need_ref[s] | (1 << (r // reqs_per_chip))
        return carry

    lax.fori_loop(0, chips * reqs_per_chip, mark, 0)

    def put(base, length, row):
        def one(t, carry):
            spot = jnp.clip(base + t, 0, 2 * chips * cap - 1)
            out_ref[row * cap + t] = jnp.where(t < length, tab_ref[spot], states)
            return carry

        lax.fori_loop(0, cap, one, 0)

    steps = jnp.int32(0)
    for up in (True, False):
        before = jnp.int32(0)
        sent = jnp.int32(0)
        came = jnp.int32(0)
        for place in range(chips - 1):
            chip = place if up else chips - 1 - place
            base = ((0 if up else chips) + place) * cap

            def wanted(s, chip=chip, up=up):
                if up:
                    return (need_ref[s] >> (chip + 1)) != 0
                return (need_ref[s] & ((1 << chip) - 1)) != 0

            def own(i, t, chip=chip, base=base, wanted=wanted):
                s = chip * per_chip + i
                tab_ref[base + t] = s
                return t + wanted(s).astype(jnp.int32)

            t = lax.fori_loop(0, per_chip, own, jnp.int32(0))
            if place:

                def forward(j, t, base=base, wanted=wanted):
                    s = tab_ref[base - cap + j]
                    take = (s < states) & wanted(jnp.minimum(s, states - 1))
                    later = jnp.where(take, jnp.maximum(t, j + LAG), t)

                    def gap(i, carry):
                        tab_ref[base + i] = states
                        return carry

                    lax.fori_loop(t, later, gap, 0)
                    tab_ref[base + later] = s
                    return later + take.astype(jnp.int32)

                t = lax.fori_loop(0, before, forward, t)
            before = t
            sent = jnp.where(chip_here == chip, t, sent)
            came = jnp.where(chip_here == (chip + 1 if up else chip - 1), t, came)
            steps = jnp.maximum(steps, t)
        here = chip_here if up else chips - 1 - chip_here
        side = 0 if up else chips

        @pl.when(core_here == (0 if up else 1))
        def _(here=here, side=side, sent=sent, came=came):
            put((side + here) * cap, sent, 0)
            put((side + here - 1) * cap, came, 1)

    out_ref[2 * cap] = steps


def route(state_ids, owner, chips, per_chip, reqs_per_chip):
    cap = chips * per_chip + LAG * chips + 8
    smem = pl.BlockSpec(memory_space=pltpu.SMEM)
    table = pl.pallas_call(
        functools.partial(route_kernel, chips, per_chip, reqs_per_chip, cap),
        out_shape=jax.ShapeDtypeStruct((2 * cap + 8,), jnp.int32),
        in_specs=[smem, smem],
        out_specs=smem,
        scratch_shapes=[
            pltpu.SMEM((chips * per_chip,), jnp.int32),
            pltpu.SMEM((2 * chips * cap,), jnp.int32),
        ],
        name="route_states",
    )(state_ids, owner.reshape(1))
    return table, cap


def start_from(state, owner, pool_ref, near_ref, others, dst, sem):
    place = state // SLOTS_DEV
    slot = state % SLOTS_DEV
    in_pool = place == owner
    in_near = place == (owner ^ 1)

    @pl.when(in_pool)
    def _():
        pltpu.make_async_copy(pool_ref.at[slot], dst, sem).start()

    @pl.when(in_near)
    def _():
        pltpu.make_async_copy(near_ref.at[slot], dst, sem).start()

    for holds, ref in others:

        @pl.when(jnp.logical_not(in_pool | in_near) & holds)
        def _(ref=ref):
            pltpu.make_async_copy(ref, dst, sem).start()


ANYWHERE = pl.BlockSpec(memory_space=pl.ANY)
IN_HBM = pl.BlockSpec(memory_space=pltpu.HBM)


def first_kernel(cap, states, here_ref, table_ref, pool_ref, near_ref, *rest):
    sends, (item_ref, sem) = rest[:-2], rest[-2:]
    for t in range(len(sends)):
        state = table_ref[t]

        @pl.when(state < states)
        def _(state=state, t=t):
            start_from(state, here_ref[0], pool_ref, near_ref, (), item_ref.at[t], sem.at[t])

    for t, send in enumerate(sends):

        @pl.when(table_ref[t] < states)
        def _(send=send, t=t):
            pltpu.make_async_copy(pool_ref.at[0], item_ref.at[t], sem.at[t]).wait()
            pltpu.make_async_copy(item_ref.at[t], send, sem.at[t]).start()

    for t, send in enumerate(sends):

        @pl.when(table_ref[t] < states)
        def _(send=send, t=t):
            pltpu.make_async_copy(item_ref.at[t], send, sem.at[t]).wait()


def first_sends(cap, states, here, table, pool, near):
    item = jax.ShapeDtypeStruct(pool.shape[1:], pool.dtype)
    return pl.pallas_call(
        functools.partial(first_kernel, cap, states),
        grid_spec=pltpu.PrefetchScalarGridSpec(
            num_scalar_prefetch=2,
            grid=(1,),
            in_specs=[IN_HBM, IN_HBM],
            out_specs=[IN_HBM] * LAG,
            scratch_shapes=[
                pltpu.VMEM((LAG,) + pool.shape[1:], pool.dtype),
                pltpu.SemaphoreType.DMA((LAG,)),
            ],
        ),
        out_shape=[item] * LAG,
        compiler_params=pltpu.CompilerParams(vmem_limit_bytes=SMALL_VMEM),
        name="first_sends",
    )(here, table, pool, near)


def turn_kernel(
    cap, states, sending, here_ref, table_ref, step_ref, pool_ref, near_ref, got_ref, _store_in, store_ref, *rest
):
    item_ref, sem = rest[-2:]
    step = step_ref[0]
    came = table_ref[cap + step - LAG]
    kept = came < states

    @pl.when(kept)
    def _():
        pltpu.make_async_copy(got_ref, item_ref.at[0], sem.at[0]).start()

    if sending:
        send_ref = rest[0]
        state = table_ref[step]

        @pl.when(state < states)
        def _():
            spot = jnp.minimum(state, states - 1)
            start_from(
                state,
                here_ref[0],
                pool_ref,
                near_ref,
                ((state == came, got_ref), (state != came, store_ref.at[spot])),
                item_ref.at[1],
                sem.at[1],
            )
            pltpu.make_async_copy(got_ref, item_ref.at[1], sem.at[1]).wait()
            pltpu.make_async_copy(item_ref.at[1], send_ref, sem.at[1]).start()

    @pl.when(kept)
    def _():
        pltpu.make_async_copy(got_ref, item_ref.at[0], sem.at[0]).wait()
        copy = pltpu.make_async_copy(item_ref.at[0], store_ref.at[came], sem.at[0])
        copy.start()
        copy.wait()

    if sending:

        @pl.when(state < states)
        def _():
            pltpu.make_async_copy(item_ref.at[1], send_ref, sem.at[1]).wait()


def turn(cap, states, sending, here, table, step, pool, near, got, store):
    item = jax.ShapeDtypeStruct(pool.shape[1:], pool.dtype)
    kept = jax.ShapeDtypeStruct((states + 1,) + pool.shape[1:], pool.dtype)
    aliases = {} if store is None else {6: 0}
    if store is None:
        store = jnp.zeros((16, 128), jnp.float32)
    return pl.pallas_call(
        functools.partial(turn_kernel, cap, states, sending),
        grid_spec=pltpu.PrefetchScalarGridSpec(
            num_scalar_prefetch=3,
            grid=(1,),
            in_specs=[IN_HBM] * 4,
            out_specs=[IN_HBM] * (1 + sending),
            scratch_shapes=[
                pltpu.VMEM((2,) + pool.shape[1:], pool.dtype),
                pltpu.SemaphoreType.DMA((2,)),
            ],
        ),
        out_shape=[kept, item][: 1 + sending],
        input_output_aliases=aliases,
        compiler_params=pltpu.CompilerParams(vmem_limit_bytes=SMALL_VMEM),
        name="turn_states",
    )(here, table, step, pool, near, got, store)


def take_kernel(states, here_ref, table_ref, step_ref, pool_ref, near_ref, store_ref, send_ref, item_ref, sem):
    state = table_ref[step_ref[0]]

    @pl.when(state < states)
    def _():
        spot = jnp.minimum(state, states - 1)
        start_from(state, here_ref[0], pool_ref, near_ref, ((state < states, store_ref.at[spot]),), item_ref, sem)
        pltpu.make_async_copy(pool_ref.at[0], item_ref, sem).wait()
        copy = pltpu.make_async_copy(item_ref, send_ref, sem)
        copy.start()
        copy.wait()


def take_out(states, here, table, step, pool, near, store):
    return pl.pallas_call(
        functools.partial(take_kernel, states),
        grid_spec=pltpu.PrefetchScalarGridSpec(
            num_scalar_prefetch=3,
            grid=(1,),
            in_specs=[IN_HBM] * 3,
            out_specs=IN_HBM,
            scratch_shapes=[pltpu.VMEM(pool.shape[1:], pool.dtype), pltpu.SemaphoreType.DMA],
        ),
        out_shape=jax.ShapeDtypeStruct(pool.shape[1:], pool.dtype),
        compiler_params=pltpu.CompilerParams(vmem_limit_bytes=SMALL_VMEM),
        name="take_state",
    )(here, table, step, pool, near, store)


def pick_kernel(count, here_ref, ids_ref, store_ref, out_ref, item_ref, sem):
    owner = here_ref[0]
    chip = owner // 2
    core = owner % 2

    def each(act):
        for r in range(count):
            state = ids_ref[(owner ^ 1) * count + r]
            place = state // (2 * SLOTS_DEV)
            held = jnp.where(core == 0, place < chip, place > chip)

            @pl.when(held)
            def _(state=state, r=r):
                act(state, r)

    def into(state, r):
        return pltpu.make_async_copy(store_ref.at[state], item_ref.at[r], sem.at[r])

    def out(r):
        return pltpu.make_async_copy(item_ref.at[r], out_ref.at[r], sem.at[r])

    def begin(state, r):
        into(state, r).start()

    def turn_over(state, r):
        into(state, r).wait()
        out(r).start()

    def finish(state, r):
        out(r).wait()

    each(begin)
    each(turn_over)
    each(finish)


def pick(count, here, ids, store):
    return pl.pallas_call(
        functools.partial(pick_kernel, count),
        grid_spec=pltpu.PrefetchScalarGridSpec(
            num_scalar_prefetch=2,
            grid=(1,),
            in_specs=[IN_HBM],
            out_specs=IN_HBM,
            scratch_shapes=[
                pltpu.VMEM((count,) + store.shape[1:], store.dtype),
                pltpu.SemaphoreType.DMA((count,)),
            ],
        ),
        out_shape=jax.ShapeDtypeStruct((count,) + store.shape[1:], store.dtype),
        compiler_params=pltpu.CompilerParams(vmem_limit_bytes=SMALL_VMEM),
        name="pick_states",
    )(here, ids, store)


def mamba_pre_kernel(
    heads,
    live_ref,
    first_ref,
    mix_ref,
    b_ref,
    c_ref,
    step_ref,
    decay_ref,
    skip_ref,
    spread_ref,
    split_ref,
    _pre_in,
    _z_in,
    _e_in,
    pre_ref,
    z_ref,
    e_ref,
    bs_ref,
    end_ref,
):
    block = pl.program_id(1)
    request = first_ref[0] + pl.program_id(0)
    copies = SPAN // heads
    row = lax.broadcasted_iota(jnp.int32, (SPAN, SPAN), 0)
    lane = lax.broadcasted_iota(jnp.int32, (SPAN, SPAN), 1)
    lower = row >= lane
    left = lane < MHDIM

    def three_way(value):
        high = value.astype(jnp.bfloat16)
        rest = value - high.astype(jnp.float32)
        middle = rest.astype(jnp.bfloat16)
        low = (rest - middle.astype(jnp.float32)).astype(jnp.bfloat16)
        high, middle, low = (v.astype(jnp.float32) for v in (high, middle, low))
        kept = jnp.where(
            lane < heads,
            high,
            jnp.where(lane < 2 * heads, middle, jnp.where(lane < 3 * heads, low, 0.0)),
        )
        return kept.astype(jnp.bfloat16)

    @pl.when((block == 0) | (live_ref[request] > SPAN))
    def _():
        raw = step_ref[...]
        rate_row = jnp.maximum(raw, 0.0) + jnp.log1p(jnp.exp(-jnp.abs(raw)))
        upper = jnp.where(row <= lane, 1.0, 0.0)
        cum_row = lax.dot_general(
            -rate_row * decay_ref[...],
            upper,
            (((1,), (0,)), ((), ())),
            precision=lax.Precision.HIGHEST,
            preferred_element_type=jnp.float32,
        )
        cum = jnp.concatenate([cum_row] * copies, axis=0).T
        rate_col = jnp.concatenate([rate_row] * copies, axis=0).T

        both = mm(split_ref[...], mix_ref[...])
        z_ref[...] = both[SPAN:].astype(jnp.bfloat16)
        x = both[:SPAN]
        x_half = x.astype(jnp.bfloat16)
        b = b_ref[...]
        c = c_ref[...]
        cross = mm(c, b, NT)

        def weights(h):
            fall = cum[:, h : h + 1] - cum_row[h : h + 1, :]
            fade = jnp.exp(jnp.where(lower, fall, NEG_FILL))
            return (cross * fade * rate_row[h : h + 1, :]).astype(jnp.bfloat16)

        for pair in range(heads // 2):
            cols = slice(pair * 2 * MHDIM, (pair + 1) * 2 * MHDIM)
            xp = x_half[:, cols]
            zero = jnp.zeros_like(xp)
            stacked = jnp.concatenate([jnp.where(left, xp, zero), jnp.where(left, zero, xp)], axis=0)
            w = jnp.concatenate([weights(2 * pair), weights(2 * pair + 1)], axis=1)
            pre_ref[:, cols] = mm(w, stacked) + skip_ref[:, cols] * x[:, cols]

        @pl.when(block == 0)
        def _():
            end = cum[SPAN - 1 : SPAN, :]
            tail = jnp.exp(end - cum) * rate_col
            scaled = (mm(three_way(tail), spread_ref[...]) * x).astype(jnp.bfloat16)
            bs_ref[...] = mm(scaled, b, TN).astype(jnp.bfloat16)
            end_ref[...] = jnp.broadcast_to(end, end_ref.shape)
            e_ref[...] = three_way(jnp.exp(cum))

        @pl.when(block == 1)
        def _():
            e_half = three_way(jnp.exp(cum))
            carried = mm(c, bs_ref[...], NT)
            pre_ref[...] += mm(e_half, spread_ref[...]) * carried
            e_ref[...] = three_way(jnp.exp(cum + end_ref[0:1, :]))


def mamba_pre(heads, first, count, live, here, mixed, b_rows, c_rows, step_row, decay, skip, spread, split, carry):
    width = heads * MHDIM
    rows = b_rows.shape[0]

    def at(r, k, *_):
        return ((first + r) * 2 + k, 0)

    def fixed(r, k, *_):
        return (0, 0)

    blocks = count * 2
    outs = [
        jax.ShapeDtypeStruct((rows, width), jnp.float32),
        jax.ShapeDtypeStruct((rows, width), jnp.bfloat16),
        jax.ShapeDtypeStruct((rows, 128), jnp.bfloat16),
    ]
    if carry is None:
        carry = tuple(jnp.zeros((16, 128), jnp.float32) for _ in outs)
        aliases = {}
    else:
        aliases = {10: 0, 11: 1, 12: 2}
    return pl.pallas_call(
        functools.partial(mamba_pre_kernel, heads),
        grid_spec=pltpu.PrefetchScalarGridSpec(
            num_scalar_prefetch=2,
            grid=(count, 2),
            in_specs=[
                pl.BlockSpec((2 * SPAN, width), at),
                pl.BlockSpec((SPAN, STATE), at),
                pl.BlockSpec((SPAN, STATE), at),
                pl.BlockSpec((heads, SPAN), lambda r, k, *_: (0, (first + r) * 2 + k)),
                pl.BlockSpec((heads, SPAN), fixed),
                pl.BlockSpec((1, width), fixed),
                pl.BlockSpec((128, width), fixed),
                pl.BlockSpec((2 * SPAN, 2 * SPAN), fixed),
                ANYWHERE,
                ANYWHERE,
                ANYWHERE,
            ],
            out_specs=[
                pl.BlockSpec((SPAN, width), at),
                pl.BlockSpec((SPAN, width), at),
                pl.BlockSpec((SPAN, 128), at),
            ],
            scratch_shapes=[
                pltpu.VMEM((width, STATE), jnp.bfloat16),
                pltpu.VMEM((8, 128), jnp.float32),
            ],
        ),
        out_shape=outs,
        input_output_aliases=aliases,
        compiler_params=pltpu.CompilerParams(vmem_limit_bytes=VMEM),
        cost_estimate=pl.CostEstimate(
            flops=blocks * heads * 40 * SPAN * SPAN * MHDIM,
            bytes_accessed=blocks * SPAN * width * 10,
            transcendentals=blocks * heads * SPAN * SPAN,
        ),
        name="mamba_pre",
    )(live, here + first, mixed, b_rows, c_rows, step_row, decay, skip, spread, split, *carry)


def mamba_post_kernel(
    heads,
    whole_group,
    count,
    here_ref,
    ids_ref,
    live_ref,
    pool_ref,
    near_ref,
    store_ref,
    other_ref,
    c_ref,
    pre_ref,
    z_ref,
    e_ref,
    spread_ref,
    gain_ref,
    out_ref,
    *rest,
):
    r = pl.program_id(0)
    width = heads * MHDIM
    state_ref, sem = rest[-2:]
    owner = here_ref[0]
    chip = owner // 2
    core = owner % 2

    def fetch(r):
        state = ids_ref[owner * count + r]
        place = state // (2 * SLOTS_DEV)
        mine = jnp.where(core == 0, place < chip, place > chip)
        slot = r % 2
        start_from(
            state,
            owner,
            pool_ref,
            near_ref,
            ((mine, store_ref.at[state]), (jnp.logical_not(mine), other_ref.at[r])),
            state_ref.at[slot],
            sem.at[slot],
        )

    @pl.when(r == 0)
    def _():
        fetch(r)

    @pl.when(r + 1 < count)
    def _():
        fetch(r + 1)

    pltpu.make_async_copy(pool_ref.at[0], state_ref.at[r % 2], sem.at[r % 2]).wait()
    c = c_ref[...]
    e = e_ref[...]
    carried = mm(c, state_ref[r % 2], NT)
    summed = pre_ref[...] + mm(e, spread_ref[...]) * carried
    z = z_ref[...].astype(jnp.float32)
    gated = summed * (z / (1.0 + jnp.exp(-z)))
    square = jnp.sum(gated * gated, axis=1, keepdims=True)
    if whole_group:
        norm = lax.rsqrt(square / width + EPSILON)
        live = lax.broadcasted_iota(jnp.int32, (SUF, 1), 0) < live_ref[owner * count + r]
        out_ref[...] = jnp.where(live, gated * norm * gain_ref[...], 0.0).astype(out_ref.dtype)
    else:
        out_ref[...] = gated
        rest[0][...] = jnp.broadcast_to(square, (SUF, 128))


def mamba_post(heads, whole_group, here, ids, live, pool, near, store, other, c_rows, pre, z, e3, spread, gain):
    width = heads * MHDIM
    rows = c_rows.shape[0]
    count = rows // SUF

    def at(r, *_):
        return (r, 0)

    def fixed(r, *_):
        return (0, 0)

    out_shape = [jax.ShapeDtypeStruct((rows, width), jnp.bfloat16 if whole_group else jnp.float32)]
    out_specs = [pl.BlockSpec((SUF, width), at)]
    if not whole_group:
        out_shape.append(jax.ShapeDtypeStruct((rows, 128), jnp.float32))
        out_specs.append(pl.BlockSpec((SUF, 128), at))
    return pl.pallas_call(
        functools.partial(mamba_post_kernel, heads, whole_group, count),
        grid_spec=pltpu.PrefetchScalarGridSpec(
            num_scalar_prefetch=3,
            grid=(count,),
            in_specs=[
                IN_HBM,
                IN_HBM,
                IN_HBM,
                IN_HBM,
                pl.BlockSpec((SUF, STATE), at),
                pl.BlockSpec((SUF, width), at),
                pl.BlockSpec((SUF, width), at),
                pl.BlockSpec((SUF, 128), at),
                pl.BlockSpec((128, width), fixed),
                pl.BlockSpec((1, width), fixed),
            ],
            out_specs=out_specs,
            scratch_shapes=[
                pltpu.VMEM((2, width, STATE), jnp.bfloat16),
                pltpu.SemaphoreType.DMA((2,)),
            ],
        ),
        out_shape=out_shape,
        compiler_params=pltpu.CompilerParams(vmem_limit_bytes=VMEM),
        cost_estimate=pl.CostEstimate(
            flops=2 * rows * width * STATE,
            bytes_accessed=rows * width * 12,
            transcendentals=rows * width,
        ),
        name="mamba_post",
    )(here, ids, live, pool, near, store, other, c_rows, pre, z, e3, spread, gain)


def attend_kernel(
    qheads,
    first_ref,
    pages_ref,
    prefix_ref,
    live_ref,
    q_ref,
    ks_ref,
    vs_ref,
    pool_ref,
    _out_in,
    out_ref,
    kv_ref,
    s_ref,
    top_ref,
    total_ref,
    mixed_ref,
    sem,
):
    half = pl.program_id(1)
    request = first_ref[0] + pl.program_id(0)
    scale = math.log2(math.e) / math.sqrt(HD)
    pairs = prefix_ref[request] // (2 * PAGE)

    @pl.when(half == 0)
    def _():
        def copy(p, kv):
            return pltpu.make_async_copy(
                pool_ref.at[pages_ref[request * MAXP + p], kv],
                kv_ref.at[kv, pl.ds(pl.multiple_of(p * PAGE, PAGE), PAGE)],
                sem,
            )

        def begin(p, carry):
            copy(p, 0).start()
            copy(p, 1).start()
            return carry

        def finish(p, carry):
            copy(p, 0).wait()
            copy(p, 1).wait()
            return carry

        lax.fori_loop(0, 2 * pairs, begin, 0)
        lax.fori_loop(0, 2 * pairs, finish, 0)

    start = half * SPAN
    live = live_ref[request]

    def columns(h):
        return slice(h * HD, (h + 1) * HD)

    def fold(s):
        return jnp.maximum(s[:, :HD], s[:, HD:])

    @pl.when(start < live)
    def _():
        row = lax.broadcasted_iota(jnp.int32, (SPAN, SUF), 0) + start
        lane = lax.broadcasted_iota(jnp.int32, (SPAN, SUF), 1)
        causal = row >= lane
        for h in range(qheads):
            s = jnp.where(causal, mm(q_ref[:, columns(h)], ks_ref[...], NT), NEG_FILL)
            s_ref[0, h] = s
            top_ref[h] = fold(s)

        def scores(i, carry):
            keys = kv_ref[0, pl.ds(pl.multiple_of(i * 2 * PAGE, 2 * PAGE), 2 * PAGE)]
            for h in range(qheads):
                s = mm(q_ref[:, columns(h)], keys, NT)
                s_ref[i + 1, h] = s
                top_ref[h] = jnp.maximum(top_ref[h], fold(s))
            return carry

        lax.fori_loop(0, pairs, scores, 0)

        def weigh(h, s, values):
            probs = jnp.exp2((s - jnp.concatenate([top_ref[h]] * 2, axis=1)) * scale)
            return probs[:, :HD] + probs[:, HD:], mm(probs.astype(jnp.bfloat16), values)

        for h in range(qheads):
            top_ref[h] = jnp.broadcast_to(jnp.max(top_ref[h], axis=1, keepdims=True), (SPAN, HD))
        for h in range(qheads):
            total_ref[h], mixed_ref[h] = weigh(h, s_ref[0, h], vs_ref[...])

        def values(i, carry):
            rows = kv_ref[1, pl.ds(pl.multiple_of(i * 2 * PAGE, 2 * PAGE), 2 * PAGE)]
            for h in range(qheads):
                total, mixed = weigh(h, s_ref[i + 1, h], rows)
                total_ref[h] += total
                mixed_ref[h] += mixed
            return carry

        lax.fori_loop(0, pairs, values, 0)
        keep = lax.broadcasted_iota(jnp.int32, (SPAN, 1), 0) + start < live
        for h in range(qheads):
            total = jnp.sum(total_ref[h], axis=1, keepdims=True)
            out_ref[:, columns(h)] = jnp.where(keep, mixed_ref[h] / total, 0.0).astype(out_ref.dtype)

    @pl.when(start >= live)
    def _():
        out_ref[...] = jnp.zeros_like(out_ref)


def attention(qheads, first, count, here, pages, prefix, live, queries, keys, values, pool, carry):
    most = MAXP // 2 + 1
    width = qheads * HD
    if carry is None:
        carry = jnp.zeros((16, 128), jnp.bfloat16)
        aliases = {}
    else:
        aliases = {8: 0}

    def at(r, k, *_):
        return ((first + r) * 2 + k, 0)

    return pl.pallas_call(
        functools.partial(attend_kernel, qheads),
        grid_spec=pltpu.PrefetchScalarGridSpec(
            num_scalar_prefetch=4,
            grid=(count, 2),
            in_specs=[
                pl.BlockSpec((SPAN, width), at),
                pl.BlockSpec((SUF, HD), lambda r, k, *_: (first + r, 0)),
                pl.BlockSpec((SUF, HD), lambda r, k, *_: (first + r, 0)),
                IN_HBM,
                ANYWHERE,
            ],
            out_specs=pl.BlockSpec((SPAN, width), at),
            scratch_shapes=[
                pltpu.VMEM((2, MAXP * PAGE, HD), jnp.bfloat16),
                pltpu.VMEM((most, qheads, SPAN, 2 * PAGE), jnp.float32),
                pltpu.VMEM((qheads, SPAN, HD), jnp.float32),
                pltpu.VMEM((qheads, SPAN, HD), jnp.float32),
                pltpu.VMEM((qheads, SPAN, HD), jnp.float32),
                pltpu.SemaphoreType.DMA,
            ],
        ),
        out_shape=jax.ShapeDtypeStruct(queries.shape, jnp.bfloat16),
        input_output_aliases=aliases,
        compiler_params=pltpu.CompilerParams(vmem_limit_bytes=VMEM),
        cost_estimate=pl.CostEstimate(
            flops=count * qheads * SUF * (MAXP * PAGE + SUF) * HD * 4,
            bytes_accessed=count * (SUF * qheads * HD * 4 + MAXP * PAGE * HD * 4),
            transcendentals=count * qheads * SUF * (MAXP * PAGE + SUF),
        ),
        name="attention",
    )(here + first, pages, prefix, live, queries, keys, values, pool, carry)


def after(value, *others):
    return lax.optimization_barrier((value,) + others)[0]


def body(
    mixer_input,
    step_raw,
    decay_rate,
    skip_gain,
    state_proj,
    queries,
    suffix_kv,
    state_pool,
    page_pool,
    norm_gain,
    hit_owner,
    hit_slot,
    page_owner,
    page_slot,
    prefix_len,
    suffix_len,
):
    owners = lax.axis_size("owner")
    owner = lax.axis_index("owner").astype(jnp.int32)
    column = lax.axis_index("tensor")
    rows = mixer_input.shape[0]
    count = rows // SUF
    heads = decay_rate.shape[0]
    width = heads * MHDIM
    qheads = queries.shape[1] // HD
    per_group = SSM_HEAD_TOTAL // GROUPS
    group = column * heads // per_group
    kv_index = column * qheads // (QHEADS // KVHEADS)
    whole_group = heads == per_group
    chips = owners // 2
    per_chip = 2 * SLOTS_DEV
    states = owners * SLOTS_DEV
    here = owner.reshape(1)
    first = (owner * count).reshape(1)
    swap = [(o, o ^ 1) for o in range(owners)]
    line = [(o, o + 2) for o in range(0, owners - 2, 2)] + [(o, o - 2) for o in range(3, owners, 2)]

    def head_of(array, index, axis):
        return lax.dynamic_index_in_dim(array, index, axis, keepdims=False)

    pool = state_pool.reshape(SLOTS_DEV, width, STATE)
    near = lax.ppermute(pool, "owner", swap)
    own_pages = jnp.transpose(head_of(page_pool, kv_index, 3), (0, 2, 1, 3))
    pages = lax.all_gather(own_pages, "owner", axis=0, tiled=True)

    state_ids = (hit_owner[:, 0] * SLOTS_DEV + hit_slot).astype(jnp.int32)
    table, cap = route(state_ids, owner, chips, per_chip, 2 * count)

    def send(item):
        return lax.ppermute(item, "owner", line)

    sends = first_sends(cap, states, here, table, pool, near)

    spread_np = np.zeros((128, width), np.float32)
    for h in range(heads):
        for k in range(3):
            spread_np[k * heads + h, h * MHDIM : (h + 1) * MHDIM] = 1.0
    spread = jnp.asarray(spread_np, jnp.bfloat16)
    split_np = np.zeros((2 * SPAN, 2 * SPAN), np.float32)
    for i in range(SPAN):
        split_np[i, 2 * i] = 1.0
        split_np[SPAN + i, 2 * i + 1] = 1.0
    split = jnp.asarray(split_np, jnp.bfloat16)
    skip = jnp.repeat(skip_gain, MHDIM)[None, :]
    decay = jnp.broadcast_to(decay_rate[:, None], (heads, SPAN))
    step_row = step_raw.T
    page_ids = (page_owner[:, :, 0] * PAGES_DEV + page_slot).astype(jnp.int32).reshape(-1)
    made = {}

    def shape_inputs(tie):
        made["mixed"] = after(mixer_input, tie).reshape(2 * rows, width)
        maps = head_of(after(state_proj, tie), group, 2)
        made["b"], made["c"] = maps[:, 0], maps[:, 1]
        suffix = head_of(after(suffix_kv, tie), kv_index, 2)
        made["k"], made["v"] = suffix[:, 0], suffix[:, 1]
        return made["mixed"]

    def pre_part(r):
        def run(tie):
            made["pre"] = mamba_pre(
                heads,
                r,
                2,
                suffix_len,
                after(first, tie),
                made["mixed"],
                made["b"],
                made["c"],
                step_row,
                decay,
                skip,
                spread,
                split,
                made.get("pre"),
            )
            return made["pre"][2]

        return run

    def attention_part(r):
        def run(tie):
            made["attn"] = attention(
                qheads,
                r,
                1,
                after(first, tie),
                page_ids,
                prefix_len,
                suffix_len,
                queries,
                made["k"],
                made["v"],
                pages,
                made.get("attn"),
            )
            return made["attn"]

        return run

    chunks = [shape_inputs] + [pre_part(r) for r in range(0, count, 2)] + [attention_part(r) for r in range(count)]

    flying = [send(item) for item in sends]
    store = None
    tie = sends[-1]
    steps = FIXED_STEPS
    for step in range(LAG, steps):
        done = None
        if chunks:
            done = chunks.pop(0)(tie)
        got = flying.pop(0)
        if done is not None:
            got = after(got, done)
        store, item = turn(
            cap, states, True, here, table, jnp.full((1,), step, jnp.int32), pool, near, got, store
        )
        flying.append(send(item))
        tie = item
    for step in range(steps, steps + LAG):
        if chunks:
            done = chunks.pop(0)(tie)
            flying[0] = after(flying[0], done)
        (store,) = turn(
            cap, states, False, here, table, jnp.full((1,), step, jnp.int32), pool, near, flying.pop(0), store
        )
        tie = store
    while chunks:
        done = chunks.pop(0)(tie)

    def late(step, store):
        item = take_out(states, here, table, step.reshape(1), pool, near, store)
        (store,) = turn(
            cap, states, False, here, table, (step + LAG).reshape(1), pool, near, send(item), store
        )
        return store

    store = lax.fori_loop(steps, table[2 * cap], late, store)

    other = lax.ppermute(pick(count, here, state_ids, store), "owner", swap)
    result = mamba_post(
        heads, whole_group, here, state_ids, suffix_len, pool, near, store, other, made["c"], *made["pre"], spread, norm_gain[None, :]
    )
    if whole_group:
        return (result[0], made["attn"])
    gated, partial_sum = result
    partial_sum = partial_sum[:, 0]
    spread_sum = jnp.where(jnp.arange(GROUPS)[:, None] == group, partial_sum[None, :], 0.0)
    totals = lax.psum(spread_sum, "tensor")
    square = lax.dynamic_index_in_dim(totals, group, 0, keepdims=False) / (per_group * MHDIM)
    my_suffix = lax.dynamic_slice_in_dim(suffix_len, first[0], count, 0)
    active = (jnp.arange(SUF)[None, :] < my_suffix[:, None]).reshape(-1)
    scaled = gated * lax.rsqrt(square + EPSILON)[:, None] * norm_gain[None, :]
    return (jnp.where(active[:, None], scaled, 0.0).astype(jnp.bfloat16), made["attn"])


def solution(mesh):
    return jax.shard_map(
        body,
        mesh=mesh,
        in_specs=(
            P("owner", None, "tensor"),
            P("owner", "tensor"),
            P("tensor"),
            P("tensor"),
            P("owner", None, None, None),
            P("owner", "tensor"),
            P("owner", None, None, None),
            P("owner", "tensor"),
            P("owner", None, None, None, None),
            P("tensor"),
            P(),
            P(),
            P(),
            P(),
            P(),
            P(),
        ),
        out_specs=(P("owner", "tensor"), P("owner", "tensor")),
        check_vma=False,
    )
```

```python
import functools
import math

import jax
import jax.numpy as jnp
import numpy as np
from jax import lax
from jax.experimental import pallas as pl
from jax.experimental.pallas import tpu as pltpu
from jax.sharding import PartitionSpec as P

SSM_HEAD_TOTAL = 128
MHDIM = 64
STATE = 256
GROUPS = 4
QHEADS = 32
KVHEADS = 4
HD = 128
PAGE = 128
SPAN = 128
SUF = 256
MAXP = 16
SLOTS_DEV = 4
PAGES_DEV = 16

EPSILON = 1e-05
NEG_FILL = -1e30
LAG = 2
FIXED_STEPS = 8
VMEM = 48 * 1024 * 1024
SMALL_VMEM = 58 * 1024 * 1024

NT = (((1,), (1,)), ((), ()))
TN = (((0,), (0,)), ((), ()))


def mm(a, b, dims=(((1,), (0,)), ((), ()))):
    return lax.dot_general(a, b, dims, preferred_element_type=jnp.float32)


def route_kernel(chips, per_chip, reqs_per_chip, cap, ids_ref, here_ref, out_ref, need_ref, own_ref, tab_ref):
    states = chips * per_chip
    chip_here = here_ref[0] // 2
    core_here = here_ref[0] % 2

    def clear(s, carry):
        need_ref[s] = 0
        return carry

    lax.fori_loop(0, states, clear, 0)

    def mark(r, carry):
        s = ids_ref[r]
        need_ref[s] = need_ref[s] | (1 << (r // reqs_per_chip))
        return carry

    lax.fori_loop(0, chips * reqs_per_chip, mark, 0)

    def put(base, length, row):
        def one(t, carry):
            spot = jnp.clip(base + t, 0, 2 * chips * cap - 1)
            out_ref[row * cap + t] = jnp.where(t < length, tab_ref[spot], states)
            return carry

        lax.fori_loop(0, cap, one, 0)

    steps = jnp.int32(0)
    for up in (True, False):
        before = jnp.int32(0)
        sent = jnp.int32(0)
        came = jnp.int32(0)
        for place in range(chips - 1):
            chip = place if up else chips - 1 - place
            base = ((0 if up else chips) + place) * cap

            def wanted(s, further=0, chip=chip, up=up):
                if up:
                    return (need_ref[s] >> (chip + 1 + further)) != 0
                return (need_ref[s] & ((1 << max(chip - further, 0)) - 1)) != 0

            count = jnp.int32(0)
            for far in (True, False):

                def own(i, n, far=far, chip=chip, wanted=wanted):
                    s = chip * per_chip + i
                    own_ref[n] = s
                    beyond = wanted(s, 1)
                    take = beyond if far else wanted(s) & jnp.logical_not(beyond)
                    return n + take.astype(jnp.int32)

                count = lax.fori_loop(0, per_chip, own, count)

            def fill(t, used, base=base, count=count):
                tab_ref[base + t] = jnp.where(used < count, own_ref[used], states)
                return jnp.minimum(used + 1, count)

            def forward(j, carry, base=base, wanted=wanted, fill=fill):
                t, used = carry
                s = tab_ref[base - cap + j]
                take = (s < states) & wanted(jnp.minimum(s, states - 1))
                later = jnp.where(take, jnp.maximum(t, j + LAG), t)
                used = lax.fori_loop(t, later, fill, used)
                tab_ref[base + later] = s
                return later + take.astype(jnp.int32), used

            t, used = jnp.int32(0), jnp.int32(0)
            if place:
                t, used = lax.fori_loop(0, before, forward, (t, used))
            end = t + count - used
            lax.fori_loop(t, end, fill, used)
            before = end
            sent = jnp.where(chip_here == chip, end, sent)
            came = jnp.where(chip_here == (chip + 1 if up else chip - 1), end, came)
            steps = jnp.maximum(steps, end)
        here = chip_here if up else chips - 1 - chip_here
        side = 0 if up else chips

        @pl.when(core_here == (0 if up else 1))
        def _(here=here, side=side, sent=sent, came=came):
            put((side + here) * cap, sent, 0)
            put((side + here - 1) * cap, came, 1)

    out_ref[2 * cap] = steps
    found = jnp.int32(0)
    for here_now in (True, False):
        for r in range(reqs_per_chip // 2):
            place = ids_ref[here_ref[0] * (reqs_per_chip // 2) + r] // per_chip
            local = (place == chip_here) | jnp.where(core_here == 0, place < chip_here, place > chip_here)
            out_ref[2 * cap + 2 + found] = r
            found += (local == here_now).astype(jnp.int32)
        if here_now:
            out_ref[2 * cap + 1] = found


def route(state_ids, owner, chips, per_chip, reqs_per_chip):
    cap = chips * per_chip + LAG * chips + 8
    smem = pl.BlockSpec(memory_space=pltpu.SMEM)
    table = pl.pallas_call(
        functools.partial(route_kernel, chips, per_chip, reqs_per_chip, cap),
        out_shape=jax.ShapeDtypeStruct((2 * cap + 4 + reqs_per_chip,), jnp.int32),
        in_specs=[smem, smem],
        out_specs=smem,
        scratch_shapes=[
            pltpu.SMEM((chips * per_chip,), jnp.int32),
            pltpu.SMEM((2 * per_chip,), jnp.int32),
            pltpu.SMEM((2 * chips * cap,), jnp.int32),
        ],
        name="route_states",
    )(state_ids, owner.reshape(1))
    return table, cap


def start_from(state, owner, pool_ref, near_ref, others, dst, sem):
    place = state // SLOTS_DEV
    slot = state % SLOTS_DEV
    in_pool = place == owner
    in_near = place == (owner ^ 1)

    @pl.when(in_pool)
    def _():
        pltpu.make_async_copy(pool_ref.at[slot], dst, sem).start()

    @pl.when(in_near)
    def _():
        pltpu.make_async_copy(near_ref.at[slot], dst, sem).start()

    for holds, ref in others:

        @pl.when(jnp.logical_not(in_pool | in_near) & holds)
        def _(ref=ref):
            pltpu.make_async_copy(ref, dst, sem).start()


ANYWHERE = pl.BlockSpec(memory_space=pl.ANY)
IN_HBM = pl.BlockSpec(memory_space=pltpu.HBM)


def first_kernel(cap, states, here_ref, table_ref, pool_ref, near_ref, *rest):
    sends, (item_ref, sem) = rest[:-2], rest[-2:]
    for t in range(len(sends)):
        state = table_ref[t]

        @pl.when(state < states)
        def _(state=state, t=t):
            start_from(state, here_ref[0], pool_ref, near_ref, (), item_ref.at[t], sem.at[t])

    for t, send in enumerate(sends):

        @pl.when(table_ref[t] < states)
        def _(send=send, t=t):
            pltpu.make_async_copy(pool_ref.at[0], item_ref.at[t], sem.at[t]).wait()
            pltpu.make_async_copy(item_ref.at[t], send, sem.at[t]).start()

    for t, send in enumerate(sends):

        @pl.when(table_ref[t] < states)
        def _(send=send, t=t):
            pltpu.make_async_copy(item_ref.at[t], send, sem.at[t]).wait()


def first_sends(cap, states, here, table, pool, near):
    item = jax.ShapeDtypeStruct(pool.shape[1:], pool.dtype)
    return pl.pallas_call(
        functools.partial(first_kernel, cap, states),
        grid_spec=pltpu.PrefetchScalarGridSpec(
            num_scalar_prefetch=2,
            grid=(1,),
            in_specs=[IN_HBM, IN_HBM],
            out_specs=[IN_HBM] * LAG,
            scratch_shapes=[
                pltpu.VMEM((LAG,) + pool.shape[1:], pool.dtype),
                pltpu.SemaphoreType.DMA((LAG,)),
            ],
        ),
        out_shape=[item] * LAG,
        compiler_params=pltpu.CompilerParams(vmem_limit_bytes=SMALL_VMEM),
        name="first_sends",
    )(here, table, pool, near)


def turn_kernel(
    cap, states, sending, here_ref, table_ref, step_ref, pool_ref, near_ref, got_ref, _store_in, store_ref, *rest
):
    item_ref, sem = rest[-2:]
    step = step_ref[0]
    came = table_ref[cap + step - LAG]
    kept = came < states

    @pl.when(kept)
    def _():
        pltpu.make_async_copy(got_ref, item_ref.at[0], sem.at[0]).start()

    if sending:
        send_ref = rest[0]
        state = table_ref[step]

        @pl.when(state < states)
        def _():
            spot = jnp.minimum(state, states - 1)
            start_from(
                state,
                here_ref[0],
                pool_ref,
                near_ref,
                ((state == came, got_ref), (state != came, store_ref.at[spot])),
                item_ref.at[1],
                sem.at[1],
            )
            pltpu.make_async_copy(got_ref, item_ref.at[1], sem.at[1]).wait()
            pltpu.make_async_copy(item_ref.at[1], send_ref, sem.at[1]).start()

    @pl.when(kept)
    def _():
        pltpu.make_async_copy(got_ref, item_ref.at[0], sem.at[0]).wait()
        copy = pltpu.make_async_copy(item_ref.at[0], store_ref.at[came], sem.at[0])
        copy.start()
        copy.wait()

    if sending:

        @pl.when(state < states)
        def _():
            pltpu.make_async_copy(item_ref.at[1], send_ref, sem.at[1]).wait()


def turn(cap, states, sending, here, table, step, pool, near, got, store):
    item = jax.ShapeDtypeStruct(pool.shape[1:], pool.dtype)
    kept = jax.ShapeDtypeStruct((states + 1,) + pool.shape[1:], pool.dtype)
    aliases = {} if store is None else {6: 0}
    if store is None:
        store = jnp.zeros((16, 128), jnp.float32)
    return pl.pallas_call(
        functools.partial(turn_kernel, cap, states, sending),
        grid_spec=pltpu.PrefetchScalarGridSpec(
            num_scalar_prefetch=3,
            grid=(1,),
            in_specs=[IN_HBM] * 4,
            out_specs=[IN_HBM] * (1 + sending),
            scratch_shapes=[
                pltpu.VMEM((2,) + pool.shape[1:], pool.dtype),
                pltpu.SemaphoreType.DMA((2,)),
            ],
        ),
        out_shape=[kept, item][: 1 + sending],
        input_output_aliases=aliases,
        compiler_params=pltpu.CompilerParams(vmem_limit_bytes=SMALL_VMEM),
        name="turn_states",
    )(here, table, step, pool, near, got, store)


def take_kernel(states, here_ref, table_ref, step_ref, pool_ref, near_ref, store_ref, send_ref, item_ref, sem):
    state = table_ref[step_ref[0]]

    @pl.when(state < states)
    def _():
        spot = jnp.minimum(state, states - 1)
        start_from(state, here_ref[0], pool_ref, near_ref, ((state < states, store_ref.at[spot]),), item_ref, sem)
        pltpu.make_async_copy(pool_ref.at[0], item_ref, sem).wait()
        copy = pltpu.make_async_copy(item_ref, send_ref, sem)
        copy.start()
        copy.wait()


def take_out(states, here, table, step, pool, near, store):
    return pl.pallas_call(
        functools.partial(take_kernel, states),
        grid_spec=pltpu.PrefetchScalarGridSpec(
            num_scalar_prefetch=3,
            grid=(1,),
            in_specs=[IN_HBM] * 3,
            out_specs=IN_HBM,
            scratch_shapes=[pltpu.VMEM(pool.shape[1:], pool.dtype), pltpu.SemaphoreType.DMA],
        ),
        out_shape=jax.ShapeDtypeStruct(pool.shape[1:], pool.dtype),
        compiler_params=pltpu.CompilerParams(vmem_limit_bytes=SMALL_VMEM),
        name="take_state",
    )(here, table, step, pool, near, store)


def pick_kernel(count, here_ref, ids_ref, store_ref, out_ref, item_ref, sem):
    owner = here_ref[0]
    chip = owner // 2
    core = owner % 2

    def each(act):
        for r in range(count):
            state = ids_ref[(owner ^ 1) * count + r]
            place = state // (2 * SLOTS_DEV)
            held = jnp.where(core == 0, place < chip, place > chip)

            @pl.when(held)
            def _(state=state, r=r):
                act(state, r)

    def into(state, r):
        return pltpu.make_async_copy(store_ref.at[state], item_ref.at[r], sem.at[r])

    def out(r):
        return pltpu.make_async_copy(item_ref.at[r], out_ref.at[r], sem.at[r])

    def begin(state, r):
        into(state, r).start()

    def turn_over(state, r):
        into(state, r).wait()
        out(r).start()

    def finish(state, r):
        out(r).wait()

    each(begin)
    each(turn_over)
    each(finish)


def pick(count, here, ids, store):
    return pl.pallas_call(
        functools.partial(pick_kernel, count),
        grid_spec=pltpu.PrefetchScalarGridSpec(
            num_scalar_prefetch=2,
            grid=(1,),
            in_specs=[IN_HBM],
            out_specs=IN_HBM,
            scratch_shapes=[
                pltpu.VMEM((count,) + store.shape[1:], store.dtype),
                pltpu.SemaphoreType.DMA((count,)),
            ],
        ),
        out_shape=jax.ShapeDtypeStruct((count,) + store.shape[1:], store.dtype),
        compiler_params=pltpu.CompilerParams(vmem_limit_bytes=SMALL_VMEM),
        name="pick_states",
    )(here, ids, store)


def mamba_pre_kernel(
    heads,
    live_ref,
    first_ref,
    mix_ref,
    b_ref,
    c_ref,
    step_ref,
    decay_ref,
    skip_ref,
    spread_ref,
    split_ref,
    _pre_in,
    _z_in,
    _e_in,
    pre_ref,
    z_ref,
    e_ref,
    bs_ref,
    end_ref,
):
    block = pl.program_id(1)
    request = first_ref[0] + pl.program_id(0)
    copies = SPAN // heads
    row = lax.broadcasted_iota(jnp.int32, (SPAN, SPAN), 0)
    lane = lax.broadcasted_iota(jnp.int32, (SPAN, SPAN), 1)
    lower = row >= lane
    left = lane < MHDIM

    def three_way(value):
        high = value.astype(jnp.bfloat16)
        rest = value - high.astype(jnp.float32)
        middle = rest.astype(jnp.bfloat16)
        low = (rest - middle.astype(jnp.float32)).astype(jnp.bfloat16)
        high, middle, low = (v.astype(jnp.float32) for v in (high, middle, low))
        kept = jnp.where(
            lane < heads,
            high,
            jnp.where(lane < 2 * heads, middle, jnp.where(lane < 3 * heads, low, 0.0)),
        )
        return kept.astype(jnp.bfloat16)

    @pl.when((block == 0) | (live_ref[request] > SPAN))
    def _():
        raw = step_ref[...]
        rate_row = jnp.maximum(raw, 0.0) + jnp.log1p(jnp.exp(-jnp.abs(raw)))
        upper = jnp.where(row <= lane, 1.0, 0.0)
        cum_row = lax.dot_general(
            -rate_row * decay_ref[...],
            upper,
            (((1,), (0,)), ((), ())),
            precision=lax.Precision.HIGHEST,
            preferred_element_type=jnp.float32,
        )
        cum = jnp.concatenate([cum_row] * copies, axis=0).T
        rate_col = jnp.concatenate([rate_row] * copies, axis=0).T

        both = mm(split_ref[...], mix_ref[...])
        z_ref[...] = both[SPAN:].astype(jnp.bfloat16)
        x = both[:SPAN]
        x_half = x.astype(jnp.bfloat16)
        b = b_ref[...]
        c = c_ref[...]
        cross = mm(c, b, NT)

        def weights(h):
            fall = cum[:, h : h + 1] - cum_row[h : h + 1, :]
            fade = jnp.exp(jnp.where(lower, fall, NEG_FILL))
            return (cross * fade * rate_row[h : h + 1, :]).astype(jnp.bfloat16)

        for pair in range(heads // 2):
            cols = slice(pair * 2 * MHDIM, (pair + 1) * 2 * MHDIM)
            xp = x_half[:, cols]
            zero = jnp.zeros_like(xp)
            stacked = jnp.concatenate([jnp.where(left, xp, zero), jnp.where(left, zero, xp)], axis=0)
            w = jnp.concatenate([weights(2 * pair), weights(2 * pair + 1)], axis=1)
            pre_ref[:, cols] = mm(w, stacked) + skip_ref[:, cols] * x[:, cols]

        @pl.when(block == 0)
        def _():
            end = cum[SPAN - 1 : SPAN, :]
            tail = jnp.exp(end - cum) * rate_col
            scaled = (mm(three_way(tail), spread_ref[...]) * x).astype(jnp.bfloat16)
            bs_ref[...] = mm(scaled, b, TN).astype(jnp.bfloat16)
            end_ref[...] = jnp.broadcast_to(end, end_ref.shape)
            e_ref[...] = three_way(jnp.exp(cum))

        @pl.when(block == 1)
        def _():
            e_half = three_way(jnp.exp(cum))
            carried = mm(c, bs_ref[...], NT)
            pre_ref[...] += mm(e_half, spread_ref[...]) * carried
            e_ref[...] = three_way(jnp.exp(cum + end_ref[0:1, :]))


def mamba_pre(heads, first, count, live, here, mixed, b_rows, c_rows, step_row, decay, skip, spread, split, carry):
    width = heads * MHDIM
    rows = b_rows.shape[0]

    def at(r, k, *_):
        return ((first + r) * 2 + k, 0)

    def fixed(r, k, *_):
        return (0, 0)

    blocks = count * 2
    outs = [
        jax.ShapeDtypeStruct((rows, width), jnp.float32),
        jax.ShapeDtypeStruct((rows, width), jnp.bfloat16),
        jax.ShapeDtypeStruct((rows, 128), jnp.bfloat16),
    ]
    if carry is None:
        carry = tuple(jnp.zeros((16, 128), jnp.float32) for _ in outs)
        aliases = {}
    else:
        aliases = {10: 0, 11: 1, 12: 2}
    return pl.pallas_call(
        functools.partial(mamba_pre_kernel, heads),
        grid_spec=pltpu.PrefetchScalarGridSpec(
            num_scalar_prefetch=2,
            grid=(count, 2),
            in_specs=[
                pl.BlockSpec((2 * SPAN, width), at),
                pl.BlockSpec((SPAN, STATE), at),
                pl.BlockSpec((SPAN, STATE), at),
                pl.BlockSpec((heads, SPAN), lambda r, k, *_: (0, (first + r) * 2 + k)),
                pl.BlockSpec((heads, SPAN), fixed),
                pl.BlockSpec((1, width), fixed),
                pl.BlockSpec((128, width), fixed),
                pl.BlockSpec((2 * SPAN, 2 * SPAN), fixed),
                ANYWHERE,
                ANYWHERE,
                ANYWHERE,
            ],
            out_specs=[
                pl.BlockSpec((SPAN, width), at),
                pl.BlockSpec((SPAN, width), at),
                pl.BlockSpec((SPAN, 128), at),
            ],
            scratch_shapes=[
                pltpu.VMEM((width, STATE), jnp.bfloat16),
                pltpu.VMEM((8, 128), jnp.float32),
            ],
        ),
        out_shape=outs,
        input_output_aliases=aliases,
        compiler_params=pltpu.CompilerParams(vmem_limit_bytes=VMEM),
        cost_estimate=pl.CostEstimate(
            flops=blocks * heads * 40 * SPAN * SPAN * MHDIM,
            bytes_accessed=blocks * SPAN * width * 10,
            transcendentals=blocks * heads * SPAN * SPAN,
        ),
        name="mamba_pre",
    )(live, here + first, mixed, b_rows, c_rows, step_row, decay, skip, spread, split, *carry)


def mamba_post_kernel(
    heads,
    whole_group,
    count,
    cap,
    late,
    here_ref,
    table_ref,
    ids_ref,
    live_ref,
    pool_ref,
    near_ref,
    store_ref,
    other_ref,
    c_ref,
    pre_ref,
    z_ref,
    e_ref,
    spread_ref,
    gain_ref,
    *rest,
):
    outs = 1 if whole_group else 2
    out_refs = rest[outs : 2 * outs]
    state_ref, sem = rest[-2:]
    i = pl.program_id(0)
    width = heads * MHDIM
    owner = here_ref[0]
    chip = owner // 2
    core = owner % 2
    here_now = table_ref[2 * cap + 1]
    active = jnp.maximum(count - here_now, 1) if late else here_now

    def fetch(i):
        r = post_request(cap, count, late, i, table_ref)
        state = ids_ref[owner * count + r]
        place = state // (2 * SLOTS_DEV)
        mine = jnp.where(core == 0, place < chip, place > chip)
        slot = i % 2
        others = ((mine, store_ref.at[state]),)
        if late:
            others += ((jnp.logical_not(mine), other_ref.at[r]),)
        start_from(state, owner, pool_ref, near_ref, others, state_ref.at[slot], sem.at[slot])

    @pl.when((i == 0) & (i < active))
    def _():
        fetch(i)

    @pl.when(i + 1 < active)
    def _():
        fetch(i + 1)

    @pl.when(i < active)
    def _():
        r = post_request(cap, count, late, i, table_ref)
        pltpu.make_async_copy(pool_ref.at[0], state_ref.at[i % 2], sem.at[i % 2]).wait()
        carried = mm(c_ref[...], state_ref[i % 2], NT)
        summed = pre_ref[...] + mm(e_ref[...], spread_ref[...]) * carried
        z = z_ref[...].astype(jnp.float32)
        gated = summed * (z / (1.0 + jnp.exp(-z)))
        square = jnp.sum(gated * gated, axis=1, keepdims=True)
        if whole_group:
            norm = lax.rsqrt(square / width + EPSILON)
            live = lax.broadcasted_iota(jnp.int32, (SUF, 1), 0) < live_ref[owner * count + r]
            out_refs[0][...] = jnp.where(live, gated * norm * gain_ref[...], 0.0).astype(jnp.bfloat16)
        else:
            out_refs[0][...] = gated
            out_refs[1][...] = jnp.broadcast_to(square, (SUF, 128))


def post_request(cap, count, late, i, table_ref):
    here_now = table_ref[2 * cap + 1]
    if late:
        spot = here_now + jnp.minimum(i, jnp.maximum(count - here_now - 1, 0))
    else:
        spot = jnp.minimum(i, jnp.maximum(here_now - 1, 0))
    return table_ref[2 * cap + 2 + jnp.minimum(spot, count - 1)]


def mamba_post(heads, whole_group, cap, here, table, ids, live, pool, near, store, other, c_rows, pre, z, e3, spread, gain, carry):
    width = heads * MHDIM
    rows = c_rows.shape[0]
    count = rows // SUF
    late = carry is not None

    def at(i, here_ref, table_ref, *_):
        return (post_request(cap, count, late, i, table_ref), 0)

    def fixed(i, *_):
        return (0, 0)

    out_shape = [jax.ShapeDtypeStruct((rows, width), jnp.bfloat16 if whole_group else jnp.float32)]
    out_specs = [pl.BlockSpec((SUF, width), at)]
    if not whole_group:
        out_shape.append(jax.ShapeDtypeStruct((rows, 128), jnp.float32))
        out_specs.append(pl.BlockSpec((SUF, 128), at))
    aliases = {}
    if late:
        aliases = {14 + k: k for k in range(len(out_shape))}
    else:
        carry = [jnp.zeros((16, 128), jnp.float32)] * len(out_shape)
        other = store
    return pl.pallas_call(
        functools.partial(mamba_post_kernel, heads, whole_group, count, cap, late),
        grid_spec=pltpu.PrefetchScalarGridSpec(
            num_scalar_prefetch=4,
            grid=(count,),
            in_specs=[
                IN_HBM,
                IN_HBM,
                IN_HBM,
                IN_HBM,
                pl.BlockSpec((SUF, STATE), at),
                pl.BlockSpec((SUF, width), at),
                pl.BlockSpec((SUF, width), at),
                pl.BlockSpec((SUF, 128), at),
                pl.BlockSpec((128, width), fixed),
                pl.BlockSpec((1, width), fixed),
            ]
            + [ANYWHERE] * len(out_shape),
            out_specs=out_specs,
            scratch_shapes=[
                pltpu.VMEM((2, width, STATE), jnp.bfloat16),
                pltpu.SemaphoreType.DMA((2,)),
            ],
        ),
        out_shape=out_shape,
        input_output_aliases=aliases,
        compiler_params=pltpu.CompilerParams(vmem_limit_bytes=VMEM),
        cost_estimate=pl.CostEstimate(
            flops=2 * rows * width * STATE,
            bytes_accessed=rows * width * 6,
            transcendentals=rows * width,
        ),
        name="mamba_post",
    )(here, table, ids, live, pool, near, store, other, c_rows, pre, z, e3, spread, gain, *carry)


def attend_kernel(
    qheads,
    chips,
    first_ref,
    pages_ref,
    prefix_ref,
    live_ref,
    q_ref,
    ks_ref,
    vs_ref,
    *rest,
):
    parts = rest[: 2 * chips - 1]
    out_ref, kv_ref, s_ref, top_ref, total_ref, mixed_ref, sem = rest[2 * chips :]
    half = pl.program_id(1)
    request = first_ref[0] + pl.program_id(0)
    owner = first_ref[1]
    scale = math.log2(math.e) / math.sqrt(HD)
    pairs = prefix_ref[request] // (2 * PAGE)

    @pl.when(half == 0)
    def _():
        def begin(p, carry):
            page = pages_ref[request * MAXP + p]
            giver = page // PAGES_DEV
            core = owner % 2
            away = giver // 2 - owner // 2
            ahead = jnp.where(core == 0, -away, away)
            which = jnp.where(ahead >= 0, ahead, chips - 1 - ahead)
            carrier = jnp.where(ahead >= 0, core, 1 - core)
            spot = ((giver % 2) ^ carrier) * PAGES_DEV + page % PAGES_DEV
            for k, part in enumerate(parts):

                @pl.when(which == k)
                def _(part=part):
                    pltpu.make_async_copy(part.at[spot], kv_ref.at[p], sem).start()

            return carry

        def finish(p, carry):
            pltpu.make_async_copy(parts[0].at[0], kv_ref.at[p], sem).wait()
            return carry

        lax.fori_loop(0, 2 * pairs, begin, 0)
        lax.fori_loop(0, 2 * pairs, finish, 0)

    start = half * SPAN
    live = live_ref[request]

    def columns(h):
        return slice(h * HD, (h + 1) * HD)

    def fold(s):
        return jnp.maximum(s[:, :HD], s[:, HD:])

    @pl.when(start < live)
    def _():
        row = lax.broadcasted_iota(jnp.int32, (SPAN, SUF), 0) + start
        lane = lax.broadcasted_iota(jnp.int32, (SPAN, SUF), 1)
        causal = row >= lane
        for h in range(qheads):
            s = jnp.where(causal, mm(q_ref[:, columns(h)], ks_ref[...], NT), NEG_FILL)
            s_ref[0, h] = s
            top_ref[h] = fold(s)

        def scores(i, carry):
            keys = kv_ref[pl.ds(i * 2, 2), 0].reshape(2 * PAGE, HD)
            for h in range(qheads):
                s = mm(q_ref[:, columns(h)], keys, NT)
                s_ref[i + 1, h] = s
                top_ref[h] = jnp.maximum(top_ref[h], fold(s))
            return carry

        lax.fori_loop(0, pairs, scores, 0)

        def weigh(h, s, values):
            probs = jnp.exp2((s - jnp.concatenate([top_ref[h]] * 2, axis=1)) * scale)
            return probs[:, :HD] + probs[:, HD:], mm(probs.astype(jnp.bfloat16), values)

        for h in range(qheads):
            top_ref[h] = jnp.broadcast_to(jnp.max(top_ref[h], axis=1, keepdims=True), (SPAN, HD))
        for h in range(qheads):
            total_ref[h], mixed_ref[h] = weigh(h, s_ref[0, h], vs_ref[...])

        def values(i, carry):
            rows = kv_ref[pl.ds(i * 2, 2), 1].reshape(2 * PAGE, HD)
            for h in range(qheads):
                total, mixed = weigh(h, s_ref[i + 1, h], rows)
                total_ref[h] += total
                mixed_ref[h] += mixed
            return carry

        lax.fori_loop(0, pairs, values, 0)
        keep = lax.broadcasted_iota(jnp.int32, (SPAN, 1), 0) + start < live
        for h in range(qheads):
            total = jnp.sum(total_ref[h], axis=1, keepdims=True)
            out_ref[:, columns(h)] = jnp.where(keep, mixed_ref[h] / total, 0.0).astype(out_ref.dtype)

    @pl.when(start >= live)
    def _():
        out_ref[...] = jnp.zeros_like(out_ref)


def attention(qheads, first, count, here, pages, prefix, live, queries, keys, values, parts, carry):
    most = MAXP // 2 + 1
    width = qheads * HD
    if carry is None:
        carry = jnp.zeros((16, 128), jnp.bfloat16)
        aliases = {}
    else:
        aliases = {7 + len(parts): 0}

    def at(r, k, *_):
        return ((first + r) * 2 + k, 0)

    return pl.pallas_call(
        functools.partial(attend_kernel, qheads, (len(parts) + 1) // 2),
        grid_spec=pltpu.PrefetchScalarGridSpec(
            num_scalar_prefetch=4,
            grid=(count, 2),
            in_specs=[
                pl.BlockSpec((SPAN, width), at),
                pl.BlockSpec((SUF, HD), lambda r, k, *_: (first + r, 0)),
                pl.BlockSpec((SUF, HD), lambda r, k, *_: (first + r, 0)),
            ]
            + [IN_HBM] * len(parts)
            + [ANYWHERE],
            out_specs=pl.BlockSpec((SPAN, width), at),
            scratch_shapes=[
                pltpu.VMEM((MAXP, 2, PAGE, HD), jnp.bfloat16),
                pltpu.VMEM((most, qheads, SPAN, 2 * PAGE), jnp.float32),
                pltpu.VMEM((qheads, SPAN, HD), jnp.float32),
                pltpu.VMEM((qheads, SPAN, HD), jnp.float32),
                pltpu.VMEM((qheads, SPAN, HD), jnp.float32),
                pltpu.SemaphoreType.DMA,
            ],
        ),
        out_shape=jax.ShapeDtypeStruct(queries.shape, jnp.bfloat16),
        input_output_aliases=aliases,
        compiler_params=pltpu.CompilerParams(vmem_limit_bytes=VMEM),
        cost_estimate=pl.CostEstimate(
            flops=count * qheads * SUF * (MAXP * PAGE + SUF) * HD * 4,
            bytes_accessed=count * (SUF * qheads * HD * 4 + MAXP * PAGE * HD * 4),
            transcendentals=count * qheads * SUF * (MAXP * PAGE + SUF),
        ),
        name="attention",
    )(here, pages, prefix, live, queries, keys, values, *parts, carry)


def after(value, *others):
    return lax.optimization_barrier((value,) + others)[0]


def body(
    mixer_input,
    step_raw,
    decay_rate,
    skip_gain,
    state_proj,
    queries,
    suffix_kv,
    state_pool,
    page_pool,
    norm_gain,
    hit_owner,
    hit_slot,
    page_owner,
    page_slot,
    prefix_len,
    suffix_len,
):
    owners = lax.axis_size("owner")
    owner = lax.axis_index("owner").astype(jnp.int32)
    column = lax.axis_index("tensor")
    rows = mixer_input.shape[0]
    count = rows // SUF
    heads = decay_rate.shape[0]
    width = heads * MHDIM
    qheads = queries.shape[1] // HD
    per_group = SSM_HEAD_TOTAL // GROUPS
    group = column * heads // per_group
    kv_index = column * qheads // (QHEADS // KVHEADS)
    whole_group = heads == per_group
    chips = owners // 2
    per_chip = 2 * SLOTS_DEV
    states = owners * SLOTS_DEV
    here = owner.reshape(1)
    first = (owner * count).reshape(1)
    swap = [(o, o ^ 1) for o in range(owners)]

    def line(hop):
        up = [(o, o + 2) for o in range(0, owners - 2, 2) if o // 2 >= hop - 1]
        return up + [(o, o - 2) for o in range(3, owners, 2) if o // 2 <= chips - hop]

    def head_of(array, index, axis):
        return lax.dynamic_index_in_dim(array, index, axis, keepdims=False)

    pool = state_pool.reshape(SLOTS_DEV, width, STATE)
    near = lax.ppermute(pool, "owner", swap)
    own_pages = jnp.transpose(head_of(page_pool, kv_index, 3), (0, 2, 1, 3))
    near_pages = lax.ppermute(own_pages, "owner", swap)
    chip_pages = jnp.concatenate([own_pages, near_pages], axis=0)

    state_ids = (hit_owner[:, 0] * SLOTS_DEV + hit_slot).astype(jnp.int32)
    table, cap = route(state_ids, owner, chips, per_chip, 2 * count)

    def send(item):
        return lax.ppermute(item, "owner", line(1))

    spread_np = np.zeros((128, width), np.float32)
    for h in range(heads):
        for k in range(3):
            spread_np[k * heads + h, h * MHDIM : (h + 1) * MHDIM] = 1.0
    spread = jnp.asarray(spread_np, jnp.bfloat16)
    split_np = np.zeros((2 * SPAN, 2 * SPAN), np.float32)
    for i in range(SPAN):
        split_np[i, 2 * i] = 1.0
        split_np[SPAN + i, 2 * i + 1] = 1.0
    split = jnp.asarray(split_np, jnp.bfloat16)
    skip = jnp.repeat(skip_gain, MHDIM)[None, :]
    decay = jnp.broadcast_to(decay_rate[:, None], (heads, SPAN))
    step_row = step_raw.T
    page_ids = (page_owner[:, :, 0] * PAGES_DEV + page_slot).astype(jnp.int32).reshape(-1)
    made = {}

    def shape_inputs(tie):
        made["mixed"] = after(mixer_input, tie).reshape(2 * rows, width)
        maps = head_of(after(state_proj, tie), group, 2)
        made["b"], made["c"] = maps[:, 0], maps[:, 1]
        suffix = head_of(after(suffix_kv, tie), kv_index, 2)
        made["k"], made["v"] = suffix[:, 0], suffix[:, 1]
        return made["mixed"], made["b"], made["k"]

    def pre_part(r):
        def run(tie):
            made["pre"] = mamba_pre(
                heads,
                r,
                2,
                suffix_len,
                after(first, tie),
                made["mixed"],
                made["b"],
                made["c"],
                step_row,
                decay,
                skip,
                spread,
                split,
                made.get("pre"),
            )
            return (made["pre"][2],)

        return run

    def attention_part(r):
        def run(tie):
            place = jnp.concatenate([first + r, here])
            made["attn"] = attention(
                qheads,
                r,
                1,
                after(place, tie),
                page_ids,
                prefix_len,
                suffix_len,
                queries,
                made["k"],
                made["v"],
                made["parts"],
                made.get("attn"),
            )
            return (made["attn"],)

        return run

    beside = [shape_inputs] + [pre_part(r) for r in range(0, count, 2)]
    ours, theirs = [], []
    piece = chip_pages
    for hop in range(1, chips):
        done = (table, near) if hop == 1 else ()
        got = lax.ppermute(piece, "owner", line(hop))
        tie = piece
        if hop == chips - 1:
            sends = first_sends(cap, states, after(here, piece), table, pool, near)
            flying = [send(item) for item in sends]
            tie = sends[-1]
        if beside:
            done += beside.pop(0)(tie)
        if theirs:
            done += (theirs[-1],)
        piece = after(got, *done)
        ours.append(piece)
        theirs.append(lax.ppermute(piece, "owner", swap))
    made["parts"] = [chip_pages] + ours + theirs

    beside += [attention_part(r) for r in range(count)]
    store = None
    tie = piece
    for step in range(LAG, FIXED_STEPS):
        part = beside.pop(0) if beside else None
        done = part(tie) if part else ()
        got = after(flying.pop(0), *done)
        store, item = turn(
            cap, states, True, here, table, jnp.full((1,), step, jnp.int32), pool, near, got, store
        )
        flying.append(send(item))
        tie = item
    for step in range(FIXED_STEPS, FIXED_STEPS + LAG):
        part = beside.pop(0) if beside else None
        done = part(tie) if part else ()
        got = after(flying.pop(0), *done)
        (store,) = turn(cap, states, False, here, table, jnp.full((1,), step, jnp.int32), pool, near, got, store)
        tie = store
    while beside:
        part = beside.pop(0)
        if part:
            part(tie)

    def late(step, store):
        item = take_out(states, here, table, step.reshape(1), pool, near, store)
        (store,) = turn(
            cap, states, False, here, table, (step + LAG).reshape(1), pool, near, send(item), store
        )
        return store

    store = lax.fori_loop(FIXED_STEPS, table[2 * cap], late, store)

    picked = pick(count, here, state_ids, store)
    other = lax.ppermute(picked, "owner", swap)
    result = None
    for place in (after(here, picked), here):
        result = mamba_post(
            heads,
            whole_group,
            cap,
            place,
            table,
            state_ids,
            suffix_len,
            pool,
            near,
            store,
            other,
            made["c"],
            *made["pre"],
            spread,
            norm_gain[None, :],
            result,
        )
    if whole_group:
        return (result[0], made["attn"])
    gated, partial_sum = result
    partial_sum = partial_sum[:, 0]
    spread_sum = jnp.where(jnp.arange(GROUPS)[:, None] == group, partial_sum[None, :], 0.0)
    totals = lax.psum(spread_sum, "tensor")
    square = lax.dynamic_index_in_dim(totals, group, 0, keepdims=False) / (per_group * MHDIM)
    my_suffix = lax.dynamic_slice_in_dim(suffix_len, first[0], count, 0)
    active = (jnp.arange(SUF)[None, :] < my_suffix[:, None]).reshape(-1)
    scaled = gated * lax.rsqrt(square + EPSILON)[:, None] * norm_gain[None, :]
    return (jnp.where(active[:, None], scaled, 0.0).astype(jnp.bfloat16), made["attn"])


def solution(mesh):
    return jax.shard_map(
        body,
        mesh=mesh,
        in_specs=(
            P("owner", None, "tensor"),
            P("owner", "tensor"),
            P("tensor"),
            P("tensor"),
            P("owner", None, None, None),
            P("owner", "tensor"),
            P("owner", None, None, None),
            P("owner", "tensor"),
            P("owner", None, None, None, None),
            P("tensor"),
            P(),
            P(),
            P(),
            P(),
            P(),
            P(),
        ),
        out_specs=(P("owner", "tensor"), P("owner", "tensor")),
        check_vma=False,
    )
```

```python
import functools
import math

import jax
import jax.numpy as jnp
import numpy as np
from jax import lax
from jax.experimental import pallas as pl
from jax.experimental.pallas import tpu as pltpu
from jax.sharding import PartitionSpec as P

SSM_HEAD_TOTAL = 128
MHDIM = 64
STATE = 256
GROUPS = 4
QHEADS = 32
KVHEADS = 4
HD = 128
PAGE = 128
SPAN = 128
SUF = 256
MAXP = 16
SLOTS_DEV = 4
PAGES_DEV = 16

EPSILON = 1e-05
NEG_FILL = -1e30
LAG = 2
FIXED_STEPS = 8
VMEM = 48 * 1024 * 1024
SMALL_VMEM = 58 * 1024 * 1024

NT = (((1,), (1,)), ((), ()))
TN = (((0,), (0,)), ((), ()))


def mm(a, b, dims=(((1,), (0,)), ((), ()))):
    return lax.dot_general(a, b, dims, preferred_element_type=jnp.float32)


def route_kernel(chips, per_chip, reqs_per_chip, cap, ids_ref, here_ref, out_ref, need_ref, own_ref, tab_ref, code_ref):
    states = chips * per_chip
    chip_here = here_ref[0] // 2
    core_here = here_ref[0] % 2

    def clear(s, carry):
        need_ref[s] = 0
        return carry

    lax.fori_loop(0, states, clear, 0)

    def mark(r, carry):
        s = ids_ref[r]
        need_ref[s] = need_ref[s] | (1 << (r // reqs_per_chip))
        return carry

    lax.fori_loop(0, chips * reqs_per_chip, mark, 0)

    def put(base, length, row, from_ref):
        def one(t, carry):
            spot = jnp.clip(base + t, 0, 2 * chips * cap - 1)
            out_ref[row * cap + t] = jnp.where(t < length, from_ref[spot], states)
            return carry

        lax.fori_loop(0, cap, one, 0)

    steps = jnp.int32(0)
    for up in (True, False):
        before = jnp.int32(0)
        sent = jnp.int32(0)
        came = jnp.int32(0)
        for place in range(chips - 1):
            chip = place if up else chips - 1 - place
            base = ((0 if up else chips) + place) * cap

            def wanted(s, further=0, chip=chip, up=up):
                if up:
                    return (need_ref[s] >> (chip + 1 + further)) != 0
                return (need_ref[s] & ((1 << max(chip - further, 0)) - 1)) != 0

            count = jnp.int32(0)
            for far in (True, False):

                def own(i, n, far=far, chip=chip, wanted=wanted):
                    s = chip * per_chip + i
                    own_ref[n] = s
                    beyond = wanted(s, 1)
                    take = beyond if far else wanted(s) & jnp.logical_not(beyond)
                    return n + take.astype(jnp.int32)

                count = lax.fori_loop(0, per_chip, own, count)

            def fill(t, used, base=base, count=count):
                s = jnp.where(used < count, own_ref[used], states)
                tab_ref[base + t] = s
                code_ref[base + t] = s
                return jnp.minimum(used + 1, count)

            def forward(j, carry, base=base, wanted=wanted, fill=fill):
                t, used = carry
                s = tab_ref[base - cap + j]
                take = (s < states) & wanted(jnp.minimum(s, states - 1))
                later = jnp.where(take, jnp.maximum(t, j + LAG), t)
                used = lax.fori_loop(t, later, fill, used)
                tab_ref[base + later] = s
                code_ref[base + later] = states + 1 + j
                return later + take.astype(jnp.int32), used

            t, used = jnp.int32(0), jnp.int32(0)
            if place:
                t, used = lax.fori_loop(0, before, forward, (t, used))
            end = t + count - used
            lax.fori_loop(t, end, fill, used)
            before = end
            sent = jnp.where(chip_here == chip, end, sent)
            came = jnp.where(chip_here == (chip + 1 if up else chip - 1), end, came)
            steps = jnp.maximum(steps, end)
        here = chip_here if up else chips - 1 - chip_here
        side = 0 if up else chips

        @pl.when(core_here == (0 if up else 1))
        def _(here=here, side=side, sent=sent, came=came):
            put((side + here) * cap, sent, 0, code_ref)
            put((side + here - 1) * cap, came, 1, tab_ref)

        arrived = came if up else jnp.where(core_here == 0, arrived, came)

    out_ref[2 * cap] = steps
    mine = reqs_per_chip // 2
    asked = [here_ref[0] * mine + r for r in range(mine)] + [(here_ref[0] ^ 1) * mine + r for r in range(mine)]
    for k, request in enumerate(asked):
        state = ids_ref[request]
        out_ref[2 * cap + 3 + mine + k] = jnp.where(state // per_chip == chip_here, state, -1)

    def look(t, carry):
        came_now = out_ref[cap + t]
        for k, request in enumerate(asked):

            @pl.when(ids_ref[request] == came_now)
            def _(k=k):
                out_ref[2 * cap + 3 + mine + k] = states + 1 + t

        return carry

    lax.fori_loop(0, arrived, look, 0)
    found = jnp.int32(0)
    for here_now in (True, False):
        for r in range(mine):
            out_ref[2 * cap + 2 + found] = r
            found += ((out_ref[2 * cap + 3 + mine + r] >= 0) == here_now).astype(jnp.int32)
        if here_now:
            out_ref[2 * cap + 1] = found


def route(state_ids, owner, chips, per_chip, reqs_per_chip):
    cap = chips * per_chip + LAG * chips + 8
    smem = pl.BlockSpec(memory_space=pltpu.SMEM)
    table = pl.pallas_call(
        functools.partial(route_kernel, chips, per_chip, reqs_per_chip, cap),
        out_shape=jax.ShapeDtypeStruct((2 * cap + 4 + 2 * reqs_per_chip,), jnp.int32),
        in_specs=[smem, smem],
        out_specs=smem,
        scratch_shapes=[
            pltpu.SMEM((chips * per_chip,), jnp.int32),
            pltpu.SMEM((2 * per_chip,), jnp.int32),
            pltpu.SMEM((2 * chips * cap,), jnp.int32),
            pltpu.SMEM((2 * chips * cap,), jnp.int32),
        ],
        name="route_states",
    )(state_ids, owner.reshape(1))
    return table, cap


ANYWHERE = pl.BlockSpec(memory_space=pl.ANY)
IN_HBM = pl.BlockSpec(memory_space=pltpu.HBM)
PIECES = 4


def piece_of(ref, k):
    rows = ref.shape[0] // PIECES
    return ref.at[pl.ds(k * rows, rows)]


def start_from(code, states, owner, pool_ref, near_ref, came_refs, late_ref, dst, sems):
    def start(ref):
        for k in range(PIECES):
            pltpu.make_async_copy(piece_of(ref, k), piece_of(dst, k), sems.at[k]).start()

    if pool_ref is not None:
        own = (code >= 0) & (code < states)
        slot = code % SLOTS_DEV

        @pl.when(own & (code // SLOTS_DEV == owner))
        def _():
            start(pool_ref.at[slot])

        @pl.when(own & (code // SLOTS_DEV != owner))
        def _():
            start(near_ref.at[slot])

    step = code - states - 1
    for k, ref in enumerate(came_refs):

        @pl.when(step == k)
        def _(ref=ref):
            start(ref)

    if late_ref is not None:

        @pl.when(step >= len(came_refs))
        def _():
            start(late_ref.at[step - len(came_refs)])


def pass_on(src, dst, sems):
    for k in range(PIECES):
        pltpu.make_async_copy(piece_of(dst, k), piece_of(src, k), sems.at[k]).wait()
        pltpu.make_async_copy(piece_of(src, k), piece_of(dst, k), sems.at[k]).start()


def finish(src, dst, sems):
    for k in range(PIECES):
        pltpu.make_async_copy(piece_of(src, k), piece_of(dst, k), sems.at[k]).wait()


def take_kernel(states, steps, late, here_ref, table_ref, step_ref, pool_ref, near_ref, *rest):
    sends, (item_ref, sem) = rest[-2 - steps : -2], rest[-2:]
    came_refs = rest[: -2 - steps]
    late_ref = None
    if late:
        came_refs, late_ref = came_refs[:-1], came_refs[-1]
    codes = [table_ref[step_ref[0] + t] for t in range(steps)]
    for t in range(steps):
        start_from(
            codes[t], states, here_ref[0], pool_ref, near_ref, came_refs, late_ref, item_ref.at[t], sem.at[t]
        )
    for act in (pass_on, finish):
        for t in range(steps):

            @pl.when(codes[t] != states)
            def _(t=t):
                act(item_ref.at[t], sends[t], sem.at[t])


def take(states, steps, here, table, step, pool, near, came, late=None):
    item = jax.ShapeDtypeStruct(pool.shape[1:], pool.dtype)
    came = list(came) + ([] if late is None else [late])
    return pl.pallas_call(
        functools.partial(take_kernel, states, steps, late is not None),
        grid_spec=pltpu.PrefetchScalarGridSpec(
            num_scalar_prefetch=3,
            grid=(1,),
            in_specs=[IN_HBM] * (2 + len(came)),
            out_specs=[IN_HBM] * steps,
            scratch_shapes=[
                pltpu.VMEM((steps,) + pool.shape[1:], pool.dtype),
                pltpu.SemaphoreType.DMA((steps, PIECES)),
            ],
        ),
        out_shape=[item] * steps,
        compiler_params=pltpu.CompilerParams(vmem_limit_bytes=SMALL_VMEM),
        name="take_states",
    )(here, table, step, pool, near, *came)


def keep_kernel(step_ref, got_ref, _late_in, late_ref, item_ref, sem):
    spot = late_ref.at[step_ref[0] - FIXED_STEPS]
    for k in range(PIECES):
        pltpu.make_async_copy(piece_of(got_ref, k), piece_of(item_ref, k), sem.at[k]).start()
    pass_on(item_ref, spot, sem)
    finish(item_ref, spot, sem)


def keep(step, got, late):
    return pl.pallas_call(
        keep_kernel,
        grid_spec=pltpu.PrefetchScalarGridSpec(
            num_scalar_prefetch=1,
            grid=(1,),
            in_specs=[IN_HBM, IN_HBM],
            out_specs=IN_HBM,
            scratch_shapes=[pltpu.VMEM(got.shape, got.dtype), pltpu.SemaphoreType.DMA((PIECES,))],
        ),
        out_shape=jax.ShapeDtypeStruct(late.shape, late.dtype),
        input_output_aliases={2: 0},
        compiler_params=pltpu.CompilerParams(vmem_limit_bytes=SMALL_VMEM),
        name="keep_state",
    )(step, got, late)


def blank_kernel(here_ref, out_ref):
    pass


def blank(here, shape, dtype):
    return pl.pallas_call(
        blank_kernel,
        in_specs=[pl.BlockSpec(memory_space=pltpu.SMEM)],
        out_specs=IN_HBM,
        out_shape=jax.ShapeDtypeStruct(shape, dtype),
        compiler_params=pltpu.CompilerParams(vmem_limit_bytes=SMALL_VMEM),
        name="room",
    )(here)


def pick_kernel(states, cap, count, table_ref, *rest):
    came_refs, late_ref = rest[:-4], rest[-4]
    out_ref, item_ref, sem = rest[-3:]
    codes = [table_ref[2 * cap + 3 + 2 * count + r] for r in range(count)]
    for r in range(count):

        @pl.when(codes[r] > states)
        def _(r=r):
            start_from(codes[r], states, -1, None, None, came_refs, late_ref, item_ref.at[r], sem.at[r])

    for act in (pass_on, finish):
        for r in range(count):

            @pl.when(codes[r] > states)
            def _(r=r):
                act(item_ref.at[r], out_ref.at[r], sem.at[r])


def pick(states, cap, count, table, came, late):
    shape = (count,) + late.shape[1:]
    return pl.pallas_call(
        functools.partial(pick_kernel, states, cap, count),
        grid_spec=pltpu.PrefetchScalarGridSpec(
            num_scalar_prefetch=1,
            grid=(1,),
            in_specs=[IN_HBM] * (len(came) + 1),
            out_specs=IN_HBM,
            scratch_shapes=[
                pltpu.VMEM(shape, late.dtype),
                pltpu.SemaphoreType.DMA((count, PIECES)),
            ],
        ),
        out_shape=jax.ShapeDtypeStruct(shape, late.dtype),
        compiler_params=pltpu.CompilerParams(vmem_limit_bytes=SMALL_VMEM),
        name="pick_states",
    )(table, *came, late)


def mamba_pre_kernel(
    heads,
    live_ref,
    first_ref,
    mix_ref,
    b_ref,
    c_ref,
    step_ref,
    decay_ref,
    skip_ref,
    spread_ref,
    split_ref,
    _pre_in,
    _z_in,
    _e_in,
    pre_ref,
    z_ref,
    e_ref,
    bs_ref,
    end_ref,
):
    block = pl.program_id(1)
    request = first_ref[0] + pl.program_id(0)
    copies = SPAN // heads
    row = lax.broadcasted_iota(jnp.int32, (SPAN, SPAN), 0)
    lane = lax.broadcasted_iota(jnp.int32, (SPAN, SPAN), 1)
    lower = row >= lane
    left = lane < MHDIM

    def three_way(value):
        high = value.astype(jnp.bfloat16)
        rest = value - high.astype(jnp.float32)
        middle = rest.astype(jnp.bfloat16)
        low = (rest - middle.astype(jnp.float32)).astype(jnp.bfloat16)
        high, middle, low = (v.astype(jnp.float32) for v in (high, middle, low))
        kept = jnp.where(
            lane < heads,
            high,
            jnp.where(lane < 2 * heads, middle, jnp.where(lane < 3 * heads, low, 0.0)),
        )
        return kept.astype(jnp.bfloat16)

    @pl.when((block == 0) | (live_ref[request] > SPAN))
    def _():
        raw = step_ref[...]
        rate_row = jnp.maximum(raw, 0.0) + jnp.log1p(jnp.exp(-jnp.abs(raw)))
        upper = jnp.where(row <= lane, 1.0, 0.0)
        cum_row = lax.dot_general(
            -rate_row * decay_ref[...],
            upper,
            (((1,), (0,)), ((), ())),
            precision=lax.Precision.HIGHEST,
            preferred_element_type=jnp.float32,
        )
        cum = jnp.concatenate([cum_row] * copies, axis=0).T
        rate_col = jnp.concatenate([rate_row] * copies, axis=0).T

        both = mm(split_ref[...], mix_ref[...])
        z_ref[...] = both[SPAN:].astype(jnp.bfloat16)
        x = both[:SPAN]
        x_half = x.astype(jnp.bfloat16)
        b = b_ref[...]
        c = c_ref[...]
        cross = mm(c, b, NT)

        def weights(h):
            fall = cum[:, h : h + 1] - cum_row[h : h + 1, :]
            fade = jnp.exp(jnp.where(lower, fall, NEG_FILL))
            return (cross * fade * rate_row[h : h + 1, :]).astype(jnp.bfloat16)

        for pair in range(heads // 2):
            cols = slice(pair * 2 * MHDIM, (pair + 1) * 2 * MHDIM)
            xp = x_half[:, cols]
            zero = jnp.zeros_like(xp)
            stacked = jnp.concatenate([jnp.where(left, xp, zero), jnp.where(left, zero, xp)], axis=0)
            w = jnp.concatenate([weights(2 * pair), weights(2 * pair + 1)], axis=1)
            pre_ref[:, cols] = mm(w, stacked) + skip_ref[:, cols] * x[:, cols]

        @pl.when(block == 0)
        def _():
            end = cum[SPAN - 1 : SPAN, :]
            tail = jnp.exp(end - cum) * rate_col
            scaled = (mm(three_way(tail), spread_ref[...]) * x).astype(jnp.bfloat16)
            bs_ref[...] = mm(scaled, b, TN).astype(jnp.bfloat16)
            end_ref[...] = jnp.broadcast_to(end, end_ref.shape)
            e_ref[...] = three_way(jnp.exp(cum))

        @pl.when(block == 1)
        def _():
            e_half = three_way(jnp.exp(cum))
            carried = mm(c, bs_ref[...], NT)
            pre_ref[...] += mm(e_half, spread_ref[...]) * carried
            e_ref[...] = three_way(jnp.exp(cum + end_ref[0:1, :]))


def mamba_pre(heads, first, count, live, here, mixed, b_rows, c_rows, step_row, decay, skip, spread, split, carry):
    width = heads * MHDIM
    rows = b_rows.shape[0]

    def at(r, k, *_):
        return ((first + r) * 2 + k, 0)

    def fixed(r, k, *_):
        return (0, 0)

    blocks = count * 2
    outs = [
        jax.ShapeDtypeStruct((rows, width), jnp.float32),
        jax.ShapeDtypeStruct((rows, width), jnp.bfloat16),
        jax.ShapeDtypeStruct((rows, 128), jnp.bfloat16),
    ]
    if carry is None:
        carry = tuple(jnp.zeros((16, 128), jnp.float32) for _ in outs)
        aliases = {}
    else:
        aliases = {10: 0, 11: 1, 12: 2}
    return pl.pallas_call(
        functools.partial(mamba_pre_kernel, heads),
        grid_spec=pltpu.PrefetchScalarGridSpec(
            num_scalar_prefetch=2,
            grid=(count, 2),
            in_specs=[
                pl.BlockSpec((2 * SPAN, width), at),
                pl.BlockSpec((SPAN, STATE), at),
                pl.BlockSpec((SPAN, STATE), at),
                pl.BlockSpec((heads, SPAN), lambda r, k, *_: (0, (first + r) * 2 + k)),
                pl.BlockSpec((heads, SPAN), fixed),
                pl.BlockSpec((1, width), fixed),
                pl.BlockSpec((128, width), fixed),
                pl.BlockSpec((2 * SPAN, 2 * SPAN), fixed),
                ANYWHERE,
                ANYWHERE,
                ANYWHERE,
            ],
            out_specs=[
                pl.BlockSpec((SPAN, width), at),
                pl.BlockSpec((SPAN, width), at),
                pl.BlockSpec((SPAN, 128), at),
            ],
            scratch_shapes=[
                pltpu.VMEM((width, STATE), jnp.bfloat16),
                pltpu.VMEM((8, 128), jnp.float32),
            ],
        ),
        out_shape=outs,
        input_output_aliases=aliases,
        compiler_params=pltpu.CompilerParams(vmem_limit_bytes=VMEM),
        cost_estimate=pl.CostEstimate(
            flops=blocks * heads * 40 * SPAN * SPAN * MHDIM,
            bytes_accessed=blocks * SPAN * width * 10,
            transcendentals=blocks * heads * SPAN * SPAN,
        ),
        name="mamba_pre",
    )(live, here + first, mixed, b_rows, c_rows, step_row, decay, skip, spread, split, *carry)


def mamba_post_kernel(
    heads,
    whole_group,
    count,
    cap,
    states,
    late,
    here_ref,
    table_ref,
    live_ref,
    *rest,
):
    outs = 1 if whole_group else 2
    pool_ref, near_ref, *came_refs, late_ref, other_ref = rest[: FIXED_STEPS + 4]
    c_ref, pre_ref, z_ref, e_ref, spread_ref, gain_ref, *rest = rest[FIXED_STEPS + 4 :]
    out_refs = rest[outs : 2 * outs]
    state_ref, sem = rest[-2:]
    i = pl.program_id(0)
    width = heads * MHDIM
    owner = here_ref[0]
    here_now = table_ref[2 * cap + 1]
    active = jnp.maximum(count - here_now, 1) if late else here_now

    def fetch(i):
        r = post_request(cap, count, late, i, table_ref)
        code = table_ref[2 * cap + 3 + count + r]
        slot = i % 2
        start_from(
            code, states, owner, pool_ref, near_ref, came_refs, late_ref, state_ref.at[slot], sem.at[slot]
        )
        if late:

            @pl.when(code < 0)
            def _():
                for k in range(PIECES):
                    pltpu.make_async_copy(
                        piece_of(other_ref.at[r], k), piece_of(state_ref.at[slot], k), sem.at[slot, k]
                    ).start()

    @pl.when((i == 0) & (i < active))
    def _():
        fetch(i)

    @pl.when(i + 1 < active)
    def _():
        fetch(i + 1)

    @pl.when(i < active)
    def _():
        r = post_request(cap, count, late, i, table_ref)
        finish(pool_ref.at[0], state_ref.at[i % 2], sem.at[i % 2])
        carried = mm(c_ref[...], state_ref[i % 2], NT)
        summed = pre_ref[...] + mm(e_ref[...], spread_ref[...]) * carried
        z = z_ref[...].astype(jnp.float32)
        gated = summed * (z / (1.0 + jnp.exp(-z)))
        square = jnp.sum(gated * gated, axis=1, keepdims=True)
        if whole_group:
            norm = lax.rsqrt(square / width + EPSILON)
            live = lax.broadcasted_iota(jnp.int32, (SUF, 1), 0) < live_ref[owner * count + r]
            out_refs[0][...] = jnp.where(live, gated * norm * gain_ref[...], 0.0).astype(jnp.bfloat16)
        else:
            out_refs[0][...] = gated
            out_refs[1][...] = jnp.broadcast_to(square, (SUF, 128))


def post_request(cap, count, late, i, table_ref):
    here_now = table_ref[2 * cap + 1]
    if late:
        spot = here_now + jnp.minimum(i, jnp.maximum(count - here_now - 1, 0))
    else:
        spot = jnp.minimum(i, jnp.maximum(here_now - 1, 0))
    return table_ref[2 * cap + 2 + jnp.minimum(spot, count - 1)]


def mamba_post(
    heads, whole_group, cap, states, here, table, live, pool, near, came, late_room, other, c_rows, pre, z, e3, spread, gain, carry
):
    width = heads * MHDIM
    rows = c_rows.shape[0]
    count = rows // SUF
    late = carry is not None

    def at(i, here_ref, table_ref, *_):
        return (post_request(cap, count, late, i, table_ref), 0)

    def fixed(i, *_):
        return (0, 0)

    out_shape = [jax.ShapeDtypeStruct((rows, width), jnp.bfloat16 if whole_group else jnp.float32)]
    out_specs = [pl.BlockSpec((SUF, width), at)]
    if not whole_group:
        out_shape.append(jax.ShapeDtypeStruct((rows, 128), jnp.float32))
        out_specs.append(pl.BlockSpec((SUF, 128), at))
    aliases = {}
    if late:
        aliases = {3 + FIXED_STEPS + 10 + k: k for k in range(len(out_shape))}
    else:
        carry = [jnp.zeros((16, 128), jnp.float32)] * len(out_shape)
        other = late_room
    return pl.pallas_call(
        functools.partial(mamba_post_kernel, heads, whole_group, count, cap, states, late),
        grid_spec=pltpu.PrefetchScalarGridSpec(
            num_scalar_prefetch=3,
            grid=(count,),
            in_specs=[IN_HBM] * (FIXED_STEPS + 4)
            + [
                pl.BlockSpec((SUF, STATE), at),
                pl.BlockSpec((SUF, width), at),
                pl.BlockSpec((SUF, width), at),
                pl.BlockSpec((SUF, 128), at),
                pl.BlockSpec((128, width), fixed),
                pl.BlockSpec((1, width), fixed),
            ]
            + [ANYWHERE] * len(out_shape),
            out_specs=out_specs,
            scratch_shapes=[
                pltpu.VMEM((2, width, STATE), jnp.bfloat16),
                pltpu.SemaphoreType.DMA((2, PIECES)),
            ],
        ),
        out_shape=out_shape,
        input_output_aliases=aliases,
        compiler_params=pltpu.CompilerParams(vmem_limit_bytes=VMEM),
        cost_estimate=pl.CostEstimate(
            flops=2 * rows * width * STATE,
            bytes_accessed=rows * width * 6,
            transcendentals=rows * width,
        ),
        name="mamba_post",
    )(here, table, live, pool, near, *came, late_room, other, c_rows, pre, z, e3, spread, gain, *carry)


def attend_kernel(
    qheads,
    chips,
    half,
    first_ref,
    pages_ref,
    prefix_ref,
    live_ref,
    q_ref,
    ks_ref,
    vs_ref,
    *rest,
):
    parts = rest[: 2 * chips - 1]
    out_ref, kv_ref, s_ref, top_ref, total_ref, mixed_ref, sem = rest[2 * chips :]
    request = first_ref[0]
    owner = first_ref[1]
    scale = math.log2(math.e) / math.sqrt(HD)
    pairs = prefix_ref[request] // (2 * PAGE)

    start = half * SPAN
    live = live_ref[request]

    def columns(h):
        return slice(h * HD, (h + 1) * HD)

    def fold(s):
        return jnp.maximum(s[:, :HD], s[:, HD:])

    @pl.when(start < live)
    def _():
        def begin(p, carry):
            page = pages_ref[request * MAXP + p]
            giver = page // PAGES_DEV
            core = owner % 2
            away = giver // 2 - owner // 2
            ahead = jnp.where(core == 0, -away, away)
            which = jnp.where(ahead >= 0, ahead, chips - 1 - ahead)
            carrier = jnp.where(ahead >= 0, core, 1 - core)
            spot = ((giver % 2) ^ carrier) * PAGES_DEV + page % PAGES_DEV
            for k, part in enumerate(parts):

                @pl.when(which == k)
                def _(part=part):
                    pltpu.make_async_copy(part.at[spot], kv_ref.at[p], sem).start()

            return carry

        def end(p, carry):
            pltpu.make_async_copy(parts[0].at[0], kv_ref.at[p], sem).wait()
            return carry

        lax.fori_loop(0, 2 * pairs, begin, 0)
        row = lax.broadcasted_iota(jnp.int32, (SPAN, SUF), 0) + start
        lane = lax.broadcasted_iota(jnp.int32, (SPAN, SUF), 1)
        causal = row >= lane
        for h in range(qheads):
            s = jnp.where(causal, mm(q_ref[:, columns(h)], ks_ref[...], NT), NEG_FILL)
            s_ref[0, h] = s
            top_ref[h] = fold(s)
        lax.fori_loop(0, 2 * pairs, end, 0)

        def scores(i, carry):
            keys = kv_ref[pl.ds(i * 2, 2), 0].reshape(2 * PAGE, HD)
            for h in range(qheads):
                s = mm(q_ref[:, columns(h)], keys, NT)
                s_ref[i + 1, h] = s
                top_ref[h] = jnp.maximum(top_ref[h], fold(s))
            return carry

        lax.fori_loop(0, pairs, scores, 0)

        def weigh(h, s, values):
            probs = jnp.exp2((s - jnp.concatenate([top_ref[h]] * 2, axis=1)) * scale)
            return probs[:, :HD] + probs[:, HD:], mm(probs.astype(jnp.bfloat16), values)

        for h in range(qheads):
            top_ref[h] = jnp.broadcast_to(jnp.max(top_ref[h], axis=1, keepdims=True), (SPAN, HD))
        for h in range(qheads):
            total_ref[h], mixed_ref[h] = weigh(h, s_ref[0, h], vs_ref[...])

        def values(i, carry):
            rows = kv_ref[pl.ds(i * 2, 2), 1].reshape(2 * PAGE, HD)
            for h in range(qheads):
                total, mixed = weigh(h, s_ref[i + 1, h], rows)
                total_ref[h] += total
                mixed_ref[h] += mixed
            return carry

        lax.fori_loop(0, pairs, values, 0)
        keep = lax.broadcasted_iota(jnp.int32, (SPAN, 1), 0) + start < live
        for h in range(qheads):
            total = jnp.sum(total_ref[h], axis=1, keepdims=True)
            out_ref[:, columns(h)] = jnp.where(keep, mixed_ref[h] / total, 0.0).astype(out_ref.dtype)

    @pl.when(start >= live)
    def _():
        out_ref[...] = jnp.zeros_like(out_ref)


def attention(qheads, first, half, here, pages, prefix, live, queries, keys, values, parts, carry):
    most = MAXP // 2 + 1
    width = qheads * HD
    if carry is None:
        carry = jnp.zeros((16, 128), jnp.bfloat16)
        aliases = {}
    else:
        aliases = {7 + len(parts): 0}

    def at(*_):
        return (first * 2 + half, 0)

    return pl.pallas_call(
        functools.partial(attend_kernel, qheads, (len(parts) + 1) // 2, half),
        grid_spec=pltpu.PrefetchScalarGridSpec(
            num_scalar_prefetch=4,
            grid=(1,),
            in_specs=[
                pl.BlockSpec((SPAN, width), at),
                pl.BlockSpec((SUF, HD), lambda *_: (first, 0)),
                pl.BlockSpec((SUF, HD), lambda *_: (first, 0)),
            ]
            + [IN_HBM] * len(parts)
            + [ANYWHERE],
            out_specs=pl.BlockSpec((SPAN, width), at),
            scratch_shapes=[
                pltpu.VMEM((MAXP, 2, PAGE, HD), jnp.bfloat16),
                pltpu.VMEM((most, qheads, SPAN, 2 * PAGE), jnp.float32),
                pltpu.VMEM((qheads, SPAN, HD), jnp.float32),
                pltpu.VMEM((qheads, SPAN, HD), jnp.float32),
                pltpu.VMEM((qheads, SPAN, HD), jnp.float32),
                pltpu.SemaphoreType.DMA,
            ],
        ),
        out_shape=jax.ShapeDtypeStruct(queries.shape, jnp.bfloat16),
        input_output_aliases=aliases,
        compiler_params=pltpu.CompilerParams(vmem_limit_bytes=VMEM),
        cost_estimate=pl.CostEstimate(
            flops=qheads * SPAN * (MAXP * PAGE + SUF) * HD * 4,
            bytes_accessed=SPAN * qheads * HD * 4 + MAXP * PAGE * HD * 4,
            transcendentals=qheads * SPAN * (MAXP * PAGE + SUF),
        ),
        name="attention",
    )(here, pages, prefix, live, queries, keys, values, *parts, carry)


def after(value, *others):
    return lax.optimization_barrier((value,) + others)[0]


def body(
    mixer_input,
    step_raw,
    decay_rate,
    skip_gain,
    state_proj,
    queries,
    suffix_kv,
    state_pool,
    page_pool,
    norm_gain,
    hit_owner,
    hit_slot,
    page_owner,
    page_slot,
    prefix_len,
    suffix_len,
):
    owners = lax.axis_size("owner")
    owner = lax.axis_index("owner").astype(jnp.int32)
    column = lax.axis_index("tensor")
    rows = mixer_input.shape[0]
    count = rows // SUF
    heads = decay_rate.shape[0]
    width = heads * MHDIM
    qheads = queries.shape[1] // HD
    per_group = SSM_HEAD_TOTAL // GROUPS
    group = column * heads // per_group
    kv_index = column * qheads // (QHEADS // KVHEADS)
    whole_group = heads == per_group
    chips = owners // 2
    per_chip = 2 * SLOTS_DEV
    states = owners * SLOTS_DEV
    here = owner.reshape(1)
    first = (owner * count).reshape(1)
    swap = [(o, o ^ 1) for o in range(owners)]

    def line(hop):
        up = [(o, o + 2) for o in range(0, owners - 2, 2) if o // 2 >= hop - 1]
        return up + [(o, o - 2) for o in range(3, owners, 2) if o // 2 <= chips - hop]

    def head_of(array, index, axis):
        return lax.dynamic_index_in_dim(array, index, axis, keepdims=False)

    pool = state_pool.reshape(SLOTS_DEV, width, STATE)
    near = lax.ppermute(pool, "owner", swap)
    own_pages = jnp.transpose(head_of(page_pool, kv_index, 3), (0, 2, 1, 3))
    near_pages = lax.ppermute(own_pages, "owner", swap)
    chip_pages = jnp.concatenate([own_pages, near_pages], axis=0)

    state_ids = (hit_owner[:, 0] * SLOTS_DEV + hit_slot).astype(jnp.int32)
    table, cap = route(state_ids, owner, chips, per_chip, 2 * count)

    def send(item):
        return lax.ppermute(item, "owner", line(1))

    spread_np = np.zeros((128, width), np.float32)
    for h in range(heads):
        for k in range(3):
            spread_np[k * heads + h, h * MHDIM : (h + 1) * MHDIM] = 1.0
    spread = jnp.asarray(spread_np, jnp.bfloat16)
    split_np = np.zeros((2 * SPAN, 2 * SPAN), np.float32)
    for i in range(SPAN):
        split_np[i, 2 * i] = 1.0
        split_np[SPAN + i, 2 * i + 1] = 1.0
    split = jnp.asarray(split_np, jnp.bfloat16)
    skip = jnp.repeat(skip_gain, MHDIM)[None, :]
    decay = jnp.broadcast_to(decay_rate[:, None], (heads, SPAN))
    step_row = step_raw.T
    page_ids = (page_owner[:, :, 0] * PAGES_DEV + page_slot).astype(jnp.int32).reshape(-1)
    made = {}

    def shape_inputs(tie):
        made["mixed"] = after(mixer_input, tie).reshape(2 * rows, width)
        maps = head_of(after(state_proj, tie), group, 2)
        made["b"], made["c"] = maps[:, 0], maps[:, 1]
        suffix = head_of(after(suffix_kv, tie), kv_index, 2)
        made["k"], made["v"] = suffix[:, 0], suffix[:, 1]
        return made["mixed"], made["b"], made["k"]

    def pre_part(r):
        def run(tie):
            made["pre"] = mamba_pre(
                heads,
                r,
                2,
                suffix_len,
                after(first, tie),
                made["mixed"],
                made["b"],
                made["c"],
                step_row,
                decay,
                skip,
                spread,
                split,
                made.get("pre"),
            )
            return (made["pre"][2],)

        return run

    def attention_part(r, half):
        def run(tie):
            place = jnp.concatenate([first + r, here])
            made["attn"] = attention(
                qheads,
                r,
                half,
                after(place, tie),
                page_ids,
                prefix_len,
                suffix_len,
                queries,
                made["k"],
                made["v"],
                made["parts"],
                made.get("attn"),
            )
            return (made["attn"],)

        return run

    beside = [shape_inputs] + [pre_part(r) for r in range(0, count, 2)]
    ours, theirs = [], []
    piece = chip_pages
    for hop in range(1, chips):
        done = (table, near) if hop == 1 else ()
        got = lax.ppermute(piece, "owner", line(hop))
        tie = piece
        if hop == chips - 1:
            sends = take(states, LAG, after(here, piece), table, jnp.zeros((1,), jnp.int32), pool, near, [])
            flying = [send(item) for item in sends]
            tie = sends[-1]
        if beside:
            done += beside.pop(0)(tie)
        if theirs:
            done += (theirs[-1],)
        piece = after(got, *done)
        ours.append(piece)
        theirs.append(lax.ppermute(piece, "owner", swap))
    made["parts"] = [chip_pages] + ours + theirs

    beside += [attention_part(r, half) for r in range(count) for half in range(2)]
    tie = piece
    came = []
    for step in range(LAG, FIXED_STEPS):
        done = beside.pop(0)(tie) if beside else ()
        came.append(after(flying.pop(0), *done))
        (item,) = take(states, 1, here, table, jnp.full((1,), step, jnp.int32), pool, near, came)
        flying.append(send(item))
        tie = item
    for got in flying:
        done = beside.pop(0)(tie) if beside else ()
        came.append(after(got, *done))
        tie = came[-1]
    while beside:
        beside.pop(0)(tie)

    def more(step, room):
        (item,) = take(states, 1, here, table, step.reshape(1), pool, near, came, room)
        return keep(step.reshape(1), send(item), room)

    room = blank(here, (cap - FIXED_STEPS,) + pool.shape[1:], pool.dtype)
    room = lax.fori_loop(FIXED_STEPS, table[2 * cap], more, room)

    picked = pick(states, cap, count, table, came, room)
    other = lax.ppermute(picked, "owner", swap)
    result = None
    for place in (after(here, picked), here):
        result = mamba_post(
            heads,
            whole_group,
            cap,
            states,
            place,
            table,
            suffix_len,
            pool,
            near,
            came,
            room,
            other,
            made["c"],
            *made["pre"],
            spread,
            norm_gain[None, :],
            result,
        )
    if whole_group:
        return (result[0], made["attn"])
    gated, partial_sum = result
    partial_sum = partial_sum[:, 0]
    spread_sum = jnp.where(jnp.arange(GROUPS)[:, None] == group, partial_sum[None, :], 0.0)
    totals = lax.psum(spread_sum, "tensor")
    square = lax.dynamic_index_in_dim(totals, group, 0, keepdims=False) / (per_group * MHDIM)
    my_suffix = lax.dynamic_slice_in_dim(suffix_len, first[0], count, 0)
    active = (jnp.arange(SUF)[None, :] < my_suffix[:, None]).reshape(-1)
    scaled = gated * lax.rsqrt(square + EPSILON)[:, None] * norm_gain[None, :]
    return (jnp.where(active[:, None], scaled, 0.0).astype(jnp.bfloat16), made["attn"])


def solution(mesh):
    return jax.shard_map(
        body,
        mesh=mesh,
        in_specs=(
            P("owner", None, "tensor"),
            P("owner", "tensor"),
            P("tensor"),
            P("tensor"),
            P("owner", None, None, None),
            P("owner", "tensor"),
            P("owner", None, None, None),
            P("owner", "tensor"),
            P("owner", None, None, None, None),
            P("tensor"),
            P(),
            P(),
            P(),
            P(),
            P(),
            P(),
        ),
        out_specs=(P("owner", "tensor"), P("owner", "tensor")),
        check_vma=False,
    )
```

```python
import functools
import math

import jax
import jax.numpy as jnp
import numpy as np
from jax import lax
from jax.experimental import pallas as pl
from jax.experimental.pallas import tpu as pltpu
from jax.sharding import PartitionSpec as P

SSM_HEAD_TOTAL = 128
MHDIM = 64
STATE = 256
GROUPS = 4
QHEADS = 32
KVHEADS = 4
HD = 128
PAGE = 128
SPAN = 128
SUF = 256
MAXP = 16
SLOTS_DEV = 4
PAGES_DEV = 16

EPSILON = 1e-05
NEG_FILL = -1e30
LAG = 2
HOP_STEPS = 2
FREE_STEPS = 6
VMEM = 48 * 1024 * 1024
SMALL_VMEM = 58 * 1024 * 1024

NT = (((1,), (1,)), ((), ()))
TN = (((0,), (0,)), ((), ()))


def mm(a, b, dims=(((1,), (0,)), ((), ()))):
    return lax.dot_general(a, b, dims, preferred_element_type=jnp.float32)


def route_kernel(chips, per_chip, reqs_per_chip, cap, ids_ref, here_ref, out_ref, need_ref, own_ref, tab_ref, code_ref):
    states = chips * per_chip
    chip_here = here_ref[0] // 2
    core_here = here_ref[0] % 2

    def clear(s, carry):
        need_ref[s] = 0
        return carry

    lax.fori_loop(0, states, clear, 0)

    def mark(r, carry):
        s = ids_ref[r]
        need_ref[s] = need_ref[s] | (1 << (r // reqs_per_chip))
        return carry

    lax.fori_loop(0, chips * reqs_per_chip, mark, 0)

    def put(base, length, row, from_ref):
        def one(t, carry):
            spot = jnp.clip(base + t, 0, 2 * chips * cap - 1)
            out_ref[row * cap + t] = jnp.where(t < length, from_ref[spot], states)
            return carry

        lax.fori_loop(0, cap, one, 0)

    steps = jnp.int32(0)
    for up in (True, False):
        before = jnp.int32(0)
        sent = jnp.int32(0)
        came = jnp.int32(0)
        for place in range(chips - 1):
            chip = place if up else chips - 1 - place
            base = ((0 if up else chips) + place) * cap

            def wanted(s, further=0, chip=chip, up=up):
                if up:
                    return (need_ref[s] >> (chip + 1 + further)) != 0
                return (need_ref[s] & ((1 << max(chip - further, 0)) - 1)) != 0

            count = jnp.int32(0)
            for far in (True, False):

                def own(i, n, far=far, chip=chip, wanted=wanted):
                    s = chip * per_chip + i
                    own_ref[n] = s
                    beyond = wanted(s, 1)
                    take = beyond if far else wanted(s) & jnp.logical_not(beyond)
                    return n + take.astype(jnp.int32)

                count = lax.fori_loop(0, per_chip, own, count)

            def fill(t, used, base=base, count=count):
                s = jnp.where(used < count, own_ref[used], states)
                tab_ref[base + t] = s
                code_ref[base + t] = s
                return jnp.minimum(used + 1, count)

            def forward(j, carry, base=base, wanted=wanted, fill=fill):
                t, used = carry
                s = tab_ref[base - cap + j]
                take = (s < states) & wanted(jnp.minimum(s, states - 1))
                later = jnp.where(take, jnp.maximum(t, j + LAG), t)
                used = lax.fori_loop(t, later, fill, used)
                tab_ref[base + later] = s
                code_ref[base + later] = states + 1 + j
                return later + take.astype(jnp.int32), used

            def idle(t, carry, base=base):
                tab_ref[base + t] = states
                code_ref[base + t] = states
                return carry

            lax.fori_loop(0, HOP_STEPS * place, idle, 0)
            t, used = jnp.int32(HOP_STEPS * place), jnp.int32(0)
            if place:
                t, used = lax.fori_loop(0, before, forward, (t, used))
            end = t + count - used
            lax.fori_loop(t, end, fill, used)
            before = end
            sent = jnp.where(chip_here == chip, end, sent)
            came = jnp.where(chip_here == (chip + 1 if up else chip - 1), end, came)
            steps = jnp.maximum(steps, end)
        here = chip_here if up else chips - 1 - chip_here
        side = 0 if up else chips

        @pl.when(core_here == (0 if up else 1))
        def _(here=here, side=side, sent=sent, came=came):
            put((side + here) * cap, sent, 0, code_ref)
            put((side + here - 1) * cap, came, 1, tab_ref)

        arrived = came if up else jnp.where(core_here == 0, arrived, came)

    out_ref[2 * cap] = steps
    mine = reqs_per_chip // 2
    asked = [here_ref[0] * mine + r for r in range(mine)] + [(here_ref[0] ^ 1) * mine + r for r in range(mine)]
    for k, request in enumerate(asked):
        state = ids_ref[request]
        out_ref[2 * cap + 3 + mine + k] = jnp.where(state // per_chip == chip_here, state, -1)

    def look(t, carry):
        came_now = out_ref[cap + t]
        for k, request in enumerate(asked):

            @pl.when(ids_ref[request] == came_now)
            def _(k=k):
                out_ref[2 * cap + 3 + mine + k] = states + 1 + t

        return carry

    lax.fori_loop(0, arrived, look, 0)
    found = jnp.int32(0)
    for here_now in (True, False):
        for r in range(mine):
            out_ref[2 * cap + 2 + found] = r
            found += ((out_ref[2 * cap + 3 + mine + r] >= 0) == here_now).astype(jnp.int32)
        if here_now:
            out_ref[2 * cap + 1] = found


def route(state_ids, owner, chips, per_chip, reqs_per_chip):
    cap = chips * per_chip + (LAG + HOP_STEPS) * chips + 8
    smem = pl.BlockSpec(memory_space=pltpu.SMEM)
    table = pl.pallas_call(
        functools.partial(route_kernel, chips, per_chip, reqs_per_chip, cap),
        out_shape=jax.ShapeDtypeStruct((2 * cap + 4 + 2 * reqs_per_chip,), jnp.int32),
        in_specs=[smem, smem],
        out_specs=smem,
        scratch_shapes=[
            pltpu.SMEM((chips * per_chip,), jnp.int32),
            pltpu.SMEM((2 * per_chip,), jnp.int32),
            pltpu.SMEM((2 * chips * cap,), jnp.int32),
            pltpu.SMEM((2 * chips * cap,), jnp.int32),
        ],
        name="route_states",
    )(state_ids, owner.reshape(1))
    return table, cap


ANYWHERE = pl.BlockSpec(memory_space=pl.ANY)
IN_HBM = pl.BlockSpec(memory_space=pltpu.HBM)
PIECES = 4


def piece_of(ref, k):
    rows = ref.shape[0] // PIECES
    return ref.at[pl.ds(k * rows, rows)]


def start_from(code, states, owner, pool_ref, near_ref, came_refs, late_ref, dst, sems):
    def start(ref):
        for k in range(PIECES):
            pltpu.make_async_copy(piece_of(ref, k), piece_of(dst, k), sems.at[k]).start()

    if pool_ref is not None:
        own = (code >= 0) & (code < states)
        slot = code % SLOTS_DEV

        @pl.when(own & (code // SLOTS_DEV == owner))
        def _():
            start(pool_ref.at[slot])

        @pl.when(own & (code // SLOTS_DEV != owner))
        def _():
            start(near_ref.at[slot])

    step = code - states - 1
    for k, ref in enumerate(came_refs):

        @pl.when(step == k)
        def _(ref=ref):
            start(ref)

    if late_ref is not None:

        @pl.when(step >= len(came_refs))
        def _():
            start(late_ref.at[step - len(came_refs)])


def pass_on(src, dst, sems):
    for k in range(PIECES):
        pltpu.make_async_copy(piece_of(dst, k), piece_of(src, k), sems.at[k]).wait()
        pltpu.make_async_copy(piece_of(src, k), piece_of(dst, k), sems.at[k]).start()


def finish(src, dst, sems):
    for k in range(PIECES):
        pltpu.make_async_copy(piece_of(src, k), piece_of(dst, k), sems.at[k]).wait()


def take_kernel(states, steps, late, here_ref, table_ref, step_ref, pool_ref, near_ref, *rest):
    sends, (item_ref, sem) = rest[-2 - steps : -2], rest[-2:]
    came_refs = rest[: -2 - steps]
    late_ref = None
    if late:
        came_refs, late_ref = came_refs[:-1], came_refs[-1]
    codes = [table_ref[step_ref[0] + t] for t in range(steps)]
    for t in range(steps):
        start_from(
            codes[t], states, here_ref[0], pool_ref, near_ref, came_refs, late_ref, item_ref.at[t], sem.at[t]
        )
    for act in (pass_on, finish):
        for t in range(steps):

            @pl.when(codes[t] != states)
            def _(t=t):
                act(item_ref.at[t], sends[t], sem.at[t])


def take(states, steps, here, table, step, pool, near, came, late=None):
    item = jax.ShapeDtypeStruct(pool.shape[1:], pool.dtype)
    came = list(came) + ([] if late is None else [late])
    return pl.pallas_call(
        functools.partial(take_kernel, states, steps, late is not None),
        grid_spec=pltpu.PrefetchScalarGridSpec(
            num_scalar_prefetch=3,
            grid=(1,),
            in_specs=[IN_HBM] * (2 + len(came)),
            out_specs=[IN_HBM] * steps,
            scratch_shapes=[
                pltpu.VMEM((steps,) + pool.shape[1:], pool.dtype),
                pltpu.SemaphoreType.DMA((steps, PIECES)),
            ],
        ),
        out_shape=[item] * steps,
        compiler_params=pltpu.CompilerParams(vmem_limit_bytes=SMALL_VMEM),
        name="take_states",
    )(here, table, step, pool, near, *came)


def keep_kernel(fixed, step_ref, got_ref, _late_in, late_ref, item_ref, sem):
    spot = late_ref.at[step_ref[0] - fixed]
    for k in range(PIECES):
        pltpu.make_async_copy(piece_of(got_ref, k), piece_of(item_ref, k), sem.at[k]).start()
    pass_on(item_ref, spot, sem)
    finish(item_ref, spot, sem)


def keep(fixed, step, got, late):
    return pl.pallas_call(
        functools.partial(keep_kernel, fixed),
        grid_spec=pltpu.PrefetchScalarGridSpec(
            num_scalar_prefetch=1,
            grid=(1,),
            in_specs=[IN_HBM, IN_HBM],
            out_specs=IN_HBM,
            scratch_shapes=[pltpu.VMEM(got.shape, got.dtype), pltpu.SemaphoreType.DMA((PIECES,))],
        ),
        out_shape=jax.ShapeDtypeStruct(late.shape, late.dtype),
        input_output_aliases={2: 0},
        compiler_params=pltpu.CompilerParams(vmem_limit_bytes=SMALL_VMEM),
        name="keep_state",
    )(step, got, late)


def blank_kernel(here_ref, out_ref):
    pass


def blank(here, shape, dtype):
    return pl.pallas_call(
        blank_kernel,
        in_specs=[pl.BlockSpec(memory_space=pltpu.SMEM)],
        out_specs=IN_HBM,
        out_shape=jax.ShapeDtypeStruct(shape, dtype),
        compiler_params=pltpu.CompilerParams(vmem_limit_bytes=SMALL_VMEM),
        name="room",
    )(here)


def pick_kernel(states, cap, count, table_ref, *rest):
    came_refs, late_ref = rest[:-4], rest[-4]
    out_ref, item_ref, sem = rest[-3:]
    codes = [table_ref[2 * cap + 3 + 2 * count + r] for r in range(count)]
    for r in range(count):

        @pl.when(codes[r] > states)
        def _(r=r):
            start_from(codes[r], states, -1, None, None, came_refs, late_ref, item_ref.at[r], sem.at[r])

    for act in (pass_on, finish):
        for r in range(count):

            @pl.when(codes[r] > states)
            def _(r=r):
                act(item_ref.at[r], out_ref.at[r], sem.at[r])


def pick(states, cap, count, table, came, late):
    shape = (count,) + late.shape[1:]
    return pl.pallas_call(
        functools.partial(pick_kernel, states, cap, count),
        grid_spec=pltpu.PrefetchScalarGridSpec(
            num_scalar_prefetch=1,
            grid=(1,),
            in_specs=[IN_HBM] * (len(came) + 1),
            out_specs=IN_HBM,
            scratch_shapes=[
                pltpu.VMEM(shape, late.dtype),
                pltpu.SemaphoreType.DMA((count, PIECES)),
            ],
        ),
        out_shape=jax.ShapeDtypeStruct(shape, late.dtype),
        compiler_params=pltpu.CompilerParams(vmem_limit_bytes=SMALL_VMEM),
        name="pick_states",
    )(table, *came, late)


def mamba_pre_kernel(
    heads,
    live_ref,
    first_ref,
    mix_ref,
    b_ref,
    c_ref,
    step_ref,
    decay_ref,
    skip_ref,
    spread_ref,
    split_ref,
    _pre_in,
    _z_in,
    _e_in,
    pre_ref,
    z_ref,
    e_ref,
    bs_ref,
    end_ref,
):
    block = pl.program_id(1)
    request = first_ref[0] + pl.program_id(0)
    copies = SPAN // heads
    row = lax.broadcasted_iota(jnp.int32, (SPAN, SPAN), 0)
    lane = lax.broadcasted_iota(jnp.int32, (SPAN, SPAN), 1)
    lower = row >= lane
    left = lane < MHDIM

    def three_way(value):
        high = value.astype(jnp.bfloat16)
        rest = value - high.astype(jnp.float32)
        middle = rest.astype(jnp.bfloat16)
        low = (rest - middle.astype(jnp.float32)).astype(jnp.bfloat16)
        high, middle, low = (v.astype(jnp.float32) for v in (high, middle, low))
        kept = jnp.where(
            lane < heads,
            high,
            jnp.where(lane < 2 * heads, middle, jnp.where(lane < 3 * heads, low, 0.0)),
        )
        return kept.astype(jnp.bfloat16)

    @pl.when((block == 0) | (live_ref[request] > SPAN))
    def _():
        raw = step_ref[...]
        rate_row = jnp.maximum(raw, 0.0) + jnp.log1p(jnp.exp(-jnp.abs(raw)))
        upper = jnp.where(row <= lane, 1.0, 0.0)
        cum_row = lax.dot_general(
            -rate_row * decay_ref[...],
            upper,
            (((1,), (0,)), ((), ())),
            precision=lax.Precision.HIGHEST,
            preferred_element_type=jnp.float32,
        )
        cum = jnp.concatenate([cum_row] * copies, axis=0).T
        rate_col = jnp.concatenate([rate_row] * copies, axis=0).T

        both = mm(split_ref[...], mix_ref[...])
        z_ref[...] = both[SPAN:].astype(jnp.bfloat16)
        x = both[:SPAN]
        x_half = x.astype(jnp.bfloat16)
        b = b_ref[...]
        c = c_ref[...]
        cross = mm(c, b, NT)

        def weights(h):
            fall = cum[:, h : h + 1] - cum_row[h : h + 1, :]
            fade = jnp.exp(jnp.where(lower, fall, NEG_FILL))
            return (cross * fade * rate_row[h : h + 1, :]).astype(jnp.bfloat16)

        for pair in range(heads // 2):
            cols = slice(pair * 2 * MHDIM, (pair + 1) * 2 * MHDIM)
            xp = x_half[:, cols]
            zero = jnp.zeros_like(xp)
            stacked = jnp.concatenate([jnp.where(left, xp, zero), jnp.where(left, zero, xp)], axis=0)
            w = jnp.concatenate([weights(2 * pair), weights(2 * pair + 1)], axis=1)
            pre_ref[:, cols] = mm(w, stacked) + skip_ref[:, cols] * x[:, cols]

        @pl.when(block == 0)
        def _():
            end = cum[SPAN - 1 : SPAN, :]
            tail = jnp.exp(end - cum) * rate_col
            scaled = (mm(three_way(tail), spread_ref[...]) * x).astype(jnp.bfloat16)
            bs_ref[...] = mm(scaled, b, TN).astype(jnp.bfloat16)
            end_ref[...] = jnp.broadcast_to(end, end_ref.shape)
            e_ref[...] = three_way(jnp.exp(cum))

        @pl.when(block == 1)
        def _():
            e_half = three_way(jnp.exp(cum))
            carried = mm(c, bs_ref[...], NT)
            pre_ref[...] += mm(e_half, spread_ref[...]) * carried
            e_ref[...] = three_way(jnp.exp(cum + end_ref[0:1, :]))


def mamba_pre(heads, first, count, live, here, mixed, b_rows, c_rows, step_row, decay, skip, spread, split, carry):
    width = heads * MHDIM
    rows = b_rows.shape[0]

    def at(r, k, *_):
        return ((first + r) * 2 + k, 0)

    def fixed(r, k, *_):
        return (0, 0)

    blocks = count * 2
    outs = [
        jax.ShapeDtypeStruct((rows, width), jnp.float32),
        jax.ShapeDtypeStruct((rows, width), jnp.bfloat16),
        jax.ShapeDtypeStruct((rows, 128), jnp.bfloat16),
    ]
    if carry is None:
        carry = tuple(jnp.zeros((16, 128), jnp.float32) for _ in outs)
        aliases = {}
    else:
        aliases = {10: 0, 11: 1, 12: 2}
    return pl.pallas_call(
        functools.partial(mamba_pre_kernel, heads),
        grid_spec=pltpu.PrefetchScalarGridSpec(
            num_scalar_prefetch=2,
            grid=(count, 2),
            in_specs=[
                pl.BlockSpec((2 * SPAN, width), at),
                pl.BlockSpec((SPAN, STATE), at),
                pl.BlockSpec((SPAN, STATE), at),
                pl.BlockSpec((heads, SPAN), lambda r, k, *_: (0, (first + r) * 2 + k)),
                pl.BlockSpec((heads, SPAN), fixed),
                pl.BlockSpec((1, width), fixed),
                pl.BlockSpec((128, width), fixed),
                pl.BlockSpec((2 * SPAN, 2 * SPAN), fixed),
                ANYWHERE,
                ANYWHERE,
                ANYWHERE,
            ],
            out_specs=[
                pl.BlockSpec((SPAN, width), at),
                pl.BlockSpec((SPAN, width), at),
                pl.BlockSpec((SPAN, 128), at),
            ],
            scratch_shapes=[
                pltpu.VMEM((width, STATE), jnp.bfloat16),
                pltpu.VMEM((8, 128), jnp.float32),
            ],
        ),
        out_shape=outs,
        input_output_aliases=aliases,
        compiler_params=pltpu.CompilerParams(vmem_limit_bytes=VMEM),
        cost_estimate=pl.CostEstimate(
            flops=blocks * heads * 40 * SPAN * SPAN * MHDIM,
            bytes_accessed=blocks * SPAN * width * 10,
            transcendentals=blocks * heads * SPAN * SPAN,
        ),
        name="mamba_pre",
    )(live, here + first, mixed, b_rows, c_rows, step_row, decay, skip, spread, split, *carry)


def mamba_post_kernel(
    heads,
    whole_group,
    count,
    cap,
    states,
    fixed,
    late,
    here_ref,
    table_ref,
    live_ref,
    *rest,
):
    outs = 1 if whole_group else 2
    pool_ref, near_ref, *came_refs, late_ref, other_ref = rest[: fixed + 4]
    c_ref, pre_ref, z_ref, e_ref, spread_ref, gain_ref, *rest = rest[fixed + 4 :]
    out_refs = rest[outs : 2 * outs]
    state_ref, sem = rest[-2:]
    i = pl.program_id(0)
    width = heads * MHDIM
    owner = here_ref[0]
    here_now = table_ref[2 * cap + 1]
    active = jnp.maximum(count - here_now, 1) if late else here_now

    def fetch(i):
        r = post_request(cap, count, late, i, table_ref)
        code = table_ref[2 * cap + 3 + count + r]
        slot = i % 2
        start_from(
            code, states, owner, pool_ref, near_ref, came_refs, late_ref, state_ref.at[slot], sem.at[slot]
        )
        if late:

            @pl.when(code < 0)
            def _():
                for k in range(PIECES):
                    pltpu.make_async_copy(
                        piece_of(other_ref.at[r], k), piece_of(state_ref.at[slot], k), sem.at[slot, k]
                    ).start()

    @pl.when((i == 0) & (i < active))
    def _():
        fetch(i)

    @pl.when(i + 1 < active)
    def _():
        fetch(i + 1)

    @pl.when(i < active)
    def _():
        r = post_request(cap, count, late, i, table_ref)
        finish(pool_ref.at[0], state_ref.at[i % 2], sem.at[i % 2])
        carried = mm(c_ref[...], state_ref[i % 2], NT)
        summed = pre_ref[...] + mm(e_ref[...], spread_ref[...]) * carried
        z = z_ref[...].astype(jnp.float32)
        gated = summed * (z / (1.0 + jnp.exp(-z)))
        square = jnp.sum(gated * gated, axis=1, keepdims=True)
        if whole_group:
            norm = lax.rsqrt(square / width + EPSILON)
            live = lax.broadcasted_iota(jnp.int32, (SUF, 1), 0) < live_ref[owner * count + r]
            out_refs[0][...] = jnp.where(live, gated * norm * gain_ref[...], 0.0).astype(jnp.bfloat16)
        else:
            out_refs[0][...] = gated
            out_refs[1][...] = jnp.broadcast_to(square, (SUF, 128))


def post_request(cap, count, late, i, table_ref):
    here_now = table_ref[2 * cap + 1]
    if late:
        spot = here_now + jnp.minimum(i, jnp.maximum(count - here_now - 1, 0))
    else:
        spot = jnp.minimum(i, jnp.maximum(here_now - 1, 0))
    return table_ref[2 * cap + 2 + jnp.minimum(spot, count - 1)]


def mamba_post(
    heads, whole_group, cap, states, here, table, live, pool, near, came, late_room, other, c_rows, pre, z, e3, spread, gain, carry
):
    width = heads * MHDIM
    rows = c_rows.shape[0]
    count = rows // SUF
    late = carry is not None
    held = len(came)

    def at(i, here_ref, table_ref, *_):
        return (post_request(cap, count, late, i, table_ref), 0)

    def fixed(i, *_):
        return (0, 0)

    out_shape = [jax.ShapeDtypeStruct((rows, width), jnp.bfloat16 if whole_group else jnp.float32)]
    out_specs = [pl.BlockSpec((SUF, width), at)]
    if not whole_group:
        out_shape.append(jax.ShapeDtypeStruct((rows, 128), jnp.float32))
        out_specs.append(pl.BlockSpec((SUF, 128), at))
    aliases = {}
    if late:
        aliases = {3 + held + 10 + k: k for k in range(len(out_shape))}
    else:
        carry = [jnp.zeros((16, 128), jnp.float32)] * len(out_shape)
        other = late_room
    return pl.pallas_call(
        functools.partial(mamba_post_kernel, heads, whole_group, count, cap, states, held, late),
        grid_spec=pltpu.PrefetchScalarGridSpec(
            num_scalar_prefetch=3,
            grid=(count,),
            in_specs=[IN_HBM] * (held + 4)
            + [
                pl.BlockSpec((SUF, STATE), at),
                pl.BlockSpec((SUF, width), at),
                pl.BlockSpec((SUF, width), at),
                pl.BlockSpec((SUF, 128), at),
                pl.BlockSpec((128, width), fixed),
                pl.BlockSpec((1, width), fixed),
            ]
            + [ANYWHERE] * len(out_shape),
            out_specs=out_specs,
            scratch_shapes=[
                pltpu.VMEM((2, width, STATE), jnp.bfloat16),
                pltpu.SemaphoreType.DMA((2, PIECES)),
            ],
        ),
        out_shape=out_shape,
        input_output_aliases=aliases,
        compiler_params=pltpu.CompilerParams(vmem_limit_bytes=VMEM),
        cost_estimate=pl.CostEstimate(
            flops=2 * rows * width * STATE,
            bytes_accessed=rows * width * 6,
            transcendentals=rows * width,
        ),
        name="mamba_post",
    )(here, table, live, pool, near, *came, late_room, other, c_rows, pre, z, e3, spread, gain, *carry)


def attend_kernel(
    qheads,
    chips,
    half,
    first_ref,
    pages_ref,
    prefix_ref,
    live_ref,
    q_ref,
    ks_ref,
    vs_ref,
    *rest,
):
    parts = rest[: 2 * chips - 1]
    out_ref, kv_ref, q_all, s_ref, p_ref, top_ref, total_ref, mixed_ref, sem = rest[2 * chips :]
    request = first_ref[0]
    owner = first_ref[1]
    scale = math.log2(math.e) / math.sqrt(HD)
    pairs = prefix_ref[request] // (2 * PAGE)
    start = half * SPAN
    live = live_ref[request]

    def rows_of(h):
        return slice(h * SPAN, (h + 1) * SPAN)

    def columns(h):
        return slice(h * HD, (h + 1) * HD)

    def fold(s):
        return jnp.maximum(s[:, :HD], s[:, HD:])

    @pl.when(start < live)
    def _():
        def begin(p, carry):
            page = pages_ref[request * MAXP + p]
            giver = page // PAGES_DEV
            core = owner % 2
            away = giver // 2 - owner // 2
            ahead = jnp.where(core == 0, -away, away)
            which = jnp.where(ahead >= 0, ahead, chips - 1 - ahead)
            carrier = jnp.where(ahead >= 0, core, 1 - core)
            spot = ((giver % 2) ^ carrier) * PAGES_DEV + page % PAGES_DEV
            for k, part in enumerate(parts):

                @pl.when(which == k)
                def _(part=part):
                    pltpu.make_async_copy(part.at[spot], kv_ref.at[p + 2], sem).start()

            return carry

        def end(p, carry):
            pltpu.make_async_copy(parts[0].at[0], kv_ref.at[p + 2], sem).wait()
            return carry

        lax.fori_loop(0, 2 * pairs, begin, 0)
        for page in range(2):
            at = slice(page * PAGE, (page + 1) * PAGE)
            kv_ref[page, 0] = ks_ref[at, :]
            kv_ref[page, 1] = vs_ref[at, :]
        for h in range(qheads):
            q_all[rows_of(h), :] = q_ref[:, columns(h)]
        row = lax.broadcasted_iota(jnp.int32, (SPAN, SUF), 0) + start
        lane = lax.broadcasted_iota(jnp.int32, (SPAN, SUF), 1)
        causal = row >= lane

        def block(i, kv):
            return kv_ref[pl.ds(i * 2, 2), kv].reshape(2 * PAGE, HD)

        s = mm(q_all[...], block(0, 0), NT)
        for h in range(qheads):
            own = jnp.where(causal, s[rows_of(h)], NEG_FILL)
            s_ref[0, rows_of(h)] = own
            top_ref[rows_of(h)] = fold(own)
        lax.fori_loop(0, 2 * pairs, end, 0)

        def scores(i, carry):
            s = mm(q_all[...], block(i, 0), NT)
            s_ref[i] = s
            top_ref[...] = jnp.maximum(top_ref[...], fold(s))
            return carry

        lax.fori_loop(1, pairs + 1, scores, 0)
        for h in range(qheads):
            top = jnp.max(top_ref[rows_of(h)], axis=1, keepdims=True)
            top_ref[rows_of(h)] = jnp.broadcast_to(top, (SPAN, HD))
        total_ref[...] = jnp.zeros_like(total_ref)
        mixed_ref[...] = jnp.zeros_like(mixed_ref)

        def weigh(i):
            for h in range(qheads):
                at = rows_of(h)
                top = top_ref[at]
                probs = jnp.exp2((s_ref[i, at] - jnp.concatenate([top, top], axis=1)) * scale)
                total_ref[at] += probs[:, :HD] + probs[:, HD:]
                p_ref[i % 2, at] = probs.astype(jnp.bfloat16)

        def mix(i):
            mixed_ref[...] += mm(p_ref[i % 2], block(i, 1))

        weigh(0)

        def values(i, carry):
            mix(i - 1)
            weigh(i)
            return carry

        lax.fori_loop(1, pairs + 1, values, 0)
        mix(pairs)
        keep_row = lax.broadcasted_iota(jnp.int32, (SPAN, 1), 0) + start < live
        for h in range(qheads):
            total = jnp.sum(total_ref[rows_of(h)], axis=1, keepdims=True)
            out_ref[:, columns(h)] = jnp.where(keep_row, mixed_ref[rows_of(h)] / total, 0.0).astype(out_ref.dtype)

    @pl.when(start >= live)
    def _():
        out_ref[...] = jnp.zeros_like(out_ref)


def attention(qheads, first, half, here, pages, prefix, live, queries, keys, values, parts, carry):
    most = MAXP // 2 + 1
    width = qheads * HD
    if carry is None:
        carry = jnp.zeros((16, 128), jnp.bfloat16)
        aliases = {}
    else:
        aliases = {7 + len(parts): 0}

    def at(*_):
        return (first * 2 + half, 0)

    return pl.pallas_call(
        functools.partial(attend_kernel, qheads, (len(parts) + 1) // 2, half),
        grid_spec=pltpu.PrefetchScalarGridSpec(
            num_scalar_prefetch=4,
            grid=(1,),
            in_specs=[
                pl.BlockSpec((SPAN, width), at),
                pl.BlockSpec((SUF, HD), lambda *_: (first, 0)),
                pl.BlockSpec((SUF, HD), lambda *_: (first, 0)),
            ]
            + [IN_HBM] * len(parts)
            + [ANYWHERE],
            out_specs=pl.BlockSpec((SPAN, width), at),
            scratch_shapes=[
                pltpu.VMEM((MAXP + 2, 2, PAGE, HD), jnp.bfloat16),
                pltpu.VMEM((qheads * SPAN, HD), jnp.bfloat16),
                pltpu.VMEM((most, qheads * SPAN, 2 * PAGE), jnp.float32),
                pltpu.VMEM((2, qheads * SPAN, 2 * PAGE), jnp.bfloat16),
                pltpu.VMEM((qheads * SPAN, HD), jnp.float32),
                pltpu.VMEM((qheads * SPAN, HD), jnp.float32),
                pltpu.VMEM((qheads * SPAN, HD), jnp.float32),
                pltpu.SemaphoreType.DMA,
            ],
        ),
        out_shape=jax.ShapeDtypeStruct(queries.shape, jnp.bfloat16),
        input_output_aliases=aliases,
        compiler_params=pltpu.CompilerParams(vmem_limit_bytes=VMEM),
        cost_estimate=pl.CostEstimate(
            flops=qheads * SPAN * (MAXP * PAGE + SUF) * HD * 4,
            bytes_accessed=SPAN * qheads * HD * 4 + MAXP * PAGE * HD * 4,
            transcendentals=qheads * SPAN * (MAXP * PAGE + SUF),
        ),
        name="attention",
    )(here, pages, prefix, live, queries, keys, values, *parts, carry)


def after(value, *others):
    return lax.optimization_barrier((value,) + others)[0]


def body(
    mixer_input,
    step_raw,
    decay_rate,
    skip_gain,
    state_proj,
    queries,
    suffix_kv,
    state_pool,
    page_pool,
    norm_gain,
    hit_owner,
    hit_slot,
    page_owner,
    page_slot,
    prefix_len,
    suffix_len,
):
    owners = lax.axis_size("owner")
    owner = lax.axis_index("owner").astype(jnp.int32)
    column = lax.axis_index("tensor")
    rows = mixer_input.shape[0]
    count = rows // SUF
    heads = decay_rate.shape[0]
    width = heads * MHDIM
    qheads = queries.shape[1] // HD
    per_group = SSM_HEAD_TOTAL // GROUPS
    group = column * heads // per_group
    kv_index = column * qheads // (QHEADS // KVHEADS)
    whole_group = heads == per_group
    chips = owners // 2
    per_chip = 2 * SLOTS_DEV
    states = owners * SLOTS_DEV
    here = owner.reshape(1)
    first = (owner * count).reshape(1)
    swap = [(o, o ^ 1) for o in range(owners)]

    def line(hop):
        up = [(o, o + 2) for o in range(0, owners - 2, 2) if o // 2 >= hop - 1]
        return up + [(o, o - 2) for o in range(3, owners, 2) if o // 2 <= chips - hop]

    def send(item, step):
        up = [(o, o + 2) for o in range(0, owners - 2, 2) if step >= HOP_STEPS * (o // 2)]
        down = [(o, o - 2) for o in range(3, owners, 2) if step >= HOP_STEPS * (chips - 1 - o // 2)]
        return lax.ppermute(item, "owner", up + down)

    def head_of(array, index, axis):
        return lax.dynamic_index_in_dim(array, index, axis, keepdims=False)

    pool = state_pool.reshape(SLOTS_DEV, width, STATE)
    near = lax.ppermute(pool, "owner", swap)
    own_pages = jnp.transpose(head_of(page_pool, kv_index, 3), (0, 2, 1, 3))
    near_pages = lax.ppermute(own_pages, "owner", swap)
    chip_pages = jnp.concatenate([own_pages, near_pages], axis=0)

    state_ids = (hit_owner[:, 0] * SLOTS_DEV + hit_slot).astype(jnp.int32)
    table, cap = route(state_ids, owner, chips, per_chip, 2 * count)

    spread_np = np.zeros((128, width), np.float32)
    for h in range(heads):
        for k in range(3):
            spread_np[k * heads + h, h * MHDIM : (h + 1) * MHDIM] = 1.0
    spread = jnp.asarray(spread_np, jnp.bfloat16)
    split_np = np.zeros((2 * SPAN, 2 * SPAN), np.float32)
    for i in range(SPAN):
        split_np[i, 2 * i] = 1.0
        split_np[SPAN + i, 2 * i + 1] = 1.0
    split = jnp.asarray(split_np, jnp.bfloat16)
    skip = jnp.repeat(skip_gain, MHDIM)[None, :]
    decay = jnp.broadcast_to(decay_rate[:, None], (heads, SPAN))
    step_row = step_raw.T
    page_ids = (page_owner[:, :, 0] * PAGES_DEV + page_slot).astype(jnp.int32).reshape(-1)
    made = {}

    def shape_inputs(tie):
        made["mixed"] = after(mixer_input, tie).reshape(2 * rows, width)
        maps = head_of(after(state_proj, tie), group, 2)
        made["b"], made["c"] = maps[:, 0], maps[:, 1]
        suffix = head_of(after(suffix_kv, tie), kv_index, 2)
        made["k"], made["v"] = suffix[:, 0], suffix[:, 1]
        return made["mixed"], made["b"], made["k"]

    def pre_part(r):
        def run(tie):
            made["pre"] = mamba_pre(
                heads,
                r,
                2,
                suffix_len,
                after(first, tie),
                made["mixed"],
                made["b"],
                made["c"],
                step_row,
                decay,
                skip,
                spread,
                split,
                made.get("pre"),
            )
            return (made["pre"][2],)

        return run

    def attention_part(r, half):
        def run(tie):
            place = jnp.concatenate([first + r, here])
            made["attn"] = attention(
                qheads,
                r,
                half,
                after(place, tie),
                page_ids,
                prefix_len,
                suffix_len,
                queries,
                made["k"],
                made["v"],
                made["parts"],
                made.get("attn"),
            )
            return (made["attn"],)

        return run

    def step_at(step):
        return jnp.full((1,), step, jnp.int32)

    beside = [shape_inputs] + [pre_part(r) for r in range(0, count, 2)]
    ours, theirs, came = [], [], []
    piece = chip_pages
    for hop in range(1, chips):
        got = lax.ppermute(piece, "owner", line(hop))
        tie, done = piece, ()
        if hop == 1:
            done = (table, near)
        else:
            step = HOP_STEPS * (hop - 2)
            items = take(states, HOP_STEPS, after(here, piece), table, step_at(step), pool, near, came)
            came += [send(item, step + k) for k, item in enumerate(items)]
            done = tuple(came[-HOP_STEPS:]) + (theirs[-1],)
            tie = items[-1]
        if beside:
            done += beside.pop(0)(tie)
        piece = after(got, *done)
        ours.append(piece)
        theirs.append(lax.ppermute(piece, "owner", swap))
    made["parts"] = [chip_pages] + ours + theirs

    beside += [attention_part(r, half) for r in range(count) for half in range(2)]
    started = HOP_STEPS * (chips - 2)
    fixed = started + FREE_STEPS
    items = take(states, LAG, after(here, piece), table, step_at(started), pool, near, came)
    flying = [send(item, started + k) for k, item in enumerate(items)]
    tie = items[-1]
    spare = len(beside) - FREE_STEPS

    def compute(tie, chunks):
        done = ()
        for _ in range(min(chunks, len(beside))):
            done = beside.pop(0)(tie)
            tie = done[0]
        return done

    for step in range(started + LAG, fixed):
        done = compute(tie, 1 + (step == started + LAG and spare > 0))
        came.append(after(flying.pop(0), *done))
        (item,) = take(states, 1, here, table, step_at(step), pool, near, came)
        flying.append(send(item, step))
        tie = item
    for k, got in enumerate(flying):
        done = compute(tie, 1 if k == 0 else len(beside))
        came.append(after(got, *done))
        tie = came[-1]

    def more(step, room):
        (item,) = take(states, 1, here, table, step.reshape(1), pool, near, came, room)
        return keep(fixed, step.reshape(1), send(item, fixed), room)

    room = blank(here, (cap - fixed,) + pool.shape[1:], pool.dtype)
    room = lax.fori_loop(fixed, table[2 * cap], more, room)

    picked = pick(states, cap, count, table, came, room)
    other = lax.ppermute(picked, "owner", swap)
    result = None
    for place in (after(here, picked), here):
        result = mamba_post(
            heads,
            whole_group,
            cap,
            states,
            place,
            table,
            suffix_len,
            pool,
            near,
            came,
            room,
            other,
            made["c"],
            *made["pre"],
            spread,
            norm_gain[None, :],
            result,
        )
    if whole_group:
        return (result[0], made["attn"])
    gated, partial_sum = result
    partial_sum = partial_sum[:, 0]
    spread_sum = jnp.where(jnp.arange(GROUPS)[:, None] == group, partial_sum[None, :], 0.0)
    totals = lax.psum(spread_sum, "tensor")
    square = lax.dynamic_index_in_dim(totals, group, 0, keepdims=False) / (per_group * MHDIM)
    my_suffix = lax.dynamic_slice_in_dim(suffix_len, first[0], count, 0)
    active = (jnp.arange(SUF)[None, :] < my_suffix[:, None]).reshape(-1)
    scaled = gated * lax.rsqrt(square + EPSILON)[:, None] * norm_gain[None, :]
    return (jnp.where(active[:, None], scaled, 0.0).astype(jnp.bfloat16), made["attn"])


def solution(mesh):
    return jax.shard_map(
        body,
        mesh=mesh,
        in_specs=(
            P("owner", None, "tensor"),
            P("owner", "tensor"),
            P("tensor"),
            P("tensor"),
            P("owner", None, None, None),
            P("owner", "tensor"),
            P("owner", None, None, None),
            P("owner", "tensor"),
            P("owner", None, None, None, None),
            P("tensor"),
            P(),
            P(),
            P(),
            P(),
            P(),
            P(),
        ),
        out_specs=(P("owner", "tensor"), P("owner", "tensor")),
        check_vma=False,
    )
```

```python
import functools
import math

import jax
import jax.numpy as jnp
import numpy as np
from jax import lax
from jax.experimental import pallas as pl
from jax.experimental.pallas import tpu as pltpu
from jax.sharding import PartitionSpec as P

SSM_HEAD_TOTAL = 128
MHDIM = 64
STATE = 256
GROUPS = 4
QHEADS = 32
KVHEADS = 4
HD = 128
PAGE = 128
SPAN = 128
SUF = 256
MAXP = 16
SLOTS_DEV = 4
PAGES_DEV = 16

EPSILON = 1e-05
NEG_FILL = -1e30
LAG = 2
HOP_STEPS = 2
FREE_STEPS = 7
VMEM = 48 * 1024 * 1024
SMALL_VMEM = 58 * 1024 * 1024

NT = (((1,), (1,)), ((), ()))
TN = (((0,), (0,)), ((), ()))


def mm(a, b, dims=(((1,), (0,)), ((), ()))):
    return lax.dot_general(a, b, dims, preferred_element_type=jnp.float32)


def route_kernel(chips, per_chip, reqs_per_chip, cap, ids_ref, here_ref, out_ref, need_ref, own_ref, tab_ref, code_ref):
    states = chips * per_chip
    chip_here = here_ref[0] // 2
    core_here = here_ref[0] % 2

    def clear(s, carry):
        need_ref[s] = 0
        return carry

    lax.fori_loop(0, states, clear, 0)

    def mark(r, carry):
        s = ids_ref[r]
        need_ref[s] = need_ref[s] | (1 << (r // reqs_per_chip))
        return carry

    lax.fori_loop(0, chips * reqs_per_chip, mark, 0)

    def put(base, length, row, from_ref):
        def one(t, carry):
            spot = jnp.clip(base + t, 0, 2 * chips * cap - 1)
            out_ref[row * cap + t] = jnp.where(t < length, from_ref[spot], states)
            return carry

        lax.fori_loop(0, cap, one, 0)

    steps = jnp.int32(0)
    for up in (True, False):
        before = jnp.int32(0)
        sent = jnp.int32(0)
        came = jnp.int32(0)
        for place in range(chips - 1):
            chip = place if up else chips - 1 - place
            base = ((0 if up else chips) + place) * cap

            def wanted(s, further=0, chip=chip, up=up):
                if up:
                    return (need_ref[s] >> (chip + 1 + further)) != 0
                return (need_ref[s] & ((1 << max(chip - further, 0)) - 1)) != 0

            count = jnp.int32(0)
            for far in (True, False):

                def own(i, n, far=far, chip=chip, wanted=wanted):
                    s = chip * per_chip + i
                    own_ref[n] = s
                    beyond = wanted(s, 1)
                    take = beyond if far else wanted(s) & jnp.logical_not(beyond)
                    return n + take.astype(jnp.int32)

                count = lax.fori_loop(0, per_chip, own, count)

            def fill(t, used, base=base, count=count):
                s = jnp.where(used < count, own_ref[used], states)
                tab_ref[base + t] = s
                code_ref[base + t] = s
                return jnp.minimum(used + 1, count)

            def forward(j, carry, base=base, wanted=wanted, fill=fill):
                t, used = carry
                s = tab_ref[base - cap + j]
                take = (s < states) & wanted(jnp.minimum(s, states - 1))
                later = jnp.where(take, jnp.maximum(t, j + LAG), t)
                used = lax.fori_loop(t, later, fill, used)
                tab_ref[base + later] = s
                code_ref[base + later] = states + 1 + j
                return later + take.astype(jnp.int32), used

            def idle(t, carry, base=base):
                tab_ref[base + t] = states
                code_ref[base + t] = states
                return carry

            lax.fori_loop(0, HOP_STEPS * place, idle, 0)
            t, used = jnp.int32(HOP_STEPS * place), jnp.int32(0)
            if place:
                t, used = lax.fori_loop(0, before, forward, (t, used))
            end = t + count - used
            lax.fori_loop(t, end, fill, used)
            before = end
            sent = jnp.where(chip_here == chip, end, sent)
            came = jnp.where(chip_here == (chip + 1 if up else chip - 1), end, came)
            steps = jnp.maximum(steps, end)
        here = chip_here if up else chips - 1 - chip_here
        side = 0 if up else chips

        @pl.when(core_here == (0 if up else 1))
        def _(here=here, side=side, sent=sent, came=came):
            put((side + here) * cap, sent, 0, code_ref)
            put((side + here - 1) * cap, came, 1, tab_ref)

        arrived = came if up else jnp.where(core_here == 0, arrived, came)

    out_ref[2 * cap] = steps
    mine = reqs_per_chip // 2
    asked = [here_ref[0] * mine + r for r in range(mine)] + [(here_ref[0] ^ 1) * mine + r for r in range(mine)]
    for k, request in enumerate(asked):
        state = ids_ref[request]
        out_ref[2 * cap + 3 + mine + k] = jnp.where(state // per_chip == chip_here, state, -1)

    def look(t, carry):
        came_now = out_ref[cap + t]
        for k, request in enumerate(asked):

            @pl.when(ids_ref[request] == came_now)
            def _(k=k):
                out_ref[2 * cap + 3 + mine + k] = states + 1 + t

        return carry

    lax.fori_loop(0, arrived, look, 0)
    found = jnp.int32(0)
    for here_now in (True, False):
        for r in range(mine):
            out_ref[2 * cap + 2 + found] = r
            found += ((out_ref[2 * cap + 3 + mine + r] >= 0) == here_now).astype(jnp.int32)
        if here_now:
            out_ref[2 * cap + 1] = found


def route(state_ids, owner, chips, per_chip, reqs_per_chip):
    cap = chips * per_chip + (LAG + HOP_STEPS) * chips + 8
    smem = pl.BlockSpec(memory_space=pltpu.SMEM)
    table = pl.pallas_call(
        functools.partial(route_kernel, chips, per_chip, reqs_per_chip, cap),
        out_shape=jax.ShapeDtypeStruct((2 * cap + 4 + 2 * reqs_per_chip,), jnp.int32),
        in_specs=[smem, smem],
        out_specs=smem,
        scratch_shapes=[
            pltpu.SMEM((chips * per_chip,), jnp.int32),
            pltpu.SMEM((2 * per_chip,), jnp.int32),
            pltpu.SMEM((2 * chips * cap,), jnp.int32),
            pltpu.SMEM((2 * chips * cap,), jnp.int32),
        ],
        name="route_states",
    )(state_ids, owner.reshape(1))
    return table, cap


ANYWHERE = pl.BlockSpec(memory_space=pl.ANY)
IN_HBM = pl.BlockSpec(memory_space=pltpu.HBM)
PIECES = 4


def piece_of(ref, k):
    rows = ref.shape[0] // PIECES
    return ref.at[pl.ds(k * rows, rows)]


def start_from(code, states, owner, pool_ref, near_ref, came_refs, late_ref, dst, sems):
    def start(ref):
        for k in range(PIECES):
            pltpu.make_async_copy(piece_of(ref, k), piece_of(dst, k), sems.at[k]).start()

    if pool_ref is not None:
        own = (code >= 0) & (code < states)
        slot = code % SLOTS_DEV

        @pl.when(own & (code // SLOTS_DEV == owner))
        def _():
            start(pool_ref.at[slot])

        @pl.when(own & (code // SLOTS_DEV != owner))
        def _():
            start(near_ref.at[slot])

    step = code - states - 1
    for k, ref in enumerate(came_refs):

        @pl.when(step == k)
        def _(ref=ref):
            start(ref)

    if late_ref is not None:

        @pl.when(step >= len(came_refs))
        def _():
            start(late_ref.at[step - len(came_refs)])


def pass_on(src, dst, sems):
    for k in range(PIECES):
        pltpu.make_async_copy(piece_of(dst, k), piece_of(src, k), sems.at[k]).wait()
        pltpu.make_async_copy(piece_of(src, k), piece_of(dst, k), sems.at[k]).start()


def finish(src, dst, sems):
    for k in range(PIECES):
        pltpu.make_async_copy(piece_of(src, k), piece_of(dst, k), sems.at[k]).wait()


def take_kernel(states, steps, late, here_ref, table_ref, step_ref, pool_ref, near_ref, *rest):
    sends, (item_ref, sem) = rest[-2 - steps : -2], rest[-2:]
    came_refs = rest[: -2 - steps]
    late_ref = None
    if late:
        came_refs, late_ref = came_refs[:-1], came_refs[-1]
    codes = [table_ref[step_ref[0] + t] for t in range(steps)]
    for t in range(steps):
        start_from(
            codes[t], states, here_ref[0], pool_ref, near_ref, came_refs, late_ref, item_ref.at[t], sem.at[t]
        )
    for act in (pass_on, finish):
        for t in range(steps):

            @pl.when(codes[t] != states)
            def _(t=t):
                act(item_ref.at[t], sends[t], sem.at[t])


def take(states, steps, here, table, step, pool, near, came, late=None):
    item = jax.ShapeDtypeStruct(pool.shape[1:], pool.dtype)
    came = list(came) + ([] if late is None else [late])
    return pl.pallas_call(
        functools.partial(take_kernel, states, steps, late is not None),
        grid_spec=pltpu.PrefetchScalarGridSpec(
            num_scalar_prefetch=3,
            grid=(1,),
            in_specs=[IN_HBM] * (2 + len(came)),
            out_specs=[IN_HBM] * steps,
            scratch_shapes=[
                pltpu.VMEM((steps,) + pool.shape[1:], pool.dtype),
                pltpu.SemaphoreType.DMA((steps, PIECES)),
            ],
        ),
        out_shape=[item] * steps,
        compiler_params=pltpu.CompilerParams(vmem_limit_bytes=SMALL_VMEM),
        name="take_states",
    )(here, table, step, pool, near, *came)


def keep_kernel(fixed, step_ref, got_ref, _late_in, late_ref, item_ref, sem):
    spot = late_ref.at[step_ref[0] - fixed]
    for k in range(PIECES):
        pltpu.make_async_copy(piece_of(got_ref, k), piece_of(item_ref, k), sem.at[k]).start()
    pass_on(item_ref, spot, sem)
    finish(item_ref, spot, sem)


def keep(fixed, step, got, late):
    return pl.pallas_call(
        functools.partial(keep_kernel, fixed),
        grid_spec=pltpu.PrefetchScalarGridSpec(
            num_scalar_prefetch=1,
            grid=(1,),
            in_specs=[IN_HBM, IN_HBM],
            out_specs=IN_HBM,
            scratch_shapes=[pltpu.VMEM(got.shape, got.dtype), pltpu.SemaphoreType.DMA((PIECES,))],
        ),
        out_shape=jax.ShapeDtypeStruct(late.shape, late.dtype),
        input_output_aliases={2: 0},
        compiler_params=pltpu.CompilerParams(vmem_limit_bytes=SMALL_VMEM),
        name="keep_state",
    )(step, got, late)


def blank_kernel(here_ref, out_ref):
    pass


def blank(here, shape, dtype):
    return pl.pallas_call(
        blank_kernel,
        in_specs=[pl.BlockSpec(memory_space=pltpu.SMEM)],
        out_specs=IN_HBM,
        out_shape=jax.ShapeDtypeStruct(shape, dtype),
        compiler_params=pltpu.CompilerParams(vmem_limit_bytes=SMALL_VMEM),
        name="room",
    )(here)


def pick_kernel(states, cap, count, table_ref, *rest):
    came_refs, late_ref = rest[:-4], rest[-4]
    out_ref, item_ref, sem = rest[-3:]
    codes = [table_ref[2 * cap + 3 + 2 * count + r] for r in range(count)]
    for r in range(count):

        @pl.when(codes[r] > states)
        def _(r=r):
            start_from(codes[r], states, -1, None, None, came_refs, late_ref, item_ref.at[r], sem.at[r])

    for act in (pass_on, finish):
        for r in range(count):

            @pl.when(codes[r] > states)
            def _(r=r):
                act(item_ref.at[r], out_ref.at[r], sem.at[r])


def pick(states, cap, count, table, came, late):
    shape = (count,) + late.shape[1:]
    return pl.pallas_call(
        functools.partial(pick_kernel, states, cap, count),
        grid_spec=pltpu.PrefetchScalarGridSpec(
            num_scalar_prefetch=1,
            grid=(1,),
            in_specs=[IN_HBM] * (len(came) + 1),
            out_specs=IN_HBM,
            scratch_shapes=[
                pltpu.VMEM(shape, late.dtype),
                pltpu.SemaphoreType.DMA((count, PIECES)),
            ],
        ),
        out_shape=jax.ShapeDtypeStruct(shape, late.dtype),
        compiler_params=pltpu.CompilerParams(vmem_limit_bytes=SMALL_VMEM),
        name="pick_states",
    )(table, *came, late)


def mamba_pre_kernel(
    heads,
    live_ref,
    first_ref,
    mix_ref,
    b_ref,
    c_ref,
    step_ref,
    decay_ref,
    skip_ref,
    spread_ref,
    split_ref,
    _pre_in,
    _z_in,
    _e_in,
    pre_ref,
    z_ref,
    e_ref,
    bs_ref,
    end_ref,
):
    block = pl.program_id(1)
    request = first_ref[0] + pl.program_id(0)
    copies = SPAN // heads
    row = lax.broadcasted_iota(jnp.int32, (SPAN, SPAN), 0)
    lane = lax.broadcasted_iota(jnp.int32, (SPAN, SPAN), 1)
    lower = row >= lane
    left = lane < MHDIM

    def three_way(value):
        high = value.astype(jnp.bfloat16)
        rest = value - high.astype(jnp.float32)
        middle = rest.astype(jnp.bfloat16)
        low = (rest - middle.astype(jnp.float32)).astype(jnp.bfloat16)
        high, middle, low = (v.astype(jnp.float32) for v in (high, middle, low))
        kept = jnp.where(
            lane < heads,
            high,
            jnp.where(lane < 2 * heads, middle, jnp.where(lane < 3 * heads, low, 0.0)),
        )
        return kept.astype(jnp.bfloat16)

    @pl.when((block == 0) | (live_ref[request] > SPAN))
    def _():
        raw = step_ref[...]
        rate_row = jnp.maximum(raw, 0.0) + jnp.log1p(jnp.exp(-jnp.abs(raw)))
        upper = jnp.where(row <= lane, 1.0, 0.0)
        cum_row = lax.dot_general(
            -rate_row * decay_ref[...],
            upper,
            (((1,), (0,)), ((), ())),
            precision=lax.Precision.HIGHEST,
            preferred_element_type=jnp.float32,
        )
        cum = jnp.concatenate([cum_row] * copies, axis=0).T
        rate_col = jnp.concatenate([rate_row] * copies, axis=0).T

        both = mm(split_ref[...], mix_ref[...])
        z_ref[...] = both[SPAN:].astype(jnp.bfloat16)
        x = both[:SPAN]
        x_half = x.astype(jnp.bfloat16)
        b = b_ref[...]
        c = c_ref[...]
        cross = mm(c, b, NT)

        def weights(h):
            fall = cum[:, h : h + 1] - cum_row[h : h + 1, :]
            fade = jnp.exp(jnp.where(lower, fall, NEG_FILL))
            return (cross * fade * rate_row[h : h + 1, :]).astype(jnp.bfloat16)

        for pair in range(heads // 2):
            cols = slice(pair * 2 * MHDIM, (pair + 1) * 2 * MHDIM)
            xp = x_half[:, cols]
            zero = jnp.zeros_like(xp)
            stacked = jnp.concatenate([jnp.where(left, xp, zero), jnp.where(left, zero, xp)], axis=0)
            w = jnp.concatenate([weights(2 * pair), weights(2 * pair + 1)], axis=1)
            pre_ref[:, cols] = mm(w, stacked) + skip_ref[:, cols] * x[:, cols]

        @pl.when(block == 0)
        def _():
            end = cum[SPAN - 1 : SPAN, :]
            tail = jnp.exp(end - cum) * rate_col
            scaled = (mm(three_way(tail), spread_ref[...]) * x).astype(jnp.bfloat16)
            bs_ref[...] = mm(scaled, b, TN).astype(jnp.bfloat16)
            end_ref[...] = jnp.broadcast_to(end, end_ref.shape)
            e_ref[...] = three_way(jnp.exp(cum))

        @pl.when(block == 1)
        def _():
            e_half = three_way(jnp.exp(cum))
            carried = mm(c, bs_ref[...], NT)
            pre_ref[...] += mm(e_half, spread_ref[...]) * carried
            e_ref[...] = three_way(jnp.exp(cum + end_ref[0:1, :]))


def mamba_pre(heads, first, count, live, here, mixed, b_rows, c_rows, step_row, decay, skip, spread, split, carry):
    width = heads * MHDIM
    rows = b_rows.shape[0]

    def at(r, k, *_):
        return ((first + r) * 2 + k, 0)

    def fixed(r, k, *_):
        return (0, 0)

    blocks = count * 2
    outs = [
        jax.ShapeDtypeStruct((rows, width), jnp.float32),
        jax.ShapeDtypeStruct((rows, width), jnp.bfloat16),
        jax.ShapeDtypeStruct((rows, 128), jnp.bfloat16),
    ]
    if carry is None:
        carry = tuple(jnp.zeros((16, 128), jnp.float32) for _ in outs)
        aliases = {}
    else:
        aliases = {10: 0, 11: 1, 12: 2}
    return pl.pallas_call(
        functools.partial(mamba_pre_kernel, heads),
        grid_spec=pltpu.PrefetchScalarGridSpec(
            num_scalar_prefetch=2,
            grid=(count, 2),
            in_specs=[
                pl.BlockSpec((2 * SPAN, width), at),
                pl.BlockSpec((SPAN, STATE), at),
                pl.BlockSpec((SPAN, STATE), at),
                pl.BlockSpec((heads, SPAN), lambda r, k, *_: (0, (first + r) * 2 + k)),
                pl.BlockSpec((heads, SPAN), fixed),
                pl.BlockSpec((1, width), fixed),
                pl.BlockSpec((128, width), fixed),
                pl.BlockSpec((2 * SPAN, 2 * SPAN), fixed),
                ANYWHERE,
                ANYWHERE,
                ANYWHERE,
            ],
            out_specs=[
                pl.BlockSpec((SPAN, width), at),
                pl.BlockSpec((SPAN, width), at),
                pl.BlockSpec((SPAN, 128), at),
            ],
            scratch_shapes=[
                pltpu.VMEM((width, STATE), jnp.bfloat16),
                pltpu.VMEM((8, 128), jnp.float32),
            ],
        ),
        out_shape=outs,
        input_output_aliases=aliases,
        compiler_params=pltpu.CompilerParams(vmem_limit_bytes=VMEM),
        cost_estimate=pl.CostEstimate(
            flops=blocks * heads * 40 * SPAN * SPAN * MHDIM,
            bytes_accessed=blocks * SPAN * width * 10,
            transcendentals=blocks * heads * SPAN * SPAN,
        ),
        name="mamba_pre",
    )(live, here + first, mixed, b_rows, c_rows, step_row, decay, skip, spread, split, *carry)


def mamba_post_kernel(
    heads,
    whole_group,
    count,
    cap,
    states,
    fixed,
    late,
    here_ref,
    table_ref,
    live_ref,
    *rest,
):
    outs = 1 if whole_group else 2
    pool_ref, near_ref, *came_refs, late_ref, other_ref = rest[: fixed + 4]
    c_ref, pre_ref, z_ref, e_ref, spread_ref, gain_ref, *rest = rest[fixed + 4 :]
    out_refs = rest[outs : 2 * outs]
    stage_refs = rest[2 * outs : 3 * outs]
    state_ref, sem, out_sem = rest[-3:]
    i = pl.program_id(0)
    width = heads * MHDIM
    owner = here_ref[0]
    here_now = table_ref[2 * cap + 1]
    active = count - here_now if late else here_now

    def put(i, r):
        rows = pl.ds(pl.multiple_of(r * SUF, SUF), SUF)
        return [
            pltpu.make_async_copy(stage.at[i % 2], out.at[rows], out_sem.at[k, i % 2])
            for k, (stage, out) in enumerate(zip(stage_refs, out_refs))
        ]

    def fetch(i):
        r = post_request(cap, count, late, i, table_ref)
        code = table_ref[2 * cap + 3 + count + r]
        slot = i % 2
        start_from(
            code, states, owner, pool_ref, near_ref, came_refs, late_ref, state_ref.at[slot], sem.at[slot]
        )
        if late:

            @pl.when(code < 0)
            def _():
                for k in range(PIECES):
                    pltpu.make_async_copy(
                        piece_of(other_ref.at[r], k), piece_of(state_ref.at[slot], k), sem.at[slot, k]
                    ).start()

    @pl.when((i == 0) & (i < active))
    def _():
        fetch(i)

    @pl.when(i + 1 < active)
    def _():
        fetch(i + 1)

    @pl.when(i < active)
    def _():
        r = post_request(cap, count, late, i, table_ref)
        finish(pool_ref.at[0], state_ref.at[i % 2], sem.at[i % 2])
        carried = mm(c_ref[...], state_ref[i % 2], NT)
        summed = pre_ref[...] + mm(e_ref[...], spread_ref[...]) * carried
        z = z_ref[...].astype(jnp.float32)
        gated = summed * (z / (1.0 + jnp.exp(-z)))
        square = jnp.sum(gated * gated, axis=1, keepdims=True)

        @pl.when(i >= 2)
        def _():
            for copy in put(i, 0):
                copy.wait()

        if whole_group:
            norm = lax.rsqrt(square / width + EPSILON)
            live = lax.broadcasted_iota(jnp.int32, (SUF, 1), 0) < live_ref[owner * count + r]
            stage_refs[0][i % 2] = jnp.where(live, gated * norm * gain_ref[...], 0.0).astype(jnp.bfloat16)
        else:
            stage_refs[0][i % 2] = gated
            stage_refs[1][i % 2] = jnp.broadcast_to(square, (SUF, 128))
        for copy in put(i, r):
            copy.start()

        @pl.when(i == active - 1)
        def _():
            for copy in put(i, 0):
                copy.wait()

            @pl.when(i >= 1)
            def _():
                for copy in put(i - 1, 0):
                    copy.wait()


def post_request(cap, count, late, i, table_ref):
    here_now = table_ref[2 * cap + 1]
    if late:
        spot = here_now + jnp.minimum(i, jnp.maximum(count - here_now - 1, 0))
    else:
        spot = jnp.minimum(i, jnp.maximum(here_now - 1, 0))
    return table_ref[2 * cap + 2 + jnp.minimum(spot, count - 1)]


def mamba_post(
    heads, whole_group, cap, states, here, table, live, pool, near, came, late_room, other, c_rows, pre, z, e3, spread, gain, carry
):
    width = heads * MHDIM
    rows = c_rows.shape[0]
    count = rows // SUF
    late = carry is not None
    held = len(came)

    def at(i, here_ref, table_ref, *_):
        return (post_request(cap, count, late, i, table_ref), 0)

    def fixed(i, *_):
        return (0, 0)

    out_shape = [jax.ShapeDtypeStruct((rows, width), jnp.bfloat16 if whole_group else jnp.float32)]
    if not whole_group:
        out_shape.append(jax.ShapeDtypeStruct((rows, 128), jnp.float32))
    aliases = {}
    if late:
        aliases = {3 + held + 10 + k: k for k in range(len(out_shape))}
    else:
        carry = [jnp.zeros((16, 128), jnp.float32)] * len(out_shape)
        other = late_room
    return pl.pallas_call(
        functools.partial(mamba_post_kernel, heads, whole_group, count, cap, states, held, late),
        grid_spec=pltpu.PrefetchScalarGridSpec(
            num_scalar_prefetch=3,
            grid=(count,),
            in_specs=[IN_HBM] * (held + 4)
            + [
                pl.BlockSpec((SUF, STATE), at),
                pl.BlockSpec((SUF, width), at),
                pl.BlockSpec((SUF, width), at),
                pl.BlockSpec((SUF, 128), at),
                pl.BlockSpec((128, width), fixed),
                pl.BlockSpec((1, width), fixed),
            ]
            + [ANYWHERE] * len(out_shape),
            out_specs=[IN_HBM] * len(out_shape),
            scratch_shapes=[pltpu.VMEM((2, SUF) + out.shape[1:], out.dtype) for out in out_shape]
            + [
                pltpu.VMEM((2, width, STATE), jnp.bfloat16),
                pltpu.SemaphoreType.DMA((2, PIECES)),
                pltpu.SemaphoreType.DMA((len(out_shape), 2)),
            ],
        ),
        out_shape=out_shape,
        input_output_aliases=aliases,
        compiler_params=pltpu.CompilerParams(vmem_limit_bytes=VMEM),
        cost_estimate=pl.CostEstimate(
            flops=2 * rows * width * STATE,
            bytes_accessed=rows * width * 6,
            transcendentals=rows * width,
        ),
        name="mamba_post",
    )(here, table, live, pool, near, *came, late_room, other, c_rows, pre, z, e3, spread, gain, *carry)


def attend_kernel(
    qheads,
    chips,
    half,
    first_ref,
    pages_ref,
    prefix_ref,
    live_ref,
    q_ref,
    ks_ref,
    vs_ref,
    *rest,
):
    parts = rest[: 2 * chips - 1]
    out_ref, kv_ref, s_ref, top_ref, total_ref, mixed_ref, sem = rest[2 * chips :]
    request = first_ref[0]
    owner = first_ref[1]
    scale = math.log2(math.e) / math.sqrt(HD)
    pairs = prefix_ref[request] // (2 * PAGE)
    start = half * SPAN
    live = live_ref[request]

    def columns(h):
        return slice(h * HD, (h + 1) * HD)

    @pl.when(start < live)
    def _():
        def begin(p, carry):
            page = pages_ref[request * MAXP + p]
            giver = page // PAGES_DEV
            core = owner % 2
            away = giver // 2 - owner // 2
            ahead = jnp.where(core == 0, -away, away)
            which = jnp.where(ahead >= 0, ahead, chips - 1 - ahead)
            carrier = jnp.where(ahead >= 0, core, 1 - core)
            spot = ((giver % 2) ^ carrier) * PAGES_DEV + page % PAGES_DEV
            for k, part in enumerate(parts):

                @pl.when(which == k)
                def _(part=part):
                    pltpu.make_async_copy(part.at[spot], kv_ref.at[p + 2], sem).start()

            return carry

        def end(p, carry):
            pltpu.make_async_copy(parts[0].at[0], kv_ref.at[p + 2], sem).wait()
            return carry

        lax.fori_loop(0, 2 * pairs, begin, 0)
        for page in range(2):
            at = slice(page * PAGE, (page + 1) * PAGE)
            kv_ref[page, 0] = ks_ref[at, :]
            kv_ref[page, 1] = vs_ref[at, :]
        lax.fori_loop(0, 2 * pairs, end, 0)
        odd = pairs % 2

        def block(first, pages, kv):
            return kv_ref[pl.ds(first, pages), kv].reshape(pages * PAGE, HD)

        def place(i):
            return 2 + 2 * odd + 4 * i

        def fold(s, act):
            return functools.reduce(act, [s[:, k : k + HD] for k in range(0, s.shape[1], HD)])

        def first_scores(pages):
            keys = block(0, pages, 0)
            row = lax.broadcasted_iota(jnp.int32, (SPAN, pages * PAGE), 0) + start
            lane = lax.broadcasted_iota(jnp.int32, (SPAN, pages * PAGE), 1)
            allowed = (row >= lane) | (lane >= SUF)
            for h in range(qheads):
                s = jnp.where(allowed, mm(q_ref[:, columns(h)], keys, NT), NEG_FILL)
                s_ref[0, h, :, : pages * PAGE] = s
                top_ref[h] = fold(s, jnp.maximum)

        def scores(i, carry):
            keys = block(place(i), 4, 0)
            for h in range(qheads):
                s = mm(q_ref[:, columns(h)], keys, NT)
                s_ref[i + 1, h] = s
                top_ref[h] = jnp.maximum(top_ref[h], fold(s, jnp.maximum))
            return carry

        def weigh(h, s, values):
            top = jnp.concatenate([top_ref[h]] * (s.shape[1] // HD), axis=1)
            probs = jnp.exp2((s - top) * scale)
            return fold(probs, jnp.add), mm(probs.astype(jnp.bfloat16), values)

        def first_values(pages):
            rows = block(0, pages, 1)
            for h in range(qheads):
                total_ref[h], mixed_ref[h] = weigh(h, s_ref[0, h, :, : pages * PAGE], rows)

        def values(i, carry):
            rows = block(place(i), 4, 1)
            for h in range(qheads):
                total, mixed = weigh(h, s_ref[i + 1, h], rows)
                total_ref[h] += total
                mixed_ref[h] += mixed
            return carry

        def first_block(act):
            @pl.when(odd == 0)
            def _():
                act(2)

            @pl.when(odd == 1)
            def _():
                act(4)

        first_block(first_scores)
        lax.fori_loop(0, pairs // 2, scores, 0)
        for h in range(qheads):
            top_ref[h] = jnp.broadcast_to(jnp.max(top_ref[h], axis=1, keepdims=True), (SPAN, HD))
        first_block(first_values)
        lax.fori_loop(0, pairs // 2, values, 0)
        keep_row = lax.broadcasted_iota(jnp.int32, (SPAN, 1), 0) + start < live
        for h in range(qheads):
            total = jnp.sum(total_ref[h], axis=1, keepdims=True)
            out_ref[:, columns(h)] = jnp.where(keep_row, mixed_ref[h] / total, 0.0).astype(out_ref.dtype)

    @pl.when(start >= live)
    def _():
        out_ref[...] = jnp.zeros_like(out_ref)


def attention(qheads, first, half, here, pages, prefix, live, queries, keys, values, parts, carry):
    most = MAXP // 4 + 1
    width = qheads * HD
    if carry is None:
        carry = jnp.zeros((16, 128), jnp.bfloat16)
        aliases = {}
    else:
        aliases = {7 + len(parts): 0}

    def at(*_):
        return (first * 2 + half, 0)

    return pl.pallas_call(
        functools.partial(attend_kernel, qheads, (len(parts) + 1) // 2, half),
        grid_spec=pltpu.PrefetchScalarGridSpec(
            num_scalar_prefetch=4,
            grid=(1,),
            in_specs=[
                pl.BlockSpec((SPAN, width), at),
                pl.BlockSpec((SUF, HD), lambda *_: (first, 0)),
                pl.BlockSpec((SUF, HD), lambda *_: (first, 0)),
            ]
            + [IN_HBM] * len(parts)
            + [ANYWHERE],
            out_specs=pl.BlockSpec((SPAN, width), at),
            scratch_shapes=[
                pltpu.VMEM((MAXP + 2, 2, PAGE, HD), jnp.bfloat16),
                pltpu.VMEM((most, qheads, SPAN, 4 * PAGE), jnp.float32),
                pltpu.VMEM((qheads, SPAN, HD), jnp.float32),
                pltpu.VMEM((qheads, SPAN, HD), jnp.float32),
                pltpu.VMEM((qheads, SPAN, HD), jnp.float32),
                pltpu.SemaphoreType.DMA,
            ],
        ),
        out_shape=jax.ShapeDtypeStruct(queries.shape, jnp.bfloat16),
        input_output_aliases=aliases,
        compiler_params=pltpu.CompilerParams(vmem_limit_bytes=VMEM),
        cost_estimate=pl.CostEstimate(
            flops=qheads * SPAN * (MAXP * PAGE + SUF) * HD * 4,
            bytes_accessed=SPAN * qheads * HD * 4 + MAXP * PAGE * HD * 4,
            transcendentals=qheads * SPAN * (MAXP * PAGE + SUF),
        ),
        name="attention",
    )(here, pages, prefix, live, queries, keys, values, *parts, carry)


def after(value, *others):
    return lax.optimization_barrier((value,) + others)[0]


def body(
    mixer_input,
    step_raw,
    decay_rate,
    skip_gain,
    state_proj,
    queries,
    suffix_kv,
    state_pool,
    page_pool,
    norm_gain,
    hit_owner,
    hit_slot,
    page_owner,
    page_slot,
    prefix_len,
    suffix_len,
):
    owners = lax.axis_size("owner")
    owner = lax.axis_index("owner").astype(jnp.int32)
    column = lax.axis_index("tensor")
    rows = mixer_input.shape[0]
    count = rows // SUF
    heads = decay_rate.shape[0]
    width = heads * MHDIM
    qheads = queries.shape[1] // HD
    per_group = SSM_HEAD_TOTAL // GROUPS
    group = column * heads // per_group
    kv_index = column * qheads // (QHEADS // KVHEADS)
    whole_group = heads == per_group
    chips = owners // 2
    per_chip = 2 * SLOTS_DEV
    states = owners * SLOTS_DEV
    here = owner.reshape(1)
    first = (owner * count).reshape(1)
    swap = [(o, o ^ 1) for o in range(owners)]

    def line(hop):
        up = [(o, o + 2) for o in range(0, owners - 2, 2) if o // 2 >= hop - 1]
        return up + [(o, o - 2) for o in range(3, owners, 2) if o // 2 <= chips - hop]

    def send(item, step):
        up = [(o, o + 2) for o in range(0, owners - 2, 2) if step >= HOP_STEPS * (o // 2)]
        down = [(o, o - 2) for o in range(3, owners, 2) if step >= HOP_STEPS * (chips - 1 - o // 2)]
        return lax.ppermute(item, "owner", up + down)

    def head_of(array, index, axis):
        return lax.dynamic_index_in_dim(array, index, axis, keepdims=False)

    pool = state_pool.reshape(SLOTS_DEV, width, STATE)
    near = lax.ppermute(pool, "owner", swap)
    own_pages = jnp.transpose(head_of(page_pool, kv_index, 3), (0, 2, 1, 3))
    near_pages = lax.ppermute(own_pages, "owner", swap)
    chip_pages = jnp.concatenate([own_pages, near_pages], axis=0)

    state_ids = (hit_owner[:, 0] * SLOTS_DEV + hit_slot).astype(jnp.int32)
    table, cap = route(state_ids, owner, chips, per_chip, 2 * count)

    spread_np = np.zeros((128, width), np.float32)
    for h in range(heads):
        for k in range(3):
            spread_np[k * heads + h, h * MHDIM : (h + 1) * MHDIM] = 1.0
    spread = jnp.asarray(spread_np, jnp.bfloat16)
    split_np = np.zeros((2 * SPAN, 2 * SPAN), np.float32)
    for i in range(SPAN):
        split_np[i, 2 * i] = 1.0
        split_np[SPAN + i, 2 * i + 1] = 1.0
    split = jnp.asarray(split_np, jnp.bfloat16)
    skip = jnp.repeat(skip_gain, MHDIM)[None, :]
    decay = jnp.broadcast_to(decay_rate[:, None], (heads, SPAN))
    step_row = step_raw.T
    page_ids = (page_owner[:, :, 0] * PAGES_DEV + page_slot).astype(jnp.int32).reshape(-1)
    made = {}

    def shape_inputs(tie):
        made["mixed"] = after(mixer_input, tie).reshape(2 * rows, width)
        maps = head_of(after(state_proj, tie), group, 2)
        made["b"], made["c"] = maps[:, 0], maps[:, 1]
        suffix = head_of(after(suffix_kv, tie), kv_index, 2)
        made["k"], made["v"] = suffix[:, 0], suffix[:, 1]
        return made["mixed"], made["b"], made["k"]

    def pre_part(r):
        def run(tie):
            made["pre"] = mamba_pre(
                heads,
                r,
                2,
                suffix_len,
                after(first, tie),
                made["mixed"],
                made["b"],
                made["c"],
                step_row,
                decay,
                skip,
                spread,
                split,
                made.get("pre"),
            )
            return (made["pre"][2],)

        return run

    def attention_part(r, half):
        def run(tie):
            place = jnp.concatenate([first + r, here])
            made["attn"] = attention(
                qheads,
                r,
                half,
                after(place, tie),
                page_ids,
                prefix_len,
                suffix_len,
                queries,
                made["k"],
                made["v"],
                made["parts"],
                made.get("attn"),
            )
            return (made["attn"],)

        return run

    def step_at(step):
        return jnp.full((1,), step, jnp.int32)

    beside = [shape_inputs] + [pre_part(r) for r in range(0, count, 2)]
    ours, theirs, came = [], [], []
    piece = chip_pages
    for hop in range(1, chips):
        got = lax.ppermute(piece, "owner", line(hop))
        tie, done = piece, ()
        if hop == 1:
            done = (table, near)
        else:
            step = HOP_STEPS * (hop - 2)
            items = take(states, HOP_STEPS, here, table, step_at(step), pool, near, came)
            items = [after(item, piece) for item in items]
            came += [send(item, step + k) for k, item in enumerate(items)]
            done = tuple(came[-HOP_STEPS:]) + tuple(theirs[-1:])
            tie = items[-1]
        beside_out = beside.pop(0)(tie) if beside else ()
        done += beside_out
        if hop > 1:
            theirs.append(lax.ppermute(after(piece, tie, *beside_out), "owner", swap))
        piece = after(got, *done)
        ours.append(piece)
    theirs.append(lax.ppermute(piece, "owner", swap))
    made["parts"] = [chip_pages] + ours + theirs

    beside += [attention_part(r, half) for r in range(count) for half in range(2)]
    started = HOP_STEPS * (chips - 2)
    fixed = started + FREE_STEPS
    items = take(states, LAG, after(here, piece), table, step_at(started), pool, near, came)
    flying = [send(item, started + k) for k, item in enumerate(items)]
    tie = items[-1]
    spare = len(beside) - FREE_STEPS

    def compute(tie, chunks):
        done = ()
        for _ in range(min(chunks, len(beside))):
            done = beside.pop(0)(tie)
            tie = done[0]
        return done

    for step in range(started + LAG, fixed):
        done = compute(tie, 1 + (step == started + LAG and spare > 0))
        came.append(after(flying.pop(0), *done))
        (item,) = take(states, 1, here, table, step_at(step), pool, near, came)
        flying.append(send(item, step))
        tie = item
    for k, got in enumerate(flying):
        done = compute(tie, 1 if k == 0 else len(beside))
        came.append(after(got, *done))
        tie = came[-1]

    def more(step, room):
        (item,) = take(states, 1, here, table, step.reshape(1), pool, near, came, room)
        return keep(fixed, step.reshape(1), send(item, fixed), room)

    room = blank(here, (cap - fixed,) + pool.shape[1:], pool.dtype)
    room = lax.fori_loop(fixed, table[2 * cap], more, room)

    picked = pick(states, cap, count, table, came, room)
    other = lax.ppermute(picked, "owner", swap)
    result = None
    for place in (after(here, picked), here):
        result = mamba_post(
            heads,
            whole_group,
            cap,
            states,
            place,
            table,
            suffix_len,
            pool,
            near,
            came,
            room,
            other,
            made["c"],
            *made["pre"],
            spread,
            norm_gain[None, :],
            result,
        )
    if whole_group:
        return (result[0], made["attn"])
    gated, partial_sum = result
    partial_sum = partial_sum[:, 0]
    spread_sum = jnp.where(jnp.arange(GROUPS)[:, None] == group, partial_sum[None, :], 0.0)
    totals = lax.psum(spread_sum, "tensor")
    square = lax.dynamic_index_in_dim(totals, group, 0, keepdims=False) / (per_group * MHDIM)
    my_suffix = lax.dynamic_slice_in_dim(suffix_len, first[0], count, 0)
    active = (jnp.arange(SUF)[None, :] < my_suffix[:, None]).reshape(-1)
    scaled = gated * lax.rsqrt(square + EPSILON)[:, None] * norm_gain[None, :]
    return (jnp.where(active[:, None], scaled, 0.0).astype(jnp.bfloat16), made["attn"])


def solution(mesh):
    return jax.shard_map(
        body,
        mesh=mesh,
        in_specs=(
            P("owner", None, "tensor"),
            P("owner", "tensor"),
            P("tensor"),
            P("tensor"),
            P("owner", None, None, None),
            P("owner", "tensor"),
            P("owner", None, None, None),
            P("owner", "tensor"),
            P("owner", None, None, None, None),
            P("tensor"),
            P(),
            P(),
            P(),
            P(),
            P(),
            P(),
        ),
        out_specs=(P("owner", "tensor"), P("owner", "tensor")),
        check_vma=False,
    )
```

```python
import functools
import math

import jax
import jax.numpy as jnp
import numpy as np
from jax import lax
from jax.experimental import pallas as pl
from jax.experimental.pallas import tpu as pltpu
from jax.sharding import PartitionSpec as P

SSM_HEAD_TOTAL = 128
MHDIM = 64
STATE = 256
GROUPS = 4
QHEADS = 32
KVHEADS = 4
HD = 128
PAGE = 128
SPAN = 128
SUF = 256
MAXP = 16
SLOTS_DEV = 4
PAGES_DEV = 16

EPSILON = 1e-05
NEG_FILL = -1e30
LAG = 2
HOP_STEPS = 2
FREE_STEPS = 7
VMEM = 48 * 1024 * 1024
SMALL_VMEM = 58 * 1024 * 1024

NT = (((1,), (1,)), ((), ()))
TN = (((0,), (0,)), ((), ()))


def mm(a, b, dims=(((1,), (0,)), ((), ()))):
    return lax.dot_general(a, b, dims, preferred_element_type=jnp.float32)


def route_kernel(chips, per_chip, reqs_per_chip, cap, ids_ref, here_ref, out_ref, need_ref, own_ref, tab_ref, code_ref):
    states = chips * per_chip
    chip_here = here_ref[0] // 2
    core_here = here_ref[0] % 2

    def clear(s, carry):
        need_ref[s] = 0
        return carry

    lax.fori_loop(0, states, clear, 0)

    def mark(r, carry):
        s = ids_ref[r]
        need_ref[s] = need_ref[s] | (1 << (r // reqs_per_chip))
        return carry

    lax.fori_loop(0, chips * reqs_per_chip, mark, 0)

    def put(base, length, row, from_ref):
        def one(t, carry):
            spot = jnp.clip(base + t, 0, 2 * chips * cap - 1)
            out_ref[row * cap + t] = jnp.where(t < length, from_ref[spot], states)
            return carry

        lax.fori_loop(0, cap, one, 0)

    steps = jnp.int32(0)
    for up in (True, False):
        before = jnp.int32(0)
        sent = jnp.int32(0)
        came = jnp.int32(0)
        for place in range(chips - 1):
            chip = place if up else chips - 1 - place
            base = ((0 if up else chips) + place) * cap

            def wanted(s, further=0, chip=chip, up=up):
                if up:
                    return (need_ref[s] >> (chip + 1 + further)) != 0
                return (need_ref[s] & ((1 << max(chip - further, 0)) - 1)) != 0

            count = jnp.int32(0)
            for far in (True, False):

                def own(i, n, far=far, chip=chip, wanted=wanted):
                    s = chip * per_chip + i
                    own_ref[n] = s
                    beyond = wanted(s, 1)
                    take = beyond if far else wanted(s) & jnp.logical_not(beyond)
                    return n + take.astype(jnp.int32)

                count = lax.fori_loop(0, per_chip, own, count)

            def fill(t, used, base=base, count=count):
                s = jnp.where(used < count, own_ref[used], states)
                tab_ref[base + t] = s
                code_ref[base + t] = s
                return jnp.minimum(used + 1, count)

            def forward(j, carry, base=base, wanted=wanted, fill=fill):
                t, used = carry
                s = tab_ref[base - cap + j]
                take = (s < states) & wanted(jnp.minimum(s, states - 1))
                later = jnp.where(take, jnp.maximum(t, j + LAG), t)
                used = lax.fori_loop(t, later, fill, used)
                tab_ref[base + later] = s
                code_ref[base + later] = states + 1 + j
                return later + take.astype(jnp.int32), used

            def idle(t, carry, base=base):
                tab_ref[base + t] = states
                code_ref[base + t] = states
                return carry

            lax.fori_loop(0, HOP_STEPS * place, idle, 0)
            t, used = jnp.int32(HOP_STEPS * place), jnp.int32(0)
            if place:
                t, used = lax.fori_loop(0, before, forward, (t, used))
            end = t + count - used
            lax.fori_loop(t, end, fill, used)
            before = end
            sent = jnp.where(chip_here == chip, end, sent)
            came = jnp.where(chip_here == (chip + 1 if up else chip - 1), end, came)
            steps = jnp.maximum(steps, end)
        here = chip_here if up else chips - 1 - chip_here
        side = 0 if up else chips

        @pl.when(core_here == (0 if up else 1))
        def _(here=here, side=side, sent=sent, came=came):
            put((side + here) * cap, sent, 0, code_ref)
            put((side + here - 1) * cap, came, 1, tab_ref)

        arrived = came if up else jnp.where(core_here == 0, arrived, came)

    out_ref[2 * cap] = steps
    mine = reqs_per_chip // 2
    asked = [here_ref[0] * mine + r for r in range(mine)] + [(here_ref[0] ^ 1) * mine + r for r in range(mine)]
    for k, request in enumerate(asked):
        state = ids_ref[request]
        out_ref[2 * cap + 3 + mine + k] = jnp.where(state // per_chip == chip_here, state, -1)

    def look(t, carry):
        came_now = out_ref[cap + t]
        for k, request in enumerate(asked):

            @pl.when(ids_ref[request] == came_now)
            def _(k=k):
                out_ref[2 * cap + 3 + mine + k] = states + 1 + t

        return carry

    lax.fori_loop(0, arrived, look, 0)
    found = jnp.int32(0)
    for here_now in (True, False):
        for r in range(mine):
            out_ref[2 * cap + 2 + found] = r
            found += ((out_ref[2 * cap + 3 + mine + r] >= 0) == here_now).astype(jnp.int32)
        if here_now:
            out_ref[2 * cap + 1] = found


def route(state_ids, owner, chips, per_chip, reqs_per_chip):
    cap = chips * per_chip + (LAG + HOP_STEPS) * chips + 8
    smem = pl.BlockSpec(memory_space=pltpu.SMEM)
    table = pl.pallas_call(
        functools.partial(route_kernel, chips, per_chip, reqs_per_chip, cap),
        out_shape=jax.ShapeDtypeStruct((2 * cap + 4 + 2 * reqs_per_chip,), jnp.int32),
        in_specs=[smem, smem],
        out_specs=smem,
        scratch_shapes=[
            pltpu.SMEM((chips * per_chip,), jnp.int32),
            pltpu.SMEM((2 * per_chip,), jnp.int32),
            pltpu.SMEM((2 * chips * cap,), jnp.int32),
            pltpu.SMEM((2 * chips * cap,), jnp.int32),
        ],
        name="route_states",
    )(state_ids, owner.reshape(1))
    return table, cap


ANYWHERE = pl.BlockSpec(memory_space=pl.ANY)
IN_HBM = pl.BlockSpec(memory_space=pltpu.HBM)
PIECES = 4


def piece_of(ref, k):
    rows = ref.shape[0] // PIECES
    return ref.at[pl.ds(k * rows, rows)]


def start_from(code, states, owner, pool_ref, near_ref, came_refs, late_ref, dst, sems):
    def start(ref):
        for k in range(PIECES):
            pltpu.make_async_copy(piece_of(ref, k), piece_of(dst, k), sems.at[k]).start()

    if pool_ref is not None:
        own = (code >= 0) & (code < states)
        slot = code % SLOTS_DEV

        @pl.when(own & (code // SLOTS_DEV == owner))
        def _():
            start(pool_ref.at[slot])

        @pl.when(own & (code // SLOTS_DEV != owner))
        def _():
            start(near_ref.at[slot])

    step = code - states - 1
    for k, ref in enumerate(came_refs):

        @pl.when(step == k)
        def _(ref=ref):
            start(ref)

    if late_ref is not None:

        @pl.when(step >= len(came_refs))
        def _():
            start(late_ref.at[step - len(came_refs)])


def pass_on(src, dst, sems):
    for k in range(PIECES):
        pltpu.make_async_copy(piece_of(dst, k), piece_of(src, k), sems.at[k]).wait()
        pltpu.make_async_copy(piece_of(src, k), piece_of(dst, k), sems.at[k]).start()


def finish(src, dst, sems):
    for k in range(PIECES):
        pltpu.make_async_copy(piece_of(src, k), piece_of(dst, k), sems.at[k]).wait()


def take_kernel(states, steps, late, here_ref, table_ref, step_ref, pool_ref, near_ref, *rest):
    sends, (item_ref, sem) = rest[-2 - steps : -2], rest[-2:]
    came_refs = rest[: -2 - steps]
    late_ref = None
    if late:
        came_refs, late_ref = came_refs[:-1], came_refs[-1]
    codes = [table_ref[step_ref[0] + t] for t in range(steps)]
    for t in range(steps):
        start_from(
            codes[t], states, here_ref[0], pool_ref, near_ref, came_refs, late_ref, item_ref.at[t], sem.at[t]
        )
    for act in (pass_on, finish):
        for t in range(steps):

            @pl.when(codes[t] != states)
            def _(t=t):
                act(item_ref.at[t], sends[t], sem.at[t])


def take(states, steps, here, table, step, pool, near, came, late=None):
    item = jax.ShapeDtypeStruct(pool.shape[1:], pool.dtype)
    came = list(came) + ([] if late is None else [late])
    return pl.pallas_call(
        functools.partial(take_kernel, states, steps, late is not None),
        grid_spec=pltpu.PrefetchScalarGridSpec(
            num_scalar_prefetch=3,
            grid=(1,),
            in_specs=[IN_HBM] * (2 + len(came)),
            out_specs=[IN_HBM] * steps,
            scratch_shapes=[
                pltpu.VMEM((steps,) + pool.shape[1:], pool.dtype),
                pltpu.SemaphoreType.DMA((steps, PIECES)),
            ],
        ),
        out_shape=[item] * steps,
        compiler_params=pltpu.CompilerParams(vmem_limit_bytes=SMALL_VMEM),
        name="take_states",
    )(here, table, step, pool, near, *came)


def keep_kernel(fixed, step_ref, got_ref, _late_in, late_ref, item_ref, sem):
    spot = late_ref.at[step_ref[0] - fixed]
    for k in range(PIECES):
        pltpu.make_async_copy(piece_of(got_ref, k), piece_of(item_ref, k), sem.at[k]).start()
    pass_on(item_ref, spot, sem)
    finish(item_ref, spot, sem)


def keep(fixed, step, got, late):
    return pl.pallas_call(
        functools.partial(keep_kernel, fixed),
        grid_spec=pltpu.PrefetchScalarGridSpec(
            num_scalar_prefetch=1,
            grid=(1,),
            in_specs=[IN_HBM, IN_HBM],
            out_specs=IN_HBM,
            scratch_shapes=[pltpu.VMEM(got.shape, got.dtype), pltpu.SemaphoreType.DMA((PIECES,))],
        ),
        out_shape=jax.ShapeDtypeStruct(late.shape, late.dtype),
        input_output_aliases={2: 0},
        compiler_params=pltpu.CompilerParams(vmem_limit_bytes=SMALL_VMEM),
        name="keep_state",
    )(step, got, late)


def blank_kernel(here_ref, out_ref):
    pass


def blank(here, shape, dtype):
    return pl.pallas_call(
        blank_kernel,
        in_specs=[pl.BlockSpec(memory_space=pltpu.SMEM)],
        out_specs=IN_HBM,
        out_shape=jax.ShapeDtypeStruct(shape, dtype),
        compiler_params=pltpu.CompilerParams(vmem_limit_bytes=SMALL_VMEM),
        name="room",
    )(here)


def pick_kernel(states, cap, count, table_ref, *rest):
    came_refs, late_ref = rest[:-4], rest[-4]
    out_ref, item_ref, sem = rest[-3:]
    codes = [table_ref[2 * cap + 3 + 2 * count + r] for r in range(count)]
    for r in range(count):

        @pl.when(codes[r] > states)
        def _(r=r):
            start_from(codes[r], states, -1, None, None, came_refs, late_ref, item_ref.at[r], sem.at[r])

    for act in (pass_on, finish):
        for r in range(count):

            @pl.when(codes[r] > states)
            def _(r=r):
                act(item_ref.at[r], out_ref.at[r], sem.at[r])


def pick(states, cap, count, table, came, late):
    shape = (count,) + late.shape[1:]
    return pl.pallas_call(
        functools.partial(pick_kernel, states, cap, count),
        grid_spec=pltpu.PrefetchScalarGridSpec(
            num_scalar_prefetch=1,
            grid=(1,),
            in_specs=[IN_HBM] * (len(came) + 1),
            out_specs=IN_HBM,
            scratch_shapes=[
                pltpu.VMEM(shape, late.dtype),
                pltpu.SemaphoreType.DMA((count, PIECES)),
            ],
        ),
        out_shape=jax.ShapeDtypeStruct(shape, late.dtype),
        compiler_params=pltpu.CompilerParams(vmem_limit_bytes=SMALL_VMEM),
        name="pick_states",
    )(table, *came, late)


def mamba_pre_kernel(
    heads,
    live_ref,
    first_ref,
    mix_ref,
    b_ref,
    c_ref,
    step_ref,
    decay_ref,
    skip_ref,
    spread_ref,
    split_ref,
    _pre_in,
    _z_in,
    _e_in,
    pre_ref,
    z_ref,
    e_ref,
    bs_ref,
    end_ref,
):
    block = pl.program_id(1)
    request = first_ref[0] + pl.program_id(0)
    copies = SPAN // heads
    row = lax.broadcasted_iota(jnp.int32, (SPAN, SPAN), 0)
    lane = lax.broadcasted_iota(jnp.int32, (SPAN, SPAN), 1)
    lower = row >= lane
    left = lane < MHDIM

    def three_way(value):
        high = value.astype(jnp.bfloat16)
        rest = value - high.astype(jnp.float32)
        middle = rest.astype(jnp.bfloat16)
        low = (rest - middle.astype(jnp.float32)).astype(jnp.bfloat16)
        high, middle, low = (v.astype(jnp.float32) for v in (high, middle, low))
        kept = jnp.where(
            lane < heads,
            high,
            jnp.where(lane < 2 * heads, middle, jnp.where(lane < 3 * heads, low, 0.0)),
        )
        return kept.astype(jnp.bfloat16)

    @pl.when((block == 0) | (live_ref[request] > SPAN))
    def _():
        raw = step_ref[...]
        rate_row = jnp.maximum(raw, 0.0) + jnp.log1p(jnp.exp(-jnp.abs(raw)))
        upper = jnp.where(row <= lane, 1.0, 0.0)
        cum_row = lax.dot_general(
            -rate_row * decay_ref[...],
            upper,
            (((1,), (0,)), ((), ())),
            precision=lax.Precision.HIGHEST,
            preferred_element_type=jnp.float32,
        )
        cum = jnp.concatenate([cum_row] * copies, axis=0).T
        rate_col = jnp.concatenate([rate_row] * copies, axis=0).T

        both = mm(split_ref[...], mix_ref[...].reshape(2 * SPAN, heads * MHDIM))
        z_ref[...] = both[SPAN:].astype(jnp.bfloat16)
        x = both[:SPAN]
        x_half = x.astype(jnp.bfloat16)
        b = b_ref[...]
        c = c_ref[...]
        cross = mm(c, b, NT)

        def weights(h):
            fall = cum[:, h : h + 1] - cum_row[h : h + 1, :]
            fade = jnp.exp(jnp.where(lower, fall, NEG_FILL))
            return (cross * fade * rate_row[h : h + 1, :]).astype(jnp.bfloat16)

        for pair in range(heads // 2):
            cols = slice(pair * 2 * MHDIM, (pair + 1) * 2 * MHDIM)
            xp = x_half[:, cols]
            zero = jnp.zeros_like(xp)
            stacked = jnp.concatenate([jnp.where(left, xp, zero), jnp.where(left, zero, xp)], axis=0)
            w = jnp.concatenate([weights(2 * pair), weights(2 * pair + 1)], axis=1)
            pre_ref[:, cols] = mm(w, stacked) + skip_ref[:, cols] * x[:, cols]

        @pl.when(block == 0)
        def _():
            end = cum[SPAN - 1 : SPAN, :]
            tail = jnp.exp(end - cum) * rate_col
            scaled = (mm(three_way(tail), spread_ref[...]) * x).astype(jnp.bfloat16)
            bs_ref[...] = mm(scaled, b, TN).astype(jnp.bfloat16)
            end_ref[...] = jnp.broadcast_to(end, end_ref.shape)
            e_ref[...] = three_way(jnp.exp(cum))

        @pl.when(block == 1)
        def _():
            e_half = three_way(jnp.exp(cum))
            carried = mm(c, bs_ref[...], NT)
            pre_ref[...] += mm(e_half, spread_ref[...]) * carried
            e_ref[...] = three_way(jnp.exp(cum + end_ref[0:1, :]))


def mamba_pre(heads, first, count, live, here, mixed, b_rows, c_rows, step_row, decay, skip, spread, split, carry):
    width = heads * MHDIM
    rows = b_rows.shape[0]

    def at(r, k, *_):
        return ((first + r) * 2 + k, 0)

    def fixed(r, k, *_):
        return (0, 0)

    blocks = count * 2
    outs = [
        jax.ShapeDtypeStruct((rows, width), jnp.float32),
        jax.ShapeDtypeStruct((rows, width), jnp.bfloat16),
        jax.ShapeDtypeStruct((rows, 128), jnp.bfloat16),
    ]
    if carry is None:
        carry = tuple(jnp.zeros((16, 128), jnp.float32) for _ in outs)
        aliases = {}
    else:
        aliases = {10: 0, 11: 1, 12: 2}
    return pl.pallas_call(
        functools.partial(mamba_pre_kernel, heads),
        grid_spec=pltpu.PrefetchScalarGridSpec(
            num_scalar_prefetch=2,
            grid=(count, 2),
            in_specs=[
                pl.BlockSpec((SPAN, 2, width), lambda r, k, *_: ((first + r) * 2 + k, 0, 0)),
                pl.BlockSpec((SPAN, STATE), at),
                pl.BlockSpec((SPAN, STATE), at),
                pl.BlockSpec((heads, SPAN), lambda r, k, *_: (0, (first + r) * 2 + k)),
                pl.BlockSpec((heads, SPAN), fixed),
                pl.BlockSpec((1, width), fixed),
                pl.BlockSpec((128, width), fixed),
                pl.BlockSpec((2 * SPAN, 2 * SPAN), fixed),
                ANYWHERE,
                ANYWHERE,
                ANYWHERE,
            ],
            out_specs=[
                pl.BlockSpec((SPAN, width), at),
                pl.BlockSpec((SPAN, width), at),
                pl.BlockSpec((SPAN, 128), at),
            ],
            scratch_shapes=[
                pltpu.VMEM((width, STATE), jnp.bfloat16),
                pltpu.VMEM((8, 128), jnp.float32),
            ],
        ),
        out_shape=outs,
        input_output_aliases=aliases,
        compiler_params=pltpu.CompilerParams(vmem_limit_bytes=VMEM),
        cost_estimate=pl.CostEstimate(
            flops=blocks * heads * 40 * SPAN * SPAN * MHDIM,
            bytes_accessed=blocks * SPAN * width * 10,
            transcendentals=blocks * heads * SPAN * SPAN,
        ),
        name="mamba_pre",
    )(live, here + first, mixed, b_rows, c_rows, step_row, decay, skip, spread, split, *carry)


def mamba_post_kernel(
    heads,
    whole_group,
    count,
    cap,
    states,
    fixed,
    late,
    here_ref,
    table_ref,
    live_ref,
    *rest,
):
    outs = 1 if whole_group else 2
    pool_ref, near_ref, *came_refs, late_ref, other_ref = rest[: fixed + 4]
    c_ref, pre_ref, z_ref, e_ref, spread_ref, gain_ref, *rest = rest[fixed + 4 :]
    out_refs = rest[outs : 2 * outs]
    stage_refs = rest[2 * outs : 3 * outs]
    state_ref, sem, out_sem = rest[-3:]
    i = pl.program_id(0)
    width = heads * MHDIM
    owner = here_ref[0]
    here_now = table_ref[2 * cap + 1]
    active = count - here_now if late else here_now

    def put(i, r):
        rows = pl.ds(pl.multiple_of(r * SUF, SUF), SUF)
        return [
            pltpu.make_async_copy(stage.at[i % 2], out.at[rows], out_sem.at[k, i % 2])
            for k, (stage, out) in enumerate(zip(stage_refs, out_refs))
        ]

    def fetch(i):
        r = post_request(cap, count, late, i, table_ref)
        code = table_ref[2 * cap + 3 + count + r]
        slot = i % 2
        start_from(
            code, states, owner, pool_ref, near_ref, came_refs, late_ref, state_ref.at[slot], sem.at[slot]
        )
        if late:

            @pl.when(code < 0)
            def _():
                for k in range(PIECES):
                    pltpu.make_async_copy(
                        piece_of(other_ref.at[r], k), piece_of(state_ref.at[slot], k), sem.at[slot, k]
                    ).start()

    @pl.when((i == 0) & (i < active))
    def _():
        fetch(i)

    @pl.when(i + 1 < active)
    def _():
        fetch(i + 1)

    @pl.when(i < active)
    def _():
        r = post_request(cap, count, late, i, table_ref)
        finish(pool_ref.at[0], state_ref.at[i % 2], sem.at[i % 2])
        carried = mm(c_ref[...], state_ref[i % 2], NT)
        summed = pre_ref[...] + mm(e_ref[...], spread_ref[...]) * carried
        z = z_ref[...].astype(jnp.float32)
        gated = summed * (z / (1.0 + jnp.exp(-z)))
        square = jnp.sum(gated * gated, axis=1, keepdims=True)

        @pl.when(i >= 2)
        def _():
            for copy in put(i, 0):
                copy.wait()

        if whole_group:
            norm = lax.rsqrt(square / width + EPSILON)
            live = lax.broadcasted_iota(jnp.int32, (SUF, 1), 0) < live_ref[owner * count + r]
            stage_refs[0][i % 2] = jnp.where(live, gated * norm * gain_ref[...], 0.0).astype(jnp.bfloat16)
        else:
            stage_refs[0][i % 2] = gated
            stage_refs[1][i % 2] = jnp.broadcast_to(square, (SUF, 128))
        for copy in put(i, r):
            copy.start()

        @pl.when(i == active - 1)
        def _():
            for copy in put(i, 0):
                copy.wait()

            @pl.when(i >= 1)
            def _():
                for copy in put(i - 1, 0):
                    copy.wait()


def post_request(cap, count, late, i, table_ref):
    here_now = table_ref[2 * cap + 1]
    if late:
        spot = here_now + jnp.minimum(i, jnp.maximum(count - here_now - 1, 0))
    else:
        spot = jnp.minimum(i, jnp.maximum(here_now - 1, 0))
    return table_ref[2 * cap + 2 + jnp.minimum(spot, count - 1)]


def mamba_post(
    heads, whole_group, cap, states, here, table, live, pool, near, came, late_room, other, c_rows, pre, z, e3, spread, gain, carry
):
    width = heads * MHDIM
    rows = c_rows.shape[0]
    count = rows // SUF
    late = carry is not None
    held = len(came)

    def at(i, here_ref, table_ref, *_):
        return (post_request(cap, count, late, i, table_ref), 0)

    def fixed(i, *_):
        return (0, 0)

    out_shape = [jax.ShapeDtypeStruct((rows, width), jnp.bfloat16 if whole_group else jnp.float32)]
    if not whole_group:
        out_shape.append(jax.ShapeDtypeStruct((rows, 128), jnp.float32))
    aliases = {}
    if late:
        aliases = {3 + held + 10 + k: k for k in range(len(out_shape))}
    else:
        carry = [jnp.zeros((16, 128), jnp.float32)] * len(out_shape)
        other = late_room
    return pl.pallas_call(
        functools.partial(mamba_post_kernel, heads, whole_group, count, cap, states, held, late),
        grid_spec=pltpu.PrefetchScalarGridSpec(
            num_scalar_prefetch=3,
            grid=(count,),
            in_specs=[IN_HBM] * (held + 4)
            + [
                pl.BlockSpec((SUF, STATE), at),
                pl.BlockSpec((SUF, width), at),
                pl.BlockSpec((SUF, width), at),
                pl.BlockSpec((SUF, 128), at),
                pl.BlockSpec((128, width), fixed),
                pl.BlockSpec((1, width), fixed),
            ]
            + [ANYWHERE] * len(out_shape),
            out_specs=[IN_HBM] * len(out_shape),
            scratch_shapes=[pltpu.VMEM((2, SUF) + out.shape[1:], out.dtype) for out in out_shape]
            + [
                pltpu.VMEM((2, width, STATE), jnp.bfloat16),
                pltpu.SemaphoreType.DMA((2, PIECES)),
                pltpu.SemaphoreType.DMA((len(out_shape), 2)),
            ],
        ),
        out_shape=out_shape,
        input_output_aliases=aliases,
        compiler_params=pltpu.CompilerParams(vmem_limit_bytes=VMEM),
        cost_estimate=pl.CostEstimate(
            flops=2 * rows * width * STATE,
            bytes_accessed=rows * width * 6,
            transcendentals=rows * width,
        ),
        name="mamba_post",
    )(here, table, live, pool, near, *came, late_room, other, c_rows, pre, z, e3, spread, gain, *carry)


def attend_kernel(
    qheads,
    chips,
    half,
    first_ref,
    pages_ref,
    prefix_ref,
    live_ref,
    q_ref,
    ks_ref,
    vs_ref,
    *rest,
):
    parts = rest[: 4 * chips - 2]
    out_ref, kv_ref, s_ref, top_ref, total_ref, mixed_ref, sem = rest[4 * chips - 1 :]
    request = first_ref[0]
    owner = first_ref[1]
    scale = math.log2(math.e) / math.sqrt(HD)
    pairs = prefix_ref[request] // (2 * PAGE)
    start = half * SPAN
    live = live_ref[request]

    def columns(h):
        return slice(h * HD, (h + 1) * HD)

    @pl.when(start < live)
    def _():
        def begin(p, carry):
            page = pages_ref[request * MAXP + p]
            giver = page // PAGES_DEV
            core = owner % 2
            away = giver // 2 - owner // 2
            ahead = jnp.where(core == 0, -away, away)
            which = jnp.where(ahead >= 0, ahead, chips - 1 - ahead)
            carrier = jnp.where(ahead >= 0, core, 1 - core)
            which = 2 * which + ((giver % 2) ^ carrier)
            spot = page % PAGES_DEV
            for k, part in enumerate(parts):

                @pl.when(which == k)
                def _(part=part):
                    pltpu.make_async_copy(part.at[spot], kv_ref.at[p + 2], sem).start()

            return carry

        def end(p, carry):
            pltpu.make_async_copy(parts[0].at[0], kv_ref.at[p + 2], sem).wait()
            return carry

        lax.fori_loop(0, 2 * pairs, begin, 0)
        for page in range(2):
            at = slice(page * PAGE, (page + 1) * PAGE)
            kv_ref[page, 0] = ks_ref[at, :]
            kv_ref[page, 1] = vs_ref[at, :]
        lax.fori_loop(0, 2 * pairs, end, 0)
        odd = pairs % 2

        def block(first, pages, kv):
            return kv_ref[pl.ds(first, pages), kv].reshape(pages * PAGE, HD)

        def place(i):
            return 2 + 2 * odd + 4 * i

        def fold(s, act):
            return functools.reduce(act, [s[:, k : k + HD] for k in range(0, s.shape[1], HD)])

        def first_scores(pages):
            keys = block(0, pages, 0)
            row = lax.broadcasted_iota(jnp.int32, (SPAN, pages * PAGE), 0) + start
            lane = lax.broadcasted_iota(jnp.int32, (SPAN, pages * PAGE), 1)
            allowed = (row >= lane) | (lane >= SUF)
            for h in range(qheads):
                s = jnp.where(allowed, mm(q_ref[:, columns(h)], keys, NT), NEG_FILL)
                s_ref[0, h, :, : pages * PAGE] = s
                top_ref[h] = fold(s, jnp.maximum)

        def scores(i, carry):
            keys = block(place(i), 4, 0)
            for h in range(qheads):
                s = mm(q_ref[:, columns(h)], keys, NT)
                s_ref[i + 1, h] = s
                top_ref[h] = jnp.maximum(top_ref[h], fold(s, jnp.maximum))
            return carry

        def weigh(h, s, values):
            top = jnp.concatenate([top_ref[h]] * (s.shape[1] // HD), axis=1)
            probs = jnp.exp2((s - top) * scale)
            return fold(probs, jnp.add), mm(probs.astype(jnp.bfloat16), values)

        def first_values(pages):
            rows = block(0, pages, 1)
            for h in range(qheads):
                total_ref[h], mixed_ref[h] = weigh(h, s_ref[0, h, :, : pages * PAGE], rows)

        def values(i, carry):
            rows = block(place(i), 4, 1)
            for h in range(qheads):
                total, mixed = weigh(h, s_ref[i + 1, h], rows)
                total_ref[h] += total
                mixed_ref[h] += mixed
            return carry

        def first_block(act):
            @pl.when(odd == 0)
            def _():
                act(2)

            @pl.when(odd == 1)
            def _():
                act(4)

        first_block(first_scores)
        lax.fori_loop(0, pairs // 2, scores, 0)
        for h in range(qheads):
            top_ref[h] = jnp.broadcast_to(jnp.max(top_ref[h], axis=1, keepdims=True), (SPAN, HD))
        first_block(first_values)
        lax.fori_loop(0, pairs // 2, values, 0)
        keep_row = lax.broadcasted_iota(jnp.int32, (SPAN, 1), 0) + start < live
        for h in range(qheads):
            total = jnp.sum(total_ref[h], axis=1, keepdims=True)
            out_ref[:, columns(h)] = jnp.where(keep_row, mixed_ref[h] / total, 0.0).astype(out_ref.dtype)

    @pl.when(start >= live)
    def _():
        out_ref[...] = jnp.zeros_like(out_ref)


def attention(qheads, first, half, here, pages, prefix, live, queries, keys, values, parts, carry):
    most = MAXP // 4 + 1
    width = qheads * HD
    if carry is None:
        carry = jnp.zeros((16, 128), jnp.bfloat16)
        aliases = {}
    else:
        aliases = {7 + len(parts): 0}

    def at(*_):
        return (first * 2 + half, 0)

    return pl.pallas_call(
        functools.partial(attend_kernel, qheads, (len(parts) + 2) // 4, half),
        grid_spec=pltpu.PrefetchScalarGridSpec(
            num_scalar_prefetch=4,
            grid=(1,),
            in_specs=[
                pl.BlockSpec((SPAN, width), at),
                pl.BlockSpec((SUF, HD), lambda *_: (first, 0)),
                pl.BlockSpec((SUF, HD), lambda *_: (first, 0)),
            ]
            + [IN_HBM] * len(parts)
            + [ANYWHERE],
            out_specs=pl.BlockSpec((SPAN, width), at),
            scratch_shapes=[
                pltpu.VMEM((MAXP + 2, 2, PAGE, HD), jnp.bfloat16),
                pltpu.VMEM((most, qheads, SPAN, 4 * PAGE), jnp.float32),
                pltpu.VMEM((qheads, SPAN, HD), jnp.float32),
                pltpu.VMEM((qheads, SPAN, HD), jnp.float32),
                pltpu.VMEM((qheads, SPAN, HD), jnp.float32),
                pltpu.SemaphoreType.DMA,
            ],
        ),
        out_shape=jax.ShapeDtypeStruct(queries.shape, jnp.bfloat16),
        input_output_aliases=aliases,
        compiler_params=pltpu.CompilerParams(vmem_limit_bytes=VMEM),
        cost_estimate=pl.CostEstimate(
            flops=qheads * SPAN * (MAXP * PAGE + SUF) * HD * 4,
            bytes_accessed=SPAN * qheads * HD * 4 + MAXP * PAGE * HD * 4,
            transcendentals=qheads * SPAN * (MAXP * PAGE + SUF),
        ),
        name="attention",
    )(here, pages, prefix, live, queries, keys, values, *parts, carry)


def after(value, *others):
    return lax.optimization_barrier((value,) + others)[0]


def body(
    mixer_input,
    step_raw,
    decay_rate,
    skip_gain,
    state_proj,
    queries,
    suffix_kv,
    state_pool,
    page_pool,
    norm_gain,
    hit_owner,
    hit_slot,
    page_owner,
    page_slot,
    prefix_len,
    suffix_len,
):
    owners = lax.axis_size("owner")
    owner = lax.axis_index("owner").astype(jnp.int32)
    column = lax.axis_index("tensor")
    rows = mixer_input.shape[0]
    count = rows // SUF
    heads = decay_rate.shape[0]
    width = heads * MHDIM
    qheads = queries.shape[1] // HD
    per_group = SSM_HEAD_TOTAL // GROUPS
    group = column * heads // per_group
    kv_index = column * qheads // (QHEADS // KVHEADS)
    whole_group = heads == per_group
    chips = owners // 2
    per_chip = 2 * SLOTS_DEV
    states = owners * SLOTS_DEV
    here = owner.reshape(1)
    first = (owner * count).reshape(1)
    swap = [(o, o ^ 1) for o in range(owners)]

    def line(hop):
        up = [(o, o + 2) for o in range(0, owners - 2, 2) if o // 2 >= hop - 1]
        return up + [(o, o - 2) for o in range(3, owners, 2) if o // 2 <= chips - hop]

    def send(item, step):
        up = [(o, o + 2) for o in range(0, owners - 2, 2) if step >= HOP_STEPS * (o // 2)]
        down = [(o, o - 2) for o in range(3, owners, 2) if step >= HOP_STEPS * (chips - 1 - o // 2)]
        return lax.ppermute(item, "owner", up + down)

    def head_of(array, index, axis):
        return lax.dynamic_index_in_dim(array, index, axis, keepdims=False)

    pool = state_pool.reshape(SLOTS_DEV, width, STATE)
    near = lax.ppermute(pool, "owner", swap)
    own_pages = jnp.transpose(head_of(page_pool, kv_index, 3), (0, 2, 1, 3))
    near_pages = lax.ppermute(own_pages, "owner", swap)

    state_ids = (hit_owner[:, 0] * SLOTS_DEV + hit_slot).astype(jnp.int32)
    table, cap = route(state_ids, owner, chips, per_chip, 2 * count)

    spread_np = np.zeros((128, width), np.float32)
    for h in range(heads):
        for k in range(3):
            spread_np[k * heads + h, h * MHDIM : (h + 1) * MHDIM] = 1.0
    spread = jnp.asarray(spread_np, jnp.bfloat16)
    split_np = np.zeros((2 * SPAN, 2 * SPAN), np.float32)
    for i in range(SPAN):
        split_np[i, 2 * i] = 1.0
        split_np[SPAN + i, 2 * i + 1] = 1.0
    split = jnp.asarray(split_np, jnp.bfloat16)
    skip = jnp.repeat(skip_gain, MHDIM)[None, :]
    decay = jnp.broadcast_to(decay_rate[:, None], (heads, SPAN))
    step_row = step_raw.T
    page_ids = (page_owner[:, :, 0] * PAGES_DEV + page_slot).astype(jnp.int32).reshape(-1)
    made = {}

    def shape_inputs(tie):
        maps = head_of(after(state_proj, tie), group, 2)
        made["b"], made["c"] = maps[:, 0], maps[:, 1]
        suffix = head_of(after(suffix_kv, tie), kv_index, 2)
        made["k"], made["v"] = suffix[:, 0], suffix[:, 1]
        return made["b"], made["k"]

    def pre_part(r):
        def run(tie):
            made["pre"] = mamba_pre(
                heads,
                r,
                2,
                suffix_len,
                after(first, tie),
                mixer_input,
                made["b"],
                made["c"],
                step_row,
                decay,
                skip,
                spread,
                split,
                made.get("pre"),
            )
            return (made["pre"][2],)

        return run

    def attention_part(r, half):
        def run(tie):
            place = jnp.concatenate([first + r, here])
            made["attn"] = attention(
                qheads,
                r,
                half,
                after(place, tie),
                page_ids,
                prefix_len,
                suffix_len,
                queries,
                made["k"],
                made["v"],
                made["parts"],
                made.get("attn"),
            )
            return (made["attn"],)

        return run

    def step_at(step):
        return jnp.full((1,), step, jnp.int32)

    beside = [shape_inputs] + [pre_part(r) for r in range(0, count, 2)]
    ours, theirs, came = [], [], []
    pieces = [own_pages, near_pages]
    for hop in range(1, chips):
        got = [lax.ppermute(piece, "owner", line(hop)) for piece in pieces]
        tie = pieces[0]
        if hop == 1:
            done = (table, near)
        else:
            step = HOP_STEPS * (hop - 2)
            items = take(states, HOP_STEPS, here, table, step_at(step), pool, near, came)
            items = [after(item, piece) for item, piece in zip(items, pieces)]
            came += [send(item, step + k) for k, item in enumerate(items)]
            tie = items[0]
            done = ()
        if beside:
            done += beside.pop(0)(tie)
        pieces = [after(piece, *done) for piece in got]
        ours += pieces
        theirs += [lax.ppermute(piece, "owner", swap) for piece in pieces]
    made["parts"] = [own_pages, near_pages] + ours + theirs

    beside += [attention_part(r, half) for r in range(count) for half in range(2)]
    started = HOP_STEPS * (chips - 2)
    fixed = started + FREE_STEPS
    items = take(states, LAG, after(here, pieces[1]), table, step_at(started), pool, near, came)
    flying = [send(item, started + k) for k, item in enumerate(items)]
    tie = items[-1]
    spare = len(beside) - FREE_STEPS

    def compute(tie, chunks):
        done = ()
        for _ in range(min(chunks, len(beside))):
            done = beside.pop(0)(tie)
            tie = done[0]
        return done

    for step in range(started + LAG, fixed):
        done = compute(tie, 1 + (step == started + LAG and spare > 0))
        came.append(after(flying.pop(0), *done))
        (item,) = take(states, 1, here, table, step_at(step), pool, near, came)
        flying.append(send(item, step))
        tie = item
    for k, got in enumerate(flying):
        done = compute(tie, 1 if k == 0 else len(beside))
        came.append(after(got, *done))
        tie = came[-1]

    def more(step, room):
        (item,) = take(states, 1, here, table, step.reshape(1), pool, near, came, room)
        return keep(fixed, step.reshape(1), send(item, fixed), room)

    room = blank(here, (cap - fixed,) + pool.shape[1:], pool.dtype)
    room = lax.fori_loop(fixed, table[2 * cap], more, room)

    picked = pick(states, cap, count, table, came, room)
    other = lax.ppermute(picked, "owner", swap)
    result = None
    for place in (after(here, picked), here):
        result = mamba_post(
            heads,
            whole_group,
            cap,
            states,
            place,
            table,
            suffix_len,
            pool,
            near,
            came,
            room,
            other,
            made["c"],
            *made["pre"],
            spread,
            norm_gain[None, :],
            result,
        )
    if whole_group:
        return (result[0], made["attn"])
    gated, partial_sum = result
    partial_sum = partial_sum[:, 0]
    spread_sum = jnp.where(jnp.arange(GROUPS)[:, None] == group, partial_sum[None, :], 0.0)
    totals = lax.psum(spread_sum, "tensor")
    square = lax.dynamic_index_in_dim(totals, group, 0, keepdims=False) / (per_group * MHDIM)
    my_suffix = lax.dynamic_slice_in_dim(suffix_len, first[0], count, 0)
    active = (jnp.arange(SUF)[None, :] < my_suffix[:, None]).reshape(-1)
    scaled = gated * lax.rsqrt(square + EPSILON)[:, None] * norm_gain[None, :]
    return (jnp.where(active[:, None], scaled, 0.0).astype(jnp.bfloat16), made["attn"])


def solution(mesh):
    return jax.shard_map(
        body,
        mesh=mesh,
        in_specs=(
            P("owner", None, "tensor"),
            P("owner", "tensor"),
            P("tensor"),
            P("tensor"),
            P("owner", None, None, None),
            P("owner", "tensor"),
            P("owner", None, None, None),
            P("owner", "tensor"),
            P("owner", None, None, None, None),
            P("tensor"),
            P(),
            P(),
            P(),
            P(),
            P(),
            P(),
        ),
        out_specs=(P("owner", "tensor"), P("owner", "tensor")),
        check_vma=False,
    )
```

```python
import functools
import math

import jax
import jax.numpy as jnp
import numpy as np
from jax import lax
from jax.experimental import pallas as pl
from jax.experimental.pallas import tpu as pltpu
from jax.sharding import PartitionSpec as P

SSM_HEAD_TOTAL = 128
MHDIM = 64
STATE = 256
GROUPS = 4
QHEADS = 32
KVHEADS = 4
HD = 128
PAGE = 128
SPAN = 128
SUF = 256
MAXP = 16
SLOTS_DEV = 4
PAGES_DEV = 16

EPSILON = 1e-05
NEG_FILL = -1e30
LAG = 2
HOP_STEPS = 2
FREE_STEPS = 7
VMEM = 48 * 1024 * 1024
SMALL_VMEM = 58 * 1024 * 1024

NT = (((1,), (1,)), ((), ()))
TN = (((0,), (0,)), ((), ()))


def mm(a, b, dims=(((1,), (0,)), ((), ()))):
    return lax.dot_general(a, b, dims, preferred_element_type=jnp.float32)


def route_kernel(chips, per_chip, reqs_per_chip, cap, ids_ref, here_ref, out_ref, need_ref, own_ref, tab_ref, code_ref):
    states = chips * per_chip
    chip_here = here_ref[0] // 2
    core_here = here_ref[0] % 2

    def clear(s, carry):
        need_ref[s] = 0
        return carry

    lax.fori_loop(0, states, clear, 0)

    def mark(r, carry):
        s = ids_ref[r]
        need_ref[s] = need_ref[s] | (1 << (r // reqs_per_chip))
        return carry

    lax.fori_loop(0, chips * reqs_per_chip, mark, 0)

    def put(base, length, row, from_ref):
        def one(t, carry):
            spot = jnp.clip(base + t, 0, 2 * chips * cap - 1)
            out_ref[row * cap + t] = jnp.where(t < length, from_ref[spot], states)
            return carry

        lax.fori_loop(0, cap, one, 0)

    steps = jnp.int32(0)
    for up in (True, False):
        before = jnp.int32(0)
        sent = jnp.int32(0)
        came = jnp.int32(0)
        for place in range(chips - 1):
            chip = place if up else chips - 1 - place
            base = ((0 if up else chips) + place) * cap

            def wanted(s, further=0, chip=chip, up=up):
                if up:
                    return (need_ref[s] >> (chip + 1 + further)) != 0
                return (need_ref[s] & ((1 << max(chip - further, 0)) - 1)) != 0

            count = jnp.int32(0)
            for far in (True, False):

                def own(i, n, far=far, chip=chip, wanted=wanted):
                    s = chip * per_chip + i
                    own_ref[n] = s
                    beyond = wanted(s, 1)
                    take = beyond if far else wanted(s) & jnp.logical_not(beyond)
                    return n + take.astype(jnp.int32)

                count = lax.fori_loop(0, per_chip, own, count)

            def fill(t, used, base=base, count=count):
                s = jnp.where(used < count, own_ref[used], states)
                tab_ref[base + t] = s
                code_ref[base + t] = s
                return jnp.minimum(used + 1, count)

            def forward(j, carry, base=base, wanted=wanted, fill=fill):
                t, used = carry
                s = tab_ref[base - cap + j]
                take = (s < states) & wanted(jnp.minimum(s, states - 1))
                later = jnp.where(take, jnp.maximum(t, j + LAG), t)
                used = lax.fori_loop(t, later, fill, used)
                tab_ref[base + later] = s
                code_ref[base + later] = states + 1 + j
                return later + take.astype(jnp.int32), used

            def idle(t, carry, base=base):
                tab_ref[base + t] = states
                code_ref[base + t] = states
                return carry

            lax.fori_loop(0, HOP_STEPS * place, idle, 0)
            t, used = jnp.int32(HOP_STEPS * place), jnp.int32(0)
            if place:
                t, used = lax.fori_loop(0, before, forward, (t, used))
            end = t + count - used
            lax.fori_loop(t, end, fill, used)
            before = end
            sent = jnp.where(chip_here == chip, end, sent)
            came = jnp.where(chip_here == (chip + 1 if up else chip - 1), end, came)
            steps = jnp.maximum(steps, end)
        here = chip_here if up else chips - 1 - chip_here
        side = 0 if up else chips

        @pl.when(core_here == (0 if up else 1))
        def _(here=here, side=side, sent=sent, came=came):
            put((side + here) * cap, sent, 0, code_ref)
            put((side + here - 1) * cap, came, 1, tab_ref)

        arrived = came if up else jnp.where(core_here == 0, arrived, came)

    out_ref[2 * cap] = steps
    mine = reqs_per_chip // 2
    asked = [here_ref[0] * mine + r for r in range(mine)] + [(here_ref[0] ^ 1) * mine + r for r in range(mine)]
    for k, request in enumerate(asked):
        state = ids_ref[request]
        out_ref[2 * cap + 3 + mine + k] = jnp.where(state // per_chip == chip_here, state, -1)

    def look(t, carry):
        came_now = out_ref[cap + t]
        for k, request in enumerate(asked):

            @pl.when(ids_ref[request] == came_now)
            def _(k=k):
                out_ref[2 * cap + 3 + mine + k] = states + 1 + t

        return carry

    lax.fori_loop(0, arrived, look, 0)
    found = jnp.int32(0)
    for here_now in (True, False):
        for r in range(mine):
            out_ref[2 * cap + 2 + found] = r
            found += ((out_ref[2 * cap + 3 + mine + r] >= 0) == here_now).astype(jnp.int32)
        if here_now:
            out_ref[2 * cap + 1] = found


def route(state_ids, owner, chips, per_chip, reqs_per_chip):
    cap = chips * per_chip + (LAG + HOP_STEPS) * chips + 8
    smem = pl.BlockSpec(memory_space=pltpu.SMEM)
    table = pl.pallas_call(
        functools.partial(route_kernel, chips, per_chip, reqs_per_chip, cap),
        out_shape=jax.ShapeDtypeStruct((2 * cap + 4 + 2 * reqs_per_chip,), jnp.int32),
        in_specs=[smem, smem],
        out_specs=smem,
        scratch_shapes=[
            pltpu.SMEM((chips * per_chip,), jnp.int32),
            pltpu.SMEM((2 * per_chip,), jnp.int32),
            pltpu.SMEM((2 * chips * cap,), jnp.int32),
            pltpu.SMEM((2 * chips * cap,), jnp.int32),
        ],
        name="route_states",
    )(state_ids, owner.reshape(1))
    return table, cap


ANYWHERE = pl.BlockSpec(memory_space=pl.ANY)
IN_HBM = pl.BlockSpec(memory_space=pltpu.HBM)
PIECES = 4


def piece_of(ref, k):
    rows = ref.shape[0] // PIECES
    return ref.at[pl.ds(k * rows, rows)]


def start_from(code, states, owner, pool_ref, near_ref, came_refs, late_ref, dst, sems):
    def start(ref):
        for k in range(PIECES):
            pltpu.make_async_copy(piece_of(ref, k), piece_of(dst, k), sems.at[k]).start()

    if pool_ref is not None:
        own = (code >= 0) & (code < states)
        slot = code % SLOTS_DEV

        @pl.when(own & (code // SLOTS_DEV == owner))
        def _():
            start(pool_ref.at[slot])

        @pl.when(own & (code // SLOTS_DEV != owner))
        def _():
            start(near_ref.at[slot])

    step = code - states - 1
    for k, ref in enumerate(came_refs):

        @pl.when(step == k)
        def _(ref=ref):
            start(ref)

    if late_ref is not None:

        @pl.when(step >= len(came_refs))
        def _():
            start(late_ref.at[step - len(came_refs)])


def pass_on(src, dst, sems):
    for k in range(PIECES):
        pltpu.make_async_copy(piece_of(dst, k), piece_of(src, k), sems.at[k]).wait()
        pltpu.make_async_copy(piece_of(src, k), piece_of(dst, k), sems.at[k]).start()


def finish(src, dst, sems):
    for k in range(PIECES):
        pltpu.make_async_copy(piece_of(src, k), piece_of(dst, k), sems.at[k]).wait()


def take_kernel(states, steps, late, here_ref, table_ref, step_ref, pool_ref, near_ref, *rest):
    sends, (item_ref, sem) = rest[-2 - steps : -2], rest[-2:]
    came_refs = rest[: -2 - steps]
    late_ref = None
    if late:
        came_refs, late_ref = came_refs[:-1], came_refs[-1]
    codes = [table_ref[step_ref[0] + t] for t in range(steps)]
    for t in range(steps):
        start_from(
            codes[t], states, here_ref[0], pool_ref, near_ref, came_refs, late_ref, item_ref.at[t], sem.at[t]
        )
    for act in (pass_on, finish):
        for t in range(steps):

            @pl.when(codes[t] != states)
            def _(t=t):
                act(item_ref.at[t], sends[t], sem.at[t])


def take(states, steps, here, table, step, pool, near, came, late=None):
    item = jax.ShapeDtypeStruct(pool.shape[1:], pool.dtype)
    came = list(came) + ([] if late is None else [late])
    return pl.pallas_call(
        functools.partial(take_kernel, states, steps, late is not None),
        grid_spec=pltpu.PrefetchScalarGridSpec(
            num_scalar_prefetch=3,
            grid=(1,),
            in_specs=[IN_HBM] * (2 + len(came)),
            out_specs=[IN_HBM] * steps,
            scratch_shapes=[
                pltpu.VMEM((steps,) + pool.shape[1:], pool.dtype),
                pltpu.SemaphoreType.DMA((steps, PIECES)),
            ],
        ),
        out_shape=[item] * steps,
        compiler_params=pltpu.CompilerParams(vmem_limit_bytes=SMALL_VMEM),
        name="take_states",
    )(here, table, step, pool, near, *came)


def keep_kernel(fixed, step_ref, got_ref, _late_in, late_ref, item_ref, sem):
    spot = late_ref.at[step_ref[0] - fixed]
    for k in range(PIECES):
        pltpu.make_async_copy(piece_of(got_ref, k), piece_of(item_ref, k), sem.at[k]).start()
    pass_on(item_ref, spot, sem)
    finish(item_ref, spot, sem)


def keep(fixed, step, got, late):
    return pl.pallas_call(
        functools.partial(keep_kernel, fixed),
        grid_spec=pltpu.PrefetchScalarGridSpec(
            num_scalar_prefetch=1,
            grid=(1,),
            in_specs=[IN_HBM, IN_HBM],
            out_specs=IN_HBM,
            scratch_shapes=[pltpu.VMEM(got.shape, got.dtype), pltpu.SemaphoreType.DMA((PIECES,))],
        ),
        out_shape=jax.ShapeDtypeStruct(late.shape, late.dtype),
        input_output_aliases={2: 0},
        compiler_params=pltpu.CompilerParams(vmem_limit_bytes=SMALL_VMEM),
        name="keep_state",
    )(step, got, late)


def blank_kernel(here_ref, out_ref):
    pass


def blank(here, shape, dtype):
    return pl.pallas_call(
        blank_kernel,
        in_specs=[pl.BlockSpec(memory_space=pltpu.SMEM)],
        out_specs=IN_HBM,
        out_shape=jax.ShapeDtypeStruct(shape, dtype),
        compiler_params=pltpu.CompilerParams(vmem_limit_bytes=SMALL_VMEM),
        name="room",
    )(here)


def pick_kernel(states, cap, count, table_ref, *rest):
    came_refs, late_ref = rest[:-4], rest[-4]
    out_ref, item_ref, sem = rest[-3:]
    codes = [table_ref[2 * cap + 3 + 2 * count + r] for r in range(count)]
    for r in range(count):

        @pl.when(codes[r] > states)
        def _(r=r):
            start_from(codes[r], states, -1, None, None, came_refs, late_ref, item_ref.at[r], sem.at[r])

    for act in (pass_on, finish):
        for r in range(count):

            @pl.when(codes[r] > states)
            def _(r=r):
                act(item_ref.at[r], out_ref.at[r], sem.at[r])


def pick(states, cap, count, table, came, late):
    shape = (count,) + late.shape[1:]
    return pl.pallas_call(
        functools.partial(pick_kernel, states, cap, count),
        grid_spec=pltpu.PrefetchScalarGridSpec(
            num_scalar_prefetch=1,
            grid=(1,),
            in_specs=[IN_HBM] * (len(came) + 1),
            out_specs=IN_HBM,
            scratch_shapes=[
                pltpu.VMEM(shape, late.dtype),
                pltpu.SemaphoreType.DMA((count, PIECES)),
            ],
        ),
        out_shape=jax.ShapeDtypeStruct(shape, late.dtype),
        compiler_params=pltpu.CompilerParams(vmem_limit_bytes=SMALL_VMEM),
        name="pick_states",
    )(table, *came, late)


def mamba_pre_kernel(
    heads,
    live_ref,
    first_ref,
    mix_ref,
    b_ref,
    c_ref,
    step_ref,
    decay_ref,
    skip_ref,
    spread_ref,
    split_ref,
    _pre_in,
    _z_in,
    _e_in,
    pre_ref,
    z_ref,
    e_ref,
    bs_ref,
    end_ref,
):
    block = pl.program_id(1)
    request = first_ref[0] + pl.program_id(0)
    copies = SPAN // heads
    row = lax.broadcasted_iota(jnp.int32, (SPAN, SPAN), 0)
    lane = lax.broadcasted_iota(jnp.int32, (SPAN, SPAN), 1)
    lower = row >= lane
    left = lane < MHDIM

    def three_way(value):
        high = value.astype(jnp.bfloat16)
        rest = value - high.astype(jnp.float32)
        middle = rest.astype(jnp.bfloat16)
        low = (rest - middle.astype(jnp.float32)).astype(jnp.bfloat16)
        high, middle, low = (v.astype(jnp.float32) for v in (high, middle, low))
        kept = jnp.where(
            lane < heads,
            high,
            jnp.where(lane < 2 * heads, middle, jnp.where(lane < 3 * heads, low, 0.0)),
        )
        return kept.astype(jnp.bfloat16)

    @pl.when((block == 0) | (live_ref[request] > SPAN))
    def _():
        raw = step_ref[...]
        rate_row = jnp.maximum(raw, 0.0) + jnp.log1p(jnp.exp(-jnp.abs(raw)))
        upper = jnp.where(row <= lane, 1.0, 0.0)
        cum_row = lax.dot_general(
            -rate_row * decay_ref[...],
            upper,
            (((1,), (0,)), ((), ())),
            precision=lax.Precision.HIGHEST,
            preferred_element_type=jnp.float32,
        )
        cum = jnp.concatenate([cum_row] * copies, axis=0).T
        rate_col = jnp.concatenate([rate_row] * copies, axis=0).T

        both = mm(split_ref[...], mix_ref[...].reshape(2 * SPAN, heads * MHDIM))
        z_ref[...] = both[SPAN:].astype(jnp.bfloat16)
        x = both[:SPAN]
        x_half = x.astype(jnp.bfloat16)
        b = b_ref[...]
        c = c_ref[...]
        cross = mm(c, b, NT)

        def weights(h):
            fall = cum[:, h : h + 1] - cum_row[h : h + 1, :]
            fade = jnp.exp(jnp.where(lower, fall, NEG_FILL))
            return (cross * fade * rate_row[h : h + 1, :]).astype(jnp.bfloat16)

        for pair in range(heads // 2):
            cols = slice(pair * 2 * MHDIM, (pair + 1) * 2 * MHDIM)
            xp = x_half[:, cols]
            zero = jnp.zeros_like(xp)
            stacked = jnp.concatenate([jnp.where(left, xp, zero), jnp.where(left, zero, xp)], axis=0)
            w = jnp.concatenate([weights(2 * pair), weights(2 * pair + 1)], axis=1)
            pre_ref[:, cols] = mm(w, stacked) + skip_ref[:, cols] * x[:, cols]

        @pl.when(block == 0)
        def _():
            end = cum[SPAN - 1 : SPAN, :]
            tail = jnp.exp(end - cum) * rate_col
            scaled = (mm(three_way(tail), spread_ref[...]) * x).astype(jnp.bfloat16)
            bs_ref[...] = mm(scaled, b, TN).astype(jnp.bfloat16)
            end_ref[...] = jnp.broadcast_to(end, end_ref.shape)
            e_ref[...] = three_way(jnp.exp(cum))

        @pl.when(block == 1)
        def _():
            e_half = three_way(jnp.exp(cum))
            carried = mm(c, bs_ref[...], NT)
            pre_ref[...] += mm(e_half, spread_ref[...]) * carried
            e_ref[...] = three_way(jnp.exp(cum + end_ref[0:1, :]))


def mamba_pre(heads, first, count, live, here, mixed, b_rows, c_rows, step_row, decay, skip, spread, split, carry):
    width = heads * MHDIM
    rows = b_rows.shape[0]

    def at(r, k, *_):
        return ((first + r) * 2 + k, 0)

    def fixed(r, k, *_):
        return (0, 0)

    blocks = count * 2
    outs = [
        jax.ShapeDtypeStruct((rows, width), jnp.float32),
        jax.ShapeDtypeStruct((rows, width), jnp.bfloat16),
        jax.ShapeDtypeStruct((rows, 128), jnp.bfloat16),
    ]
    if carry is None:
        carry = tuple(jnp.zeros((16, 128), jnp.float32) for _ in outs)
        aliases = {}
    else:
        aliases = {10: 0, 11: 1, 12: 2}
    return pl.pallas_call(
        functools.partial(mamba_pre_kernel, heads),
        grid_spec=pltpu.PrefetchScalarGridSpec(
            num_scalar_prefetch=2,
            grid=(count, 2),
            in_specs=[
                pl.BlockSpec((SPAN, 2, width), lambda r, k, *_: ((first + r) * 2 + k, 0, 0)),
                pl.BlockSpec((SPAN, STATE), at),
                pl.BlockSpec((SPAN, STATE), at),
                pl.BlockSpec((heads, SPAN), lambda r, k, *_: (0, (first + r) * 2 + k)),
                pl.BlockSpec((heads, SPAN), fixed),
                pl.BlockSpec((1, width), fixed),
                pl.BlockSpec((128, width), fixed),
                pl.BlockSpec((2 * SPAN, 2 * SPAN), fixed),
                ANYWHERE,
                ANYWHERE,
                ANYWHERE,
            ],
            out_specs=[
                pl.BlockSpec((SPAN, width), at),
                pl.BlockSpec((SPAN, width), at),
                pl.BlockSpec((SPAN, 128), at),
            ],
            scratch_shapes=[
                pltpu.VMEM((width, STATE), jnp.bfloat16),
                pltpu.VMEM((8, 128), jnp.float32),
            ],
        ),
        out_shape=outs,
        input_output_aliases=aliases,
        compiler_params=pltpu.CompilerParams(vmem_limit_bytes=VMEM),
        cost_estimate=pl.CostEstimate(
            flops=blocks * heads * 40 * SPAN * SPAN * MHDIM,
            bytes_accessed=blocks * SPAN * width * 10,
            transcendentals=blocks * heads * SPAN * SPAN,
        ),
        name="mamba_pre",
    )(live, here + first, mixed, b_rows, c_rows, step_row, decay, skip, spread, split, *carry)


def mamba_post_kernel(
    heads,
    whole_group,
    count,
    cap,
    states,
    fixed,
    late,
    here_ref,
    table_ref,
    live_ref,
    *rest,
):
    outs = 1 if whole_group else 2
    pool_ref, near_ref, *came_refs, late_ref, other_ref = rest[: fixed + 4]
    c_ref, pre_ref, z_ref, e_ref, spread_ref, gain_ref, *rest = rest[fixed + 4 :]
    out_refs = rest[outs : 2 * outs]
    stage_refs = rest[2 * outs : 3 * outs]
    state_ref, sem, out_sem = rest[-3:]
    i = pl.program_id(0)
    width = heads * MHDIM
    owner = here_ref[0]
    here_now = table_ref[2 * cap + 1]
    active = count - here_now if late else here_now

    def put(i, r):
        rows = pl.ds(pl.multiple_of(r * SUF, SUF), SUF)
        return [
            pltpu.make_async_copy(stage.at[i % 2], out.at[rows], out_sem.at[k, i % 2])
            for k, (stage, out) in enumerate(zip(stage_refs, out_refs))
        ]

    def fetch(i):
        r = post_request(cap, count, late, i, table_ref)
        code = table_ref[2 * cap + 3 + count + r]
        slot = i % 2
        start_from(
            code, states, owner, pool_ref, near_ref, came_refs, late_ref, state_ref.at[slot], sem.at[slot]
        )
        if late:

            @pl.when(code < 0)
            def _():
                for k in range(PIECES):
                    pltpu.make_async_copy(
                        piece_of(other_ref.at[r], k), piece_of(state_ref.at[slot], k), sem.at[slot, k]
                    ).start()

    @pl.when((i == 0) & (i < active))
    def _():
        fetch(i)

    @pl.when(i + 1 < active)
    def _():
        fetch(i + 1)

    @pl.when(i < active)
    def _():
        r = post_request(cap, count, late, i, table_ref)
        finish(pool_ref.at[0], state_ref.at[i % 2], sem.at[i % 2])
        carried = mm(c_ref[...], state_ref[i % 2], NT)
        summed = pre_ref[...] + mm(e_ref[...], spread_ref[...]) * carried
        z = z_ref[...].astype(jnp.float32)
        gated = summed * (z / (1.0 + jnp.exp(-z)))
        square = jnp.sum(gated * gated, axis=1, keepdims=True)

        @pl.when(i >= 2)
        def _():
            for copy in put(i, 0):
                copy.wait()

        if whole_group:
            norm = lax.rsqrt(square / width + EPSILON)
            live = lax.broadcasted_iota(jnp.int32, (SUF, 1), 0) < live_ref[owner * count + r]
            stage_refs[0][i % 2] = jnp.where(live, gated * norm * gain_ref[...], 0.0).astype(jnp.bfloat16)
        else:
            stage_refs[0][i % 2] = gated
            stage_refs[1][i % 2] = jnp.broadcast_to(square, (SUF, 128))
        for copy in put(i, r):
            copy.start()

        @pl.when(i == active - 1)
        def _():
            for copy in put(i, 0):
                copy.wait()

            @pl.when(i >= 1)
            def _():
                for copy in put(i - 1, 0):
                    copy.wait()


def post_request(cap, count, late, i, table_ref):
    here_now = table_ref[2 * cap + 1]
    if late:
        spot = here_now + jnp.minimum(i, jnp.maximum(count - here_now - 1, 0))
    else:
        spot = jnp.minimum(i, jnp.maximum(here_now - 1, 0))
    return table_ref[2 * cap + 2 + jnp.minimum(spot, count - 1)]


def mamba_post(
    heads, whole_group, cap, states, here, table, live, pool, near, came, late_room, other, c_rows, pre, z, e3, spread, gain, carry
):
    width = heads * MHDIM
    rows = c_rows.shape[0]
    count = rows // SUF
    late = carry is not None
    held = len(came)

    def at(i, here_ref, table_ref, *_):
        return (post_request(cap, count, late, i, table_ref), 0)

    def fixed(i, *_):
        return (0, 0)

    out_shape = [jax.ShapeDtypeStruct((rows, width), jnp.bfloat16 if whole_group else jnp.float32)]
    if not whole_group:
        out_shape.append(jax.ShapeDtypeStruct((rows, 128), jnp.float32))
    aliases = {}
    if late:
        aliases = {3 + held + 10 + k: k for k in range(len(out_shape))}
    else:
        carry = [jnp.zeros((16, 128), jnp.float32)] * len(out_shape)
        other = late_room
    return pl.pallas_call(
        functools.partial(mamba_post_kernel, heads, whole_group, count, cap, states, held, late),
        grid_spec=pltpu.PrefetchScalarGridSpec(
            num_scalar_prefetch=3,
            grid=(count,),
            in_specs=[IN_HBM] * (held + 4)
            + [
                pl.BlockSpec((SUF, STATE), at),
                pl.BlockSpec((SUF, width), at),
                pl.BlockSpec((SUF, width), at),
                pl.BlockSpec((SUF, 128), at),
                pl.BlockSpec((128, width), fixed),
                pl.BlockSpec((1, width), fixed),
            ]
            + [ANYWHERE] * len(out_shape),
            out_specs=[IN_HBM] * len(out_shape),
            scratch_shapes=[pltpu.VMEM((2, SUF) + out.shape[1:], out.dtype) for out in out_shape]
            + [
                pltpu.VMEM((2, width, STATE), jnp.bfloat16),
                pltpu.SemaphoreType.DMA((2, PIECES)),
                pltpu.SemaphoreType.DMA((len(out_shape), 2)),
            ],
        ),
        out_shape=out_shape,
        input_output_aliases=aliases,
        compiler_params=pltpu.CompilerParams(vmem_limit_bytes=VMEM),
        cost_estimate=pl.CostEstimate(
            flops=2 * rows * width * STATE,
            bytes_accessed=rows * width * 6,
            transcendentals=rows * width,
        ),
        name="mamba_post",
    )(here, table, live, pool, near, *came, late_room, other, c_rows, pre, z, e3, spread, gain, *carry)


def attend_kernel(
    qheads,
    chips,
    first_ref,
    pages_ref,
    prefix_ref,
    live_ref,
    q_ref,
    ks_ref,
    vs_ref,
    *rest,
):
    parts = rest[: 4 * chips - 2]
    out_ref, kv_ref, s_ref, top_ref, total_ref, mixed_ref, sem = rest[4 * chips - 1 :]
    request = first_ref[0]
    owner = first_ref[1]
    scale = math.log2(math.e) / math.sqrt(HD)
    pairs = prefix_ref[request] // (2 * PAGE)
    half = pl.program_id(0)
    start = half * SPAN
    live = live_ref[request]

    def columns(h):
        return slice(h * HD, (h + 1) * HD)

    @pl.when(half == 0)
    def _():
        def begin(p, carry):
            page = pages_ref[request * MAXP + p]
            giver = page // PAGES_DEV
            core = owner % 2
            away = giver // 2 - owner // 2
            ahead = jnp.where(core == 0, -away, away)
            which = jnp.where(ahead >= 0, ahead, chips - 1 - ahead)
            carrier = jnp.where(ahead >= 0, core, 1 - core)
            which = 2 * which + ((giver % 2) ^ carrier)
            spot = page % PAGES_DEV

            def fetch(low, high):
                if high - low == 1:
                    pltpu.make_async_copy(parts[low].at[spot], kv_ref.at[p + 2], sem).start()
                    return
                middle = (low + high) // 2

                @pl.when(which < middle)
                def _():
                    fetch(low, middle)

                @pl.when(which >= middle)
                def _():
                    fetch(middle, high)

            fetch(0, len(parts))
            return carry

        def end(p, carry):
            pltpu.make_async_copy(parts[0].at[0], kv_ref.at[p + 2], sem).wait()
            return carry

        lax.fori_loop(0, 2 * pairs, begin, 0)
        for page in range(2):
            at = slice(page * PAGE, (page + 1) * PAGE)
            kv_ref[page, 0] = ks_ref[at, :]
            kv_ref[page, 1] = vs_ref[at, :]
        lax.fori_loop(0, 2 * pairs, end, 0)

    @pl.when(start < live)
    def _():
        odd = pairs % 2

        def block(first, pages, kv):
            return kv_ref[pl.ds(first, pages), kv].reshape(pages * PAGE, HD)

        def place(i):
            return 2 + 2 * odd + 4 * i

        def fold(s, act):
            return functools.reduce(act, [s[:, k : k + HD] for k in range(0, s.shape[1], HD)])

        def first_scores(pages):
            keys = block(0, pages, 0)
            row = lax.broadcasted_iota(jnp.int32, (SPAN, pages * PAGE), 0) + start
            lane = lax.broadcasted_iota(jnp.int32, (SPAN, pages * PAGE), 1)
            allowed = (row >= lane) | (lane >= SUF)
            for h in range(qheads):
                s = jnp.where(allowed, mm(q_ref[:, columns(h)], keys, NT), NEG_FILL)
                s_ref[0, h, :, : pages * PAGE] = s
                top_ref[h] = fold(s, jnp.maximum)

        def scores(i, carry):
            keys = block(place(i), 4, 0)
            for h in range(qheads):
                s = mm(q_ref[:, columns(h)], keys, NT)
                s_ref[i + 1, h] = s
                top_ref[h] = jnp.maximum(top_ref[h], fold(s, jnp.maximum))
            return carry

        def weigh(h, s, values):
            top = jnp.concatenate([top_ref[h]] * (s.shape[1] // HD), axis=1)
            probs = jnp.exp2((s - top) * scale)
            return fold(probs, jnp.add), mm(probs.astype(jnp.bfloat16), values)

        def first_values(pages):
            rows = block(0, pages, 1)
            for h in range(qheads):
                total_ref[h], mixed_ref[h] = weigh(h, s_ref[0, h, :, : pages * PAGE], rows)

        def values(i, carry):
            rows = block(place(i), 4, 1)
            for h in range(qheads):
                total, mixed = weigh(h, s_ref[i + 1, h], rows)
                total_ref[h] += total
                mixed_ref[h] += mixed
            return carry

        def first_block(act):
            @pl.when(odd == 0)
            def _():
                act(2)

            @pl.when(odd == 1)
            def _():
                act(4)

        first_block(first_scores)
        lax.fori_loop(0, pairs // 2, scores, 0)
        for h in range(qheads):
            top_ref[h] = jnp.broadcast_to(jnp.max(top_ref[h], axis=1, keepdims=True), (SPAN, HD))
        first_block(first_values)
        lax.fori_loop(0, pairs // 2, values, 0)
        keep_row = lax.broadcasted_iota(jnp.int32, (SPAN, 1), 0) + start < live
        for h in range(qheads):
            total = jnp.sum(total_ref[h], axis=1, keepdims=True)
            out_ref[:, columns(h)] = jnp.where(keep_row, mixed_ref[h] / total, 0.0).astype(out_ref.dtype)

    @pl.when(start >= live)
    def _():
        out_ref[...] = jnp.zeros_like(out_ref)


def attention(qheads, first, here, pages, prefix, live, queries, keys, values, parts, carry):
    most = MAXP // 4 + 1
    width = qheads * HD
    if carry is None:
        carry = jnp.zeros((16, 128), jnp.bfloat16)
        aliases = {}
    else:
        aliases = {7 + len(parts): 0}

    def at(half, *_):
        return (first * 2 + half, 0)

    return pl.pallas_call(
        functools.partial(attend_kernel, qheads, (len(parts) + 2) // 4),
        grid_spec=pltpu.PrefetchScalarGridSpec(
            num_scalar_prefetch=4,
            grid=(2,),
            in_specs=[
                pl.BlockSpec((SPAN, width), at),
                pl.BlockSpec((SUF, HD), lambda *_: (first, 0)),
                pl.BlockSpec((SUF, HD), lambda *_: (first, 0)),
            ]
            + [IN_HBM] * len(parts)
            + [ANYWHERE],
            out_specs=pl.BlockSpec((SPAN, width), at),
            scratch_shapes=[
                pltpu.VMEM((MAXP + 2, 2, PAGE, HD), jnp.bfloat16),
                pltpu.VMEM((most, qheads, SPAN, 4 * PAGE), jnp.float32),
                pltpu.VMEM((qheads, SPAN, HD), jnp.float32),
                pltpu.VMEM((qheads, SPAN, HD), jnp.float32),
                pltpu.VMEM((qheads, SPAN, HD), jnp.float32),
                pltpu.SemaphoreType.DMA,
            ],
        ),
        out_shape=jax.ShapeDtypeStruct(queries.shape, jnp.bfloat16),
        input_output_aliases=aliases,
        compiler_params=pltpu.CompilerParams(vmem_limit_bytes=VMEM),
        cost_estimate=pl.CostEstimate(
            flops=qheads * SUF * (MAXP * PAGE + SUF) * HD * 4,
            bytes_accessed=SUF * qheads * HD * 4 + MAXP * PAGE * HD * 4,
            transcendentals=qheads * SUF * (MAXP * PAGE + SUF),
        ),
        name="attention",
    )(here, pages, prefix, live, queries, keys, values, *parts, carry)


def after(value, *others):
    return lax.optimization_barrier((value,) + others)[0]


def body(
    mixer_input,
    step_raw,
    decay_rate,
    skip_gain,
    state_proj,
    queries,
    suffix_kv,
    state_pool,
    page_pool,
    norm_gain,
    hit_owner,
    hit_slot,
    page_owner,
    page_slot,
    prefix_len,
    suffix_len,
):
    owners = lax.axis_size("owner")
    owner = lax.axis_index("owner").astype(jnp.int32)
    column = lax.axis_index("tensor")
    rows = mixer_input.shape[0]
    count = rows // SUF
    heads = decay_rate.shape[0]
    width = heads * MHDIM
    qheads = queries.shape[1] // HD
    per_group = SSM_HEAD_TOTAL // GROUPS
    group = column * heads // per_group
    kv_index = column * qheads // (QHEADS // KVHEADS)
    whole_group = heads == per_group
    chips = owners // 2
    per_chip = 2 * SLOTS_DEV
    states = owners * SLOTS_DEV
    here = owner.reshape(1)
    first = (owner * count).reshape(1)
    swap = [(o, o ^ 1) for o in range(owners)]

    def line(hop):
        up = [(o, o + 2) for o in range(0, owners - 2, 2) if o // 2 >= hop - 1]
        return up + [(o, o - 2) for o in range(3, owners, 2) if o // 2 <= chips - hop]

    def send(item, step):
        up = [(o, o + 2) for o in range(0, owners - 2, 2) if step >= HOP_STEPS * (o // 2)]
        down = [(o, o - 2) for o in range(3, owners, 2) if step >= HOP_STEPS * (chips - 1 - o // 2)]
        return lax.ppermute(item, "owner", up + down)

    def head_of(array, index, axis):
        return lax.dynamic_index_in_dim(array, index, axis, keepdims=False)

    pool = state_pool.reshape(SLOTS_DEV, width, STATE)
    near = lax.ppermute(pool, "owner", swap)
    own_pages = jnp.transpose(head_of(page_pool, kv_index, 3), (0, 2, 1, 3))
    near_pages = lax.ppermute(own_pages, "owner", swap)

    state_ids = (hit_owner[:, 0] * SLOTS_DEV + hit_slot).astype(jnp.int32)
    table, cap = route(after(state_ids, near_pages), owner, chips, per_chip, 2 * count)

    spread_np = np.zeros((128, width), np.float32)
    for h in range(heads):
        for k in range(3):
            spread_np[k * heads + h, h * MHDIM : (h + 1) * MHDIM] = 1.0
    spread = jnp.asarray(spread_np, jnp.bfloat16)
    split_np = np.zeros((2 * SPAN, 2 * SPAN), np.float32)
    for i in range(SPAN):
        split_np[i, 2 * i] = 1.0
        split_np[SPAN + i, 2 * i + 1] = 1.0
    split = jnp.asarray(split_np, jnp.bfloat16)
    skip = jnp.repeat(skip_gain, MHDIM)[None, :]
    decay = jnp.broadcast_to(decay_rate[:, None], (heads, SPAN))
    step_row = step_raw.T
    page_ids = (page_owner[:, :, 0] * PAGES_DEV + page_slot).astype(jnp.int32).reshape(-1)
    made = {}

    def shape_inputs(tie):
        maps = head_of(after(state_proj, tie), group, 2)
        made["b"], made["c"] = maps[:, 0], maps[:, 1]
        suffix = head_of(after(suffix_kv, tie), kv_index, 2)
        made["k"], made["v"] = suffix[:, 0], suffix[:, 1]
        return made["b"], made["k"]

    def pre_part(r):
        def run(tie):
            made["pre"] = mamba_pre(
                heads,
                r,
                2,
                suffix_len,
                after(first, tie),
                mixer_input,
                made["b"],
                made["c"],
                step_row,
                decay,
                skip,
                spread,
                split,
                made.get("pre"),
            )
            return (made["pre"][2],)

        return run

    def attention_part(r):
        def run(tie):
            place = jnp.concatenate([first + r, here])
            made["attn"] = attention(
                qheads,
                r,
                after(place, tie),
                page_ids,
                prefix_len,
                suffix_len,
                queries,
                made["k"],
                made["v"],
                made["parts"],
                made.get("attn"),
            )
            return (made["attn"],)

        return run

    def step_at(step):
        return jnp.full((1,), step, jnp.int32)

    beside = [shape_inputs] + [pre_part(r) for r in range(0, count, 2)]
    ours, theirs, came = [], [], []
    pieces = [own_pages, near_pages]
    for hop in range(1, chips):
        got = [lax.ppermute(piece, "owner", line(hop)) for piece in pieces]
        tie = pieces[1]
        if hop == 1:
            done = (table, near)
        else:
            step = HOP_STEPS * (hop - 2)
            items = take(states, HOP_STEPS, here, table, step_at(step), pool, near, came)
            items = [after(item, piece) for item, piece in zip(items, pieces)]
            came += [send(item, step + k) for k, item in enumerate(items)]
            tie = items[0]
            done = ()
        if beside:
            done += beside.pop(0)(tie)
        pieces = [after(piece, *done) for piece in got]
        ours += pieces
        theirs += [lax.ppermute(piece, "owner", swap) for piece in pieces]
    made["parts"] = [own_pages, near_pages] + ours + theirs

    beside += [attention_part(r) for r in range(count)]
    started = HOP_STEPS * (chips - 2)
    fixed = started + FREE_STEPS
    items = take(states, LAG, after(here, pieces[1]), table, step_at(started), pool, near, came)
    flying = [send(item, started + k) for k, item in enumerate(items)]
    tie = items[-1]
    for step in range(started + LAG, fixed):
        done = ()
        if (step - started) % 2 == 0 and beside:
            done = beside.pop(0)(tie)
        came.append(after(flying.pop(0), *done))
        (item,) = take(states, 1, here, table, step_at(step), pool, near, came)
        flying.append(send(item, step))
        tie = item
    done = ()
    while beside:
        done = beside.pop(0)(tie)
        tie = done[0]
    came.append(after(flying[0], *done))
    came.append(flying[1])

    def more(step, room):
        (item,) = take(states, 1, here, table, step.reshape(1), pool, near, came, room)
        return keep(fixed, step.reshape(1), send(item, fixed), room)

    room = blank(here, (cap - fixed,) + pool.shape[1:], pool.dtype)
    room = lax.fori_loop(fixed, table[2 * cap], more, room)

    picked = pick(states, cap, count, table, came, room)
    other = lax.ppermute(picked, "owner", swap)
    result = None
    for place in (after(here, picked), here):
        result = mamba_post(
            heads,
            whole_group,
            cap,
            states,
            place,
            table,
            suffix_len,
            pool,
            near,
            came,
            room,
            other,
            made["c"],
            *made["pre"],
            spread,
            norm_gain[None, :],
            result,
        )
    if whole_group:
        return (result[0], made["attn"])
    gated, partial_sum = result
    partial_sum = partial_sum[:, 0]
    spread_sum = jnp.where(jnp.arange(GROUPS)[:, None] == group, partial_sum[None, :], 0.0)
    totals = lax.psum(spread_sum, "tensor")
    square = lax.dynamic_index_in_dim(totals, group, 0, keepdims=False) / (per_group * MHDIM)
    my_suffix = lax.dynamic_slice_in_dim(suffix_len, first[0], count, 0)
    active = (jnp.arange(SUF)[None, :] < my_suffix[:, None]).reshape(-1)
    scaled = gated * lax.rsqrt(square + EPSILON)[:, None] * norm_gain[None, :]
    return (jnp.where(active[:, None], scaled, 0.0).astype(jnp.bfloat16), made["attn"])


def solution(mesh):
    return jax.shard_map(
        body,
        mesh=mesh,
        in_specs=(
            P("owner", None, "tensor"),
            P("owner", "tensor"),
            P("tensor"),
            P("tensor"),
            P("owner", None, None, None),
            P("owner", "tensor"),
            P("owner", None, None, None),
            P("owner", "tensor"),
            P("owner", None, None, None, None),
            P("tensor"),
            P(),
            P(),
            P(),
            P(),
            P(),
            P(),
        ),
        out_specs=(P("owner", "tensor"), P("owner", "tensor")),
        check_vma=False,
    )
```

```python
import functools
import math

import jax
import jax.numpy as jnp
import numpy as np
from jax import lax
from jax.experimental import pallas as pl
from jax.experimental.pallas import tpu as pltpu
from jax.sharding import PartitionSpec as P

SSM_HEAD_TOTAL = 128
MHDIM = 64
STATE = 256
GROUPS = 4
QHEADS = 32
KVHEADS = 4
HD = 128
PAGE = 128
SPAN = 128
SUF = 256
MAXP = 16
SLOTS_DEV = 4
PAGES_DEV = 16

EPSILON = 1e-05
NEG_FILL = -1e30
LAG = 2
HOP_STEPS = 2
FREE_STEPS = 7
VMEM = 48 * 1024 * 1024
SMALL_VMEM = 58 * 1024 * 1024

NT = (((1,), (1,)), ((), ()))
TN = (((0,), (0,)), ((), ()))


def mm(a, b, dims=(((1,), (0,)), ((), ()))):
    return lax.dot_general(a, b, dims, preferred_element_type=jnp.float32)


def route_kernel(chips, per_chip, reqs_per_chip, cap, ids_ref, here_ref, out_ref, need_ref, own_ref, tab_ref, code_ref):
    states = chips * per_chip
    chip_here = here_ref[0] // 2
    core_here = here_ref[0] % 2

    def clear(s, carry):
        need_ref[s] = 0
        return carry

    lax.fori_loop(0, states, clear, 0)

    def mark(r, carry):
        s = ids_ref[r]
        need_ref[s] = need_ref[s] | (1 << (r // reqs_per_chip))
        return carry

    lax.fori_loop(0, chips * reqs_per_chip, mark, 0)

    def put(base, length, row, from_ref):
        def one(t, carry):
            spot = jnp.clip(base + t, 0, 2 * chips * cap - 1)
            out_ref[row * cap + t] = jnp.where(t < length, from_ref[spot], states)
            return carry

        lax.fori_loop(0, cap, one, 0)

    steps = jnp.int32(0)
    for up in (True, False):
        before = jnp.int32(0)
        sent = jnp.int32(0)
        came = jnp.int32(0)
        for place in range(chips - 1):
            chip = place if up else chips - 1 - place
            base = ((0 if up else chips) + place) * cap

            def wanted(s, further=0, chip=chip, up=up):
                if up:
                    return (need_ref[s] >> (chip + 1 + further)) != 0
                return (need_ref[s] & ((1 << max(chip - further, 0)) - 1)) != 0

            count = jnp.int32(0)
            for far in (True, False):

                def own(i, n, far=far, chip=chip, wanted=wanted):
                    s = chip * per_chip + i
                    own_ref[n] = s
                    beyond = wanted(s, 1)
                    take = beyond if far else wanted(s) & jnp.logical_not(beyond)
                    return n + take.astype(jnp.int32)

                count = lax.fori_loop(0, per_chip, own, count)

            def fill(t, used, base=base, count=count):
                s = jnp.where(used < count, own_ref[used], states)
                tab_ref[base + t] = s
                code_ref[base + t] = s
                return jnp.minimum(used + 1, count)

            def forward(j, carry, base=base, wanted=wanted, fill=fill):
                t, used = carry
                s = tab_ref[base - cap + j]
                take = (s < states) & wanted(jnp.minimum(s, states - 1))
                later = jnp.where(take, jnp.maximum(t, j + LAG), t)
                used = lax.fori_loop(t, later, fill, used)
                tab_ref[base + later] = s
                code_ref[base + later] = states + 1 + j
                return later + take.astype(jnp.int32), used

            def idle(t, carry, base=base):
                tab_ref[base + t] = states
                code_ref[base + t] = states
                return carry

            lax.fori_loop(0, HOP_STEPS * place, idle, 0)
            t, used = jnp.int32(HOP_STEPS * place), jnp.int32(0)
            if place:
                t, used = lax.fori_loop(0, before, forward, (t, used))
            end = t + count - used
            lax.fori_loop(t, end, fill, used)
            before = end
            sent = jnp.where(chip_here == chip, end, sent)
            came = jnp.where(chip_here == (chip + 1 if up else chip - 1), end, came)
            steps = jnp.maximum(steps, end)
        here = chip_here if up else chips - 1 - chip_here
        side = 0 if up else chips

        @pl.when(core_here == (0 if up else 1))
        def _(here=here, side=side, sent=sent, came=came):
            put((side + here) * cap, sent, 0, code_ref)
            put((side + here - 1) * cap, came, 1, tab_ref)

        arrived = came if up else jnp.where(core_here == 0, arrived, came)

    out_ref[2 * cap] = steps
    mine = reqs_per_chip // 2
    asked = [here_ref[0] * mine + r for r in range(mine)] + [(here_ref[0] ^ 1) * mine + r for r in range(mine)]
    for k, request in enumerate(asked):
        state = ids_ref[request]
        out_ref[2 * cap + 3 + mine + k] = jnp.where(state // per_chip == chip_here, state, -1)

    def look(t, carry):
        came_now = out_ref[cap + t]
        for k, request in enumerate(asked):

            @pl.when(ids_ref[request] == came_now)
            def _(k=k):
                out_ref[2 * cap + 3 + mine + k] = states + 1 + t

        return carry

    lax.fori_loop(0, arrived, look, 0)
    found = jnp.int32(0)
    for here_now in (True, False):
        for r in range(mine):
            out_ref[2 * cap + 2 + found] = r
            found += ((out_ref[2 * cap + 3 + mine + r] >= 0) == here_now).astype(jnp.int32)
        if here_now:
            out_ref[2 * cap + 1] = found


def route(state_ids, owner, chips, per_chip, reqs_per_chip):
    cap = chips * per_chip + (LAG + HOP_STEPS) * chips + 8
    smem = pl.BlockSpec(memory_space=pltpu.SMEM)
    table = pl.pallas_call(
        functools.partial(route_kernel, chips, per_chip, reqs_per_chip, cap),
        out_shape=jax.ShapeDtypeStruct((2 * cap + 4 + 2 * reqs_per_chip,), jnp.int32),
        in_specs=[smem, smem],
        out_specs=smem,
        scratch_shapes=[
            pltpu.SMEM((chips * per_chip,), jnp.int32),
            pltpu.SMEM((2 * per_chip,), jnp.int32),
            pltpu.SMEM((2 * chips * cap,), jnp.int32),
            pltpu.SMEM((2 * chips * cap,), jnp.int32),
        ],
        name="route_states",
    )(state_ids, owner.reshape(1))
    return table, cap


ANYWHERE = pl.BlockSpec(memory_space=pl.ANY)
IN_HBM = pl.BlockSpec(memory_space=pltpu.HBM)
PIECES = 4


def piece_of(ref, k):
    rows = ref.shape[0] // PIECES
    return ref.at[pl.ds(k * rows, rows)]


def start_from(code, states, owner, pool_ref, near_ref, came_refs, late_ref, dst, sems):
    def start(ref):
        for k in range(PIECES):
            pltpu.make_async_copy(piece_of(ref, k), piece_of(dst, k), sems.at[k]).start()

    if pool_ref is not None:
        own = (code >= 0) & (code < states)
        slot = code % SLOTS_DEV

        @pl.when(own & (code // SLOTS_DEV == owner))
        def _():
            start(pool_ref.at[slot])

        @pl.when(own & (code // SLOTS_DEV != owner))
        def _():
            start(near_ref.at[slot])

    step = code - states - 1
    for k, ref in enumerate(came_refs):

        @pl.when(step == k)
        def _(ref=ref):
            start(ref)

    if late_ref is not None:

        @pl.when(step >= len(came_refs))
        def _():
            start(late_ref.at[step - len(came_refs)])


def pass_on(src, dst, sems):
    for k in range(PIECES):
        pltpu.make_async_copy(piece_of(dst, k), piece_of(src, k), sems.at[k]).wait()
        pltpu.make_async_copy(piece_of(src, k), piece_of(dst, k), sems.at[k]).start()


def finish(src, dst, sems):
    for k in range(PIECES):
        pltpu.make_async_copy(piece_of(src, k), piece_of(dst, k), sems.at[k]).wait()


def each_step(refs):
    return [part for ref in refs for part in ([ref.at[k] for k in range(ref.shape[0])] if len(ref.shape) == 3 else [ref])]


def take_kernel(states, steps, late, here_ref, table_ref, step_ref, pool_ref, near_ref, *rest):
    send_ref, item_ref, sem = rest[-3:]
    sends = each_step([send_ref])
    came_refs = rest[:-3]
    late_ref = None
    if late:
        came_refs, late_ref = came_refs[:-1], came_refs[-1]
    came_refs = each_step(came_refs)
    codes = [table_ref[step_ref[0] + t] for t in range(steps)]
    for t in range(steps):
        start_from(
            codes[t], states, here_ref[0], pool_ref, near_ref, came_refs, late_ref, item_ref.at[t], sem.at[t]
        )
    for act in (pass_on, finish):
        for t in range(steps):

            @pl.when(codes[t] != states)
            def _(t=t):
                act(item_ref.at[t], sends[t], sem.at[t])


def take(states, steps, here, table, step, pool, near, came, late=None):
    shape = pool.shape[1:] if steps == 1 else (steps,) + pool.shape[1:]
    came = list(came) + ([] if late is None else [late])
    return pl.pallas_call(
        functools.partial(take_kernel, states, steps, late is not None),
        grid_spec=pltpu.PrefetchScalarGridSpec(
            num_scalar_prefetch=3,
            grid=(1,),
            in_specs=[IN_HBM] * (2 + len(came)),
            out_specs=IN_HBM,
            scratch_shapes=[
                pltpu.VMEM((steps,) + pool.shape[1:], pool.dtype),
                pltpu.SemaphoreType.DMA((steps, PIECES)),
            ],
        ),
        out_shape=jax.ShapeDtypeStruct(shape, pool.dtype),
        compiler_params=pltpu.CompilerParams(vmem_limit_bytes=SMALL_VMEM),
        name="take_states",
    )(here, table, step, pool, near, *came)


def keep_kernel(fixed, step_ref, got_ref, _late_in, late_ref, item_ref, sem):
    spot = late_ref.at[step_ref[0] - fixed]
    for k in range(PIECES):
        pltpu.make_async_copy(piece_of(got_ref, k), piece_of(item_ref, k), sem.at[k]).start()
    pass_on(item_ref, spot, sem)
    finish(item_ref, spot, sem)


def keep(fixed, step, got, late):
    return pl.pallas_call(
        functools.partial(keep_kernel, fixed),
        grid_spec=pltpu.PrefetchScalarGridSpec(
            num_scalar_prefetch=1,
            grid=(1,),
            in_specs=[IN_HBM, IN_HBM],
            out_specs=IN_HBM,
            scratch_shapes=[pltpu.VMEM(got.shape, got.dtype), pltpu.SemaphoreType.DMA((PIECES,))],
        ),
        out_shape=jax.ShapeDtypeStruct(late.shape, late.dtype),
        input_output_aliases={2: 0},
        compiler_params=pltpu.CompilerParams(vmem_limit_bytes=SMALL_VMEM),
        name="keep_state",
    )(step, got, late)


def blank_kernel(here_ref, out_ref):
    pass


def blank(here, shape, dtype):
    return pl.pallas_call(
        blank_kernel,
        in_specs=[pl.BlockSpec(memory_space=pltpu.SMEM)],
        out_specs=IN_HBM,
        out_shape=jax.ShapeDtypeStruct(shape, dtype),
        compiler_params=pltpu.CompilerParams(vmem_limit_bytes=SMALL_VMEM),
        name="room",
    )(here)


def pick_kernel(states, cap, count, table_ref, *rest):
    came_refs, late_ref = each_step(rest[:-4]), rest[-4]
    out_ref, item_ref, sem = rest[-3:]
    codes = [table_ref[2 * cap + 3 + 2 * count + r] for r in range(count)]
    for r in range(count):

        @pl.when(codes[r] > states)
        def _(r=r):
            start_from(codes[r], states, -1, None, None, came_refs, late_ref, item_ref.at[r], sem.at[r])

    for act in (pass_on, finish):
        for r in range(count):

            @pl.when(codes[r] > states)
            def _(r=r):
                act(item_ref.at[r], out_ref.at[r], sem.at[r])


def pick(states, cap, count, table, came, late):
    shape = (count,) + late.shape[1:]
    return pl.pallas_call(
        functools.partial(pick_kernel, states, cap, count),
        grid_spec=pltpu.PrefetchScalarGridSpec(
            num_scalar_prefetch=1,
            grid=(1,),
            in_specs=[IN_HBM] * (len(came) + 1),
            out_specs=IN_HBM,
            scratch_shapes=[
                pltpu.VMEM(shape, late.dtype),
                pltpu.SemaphoreType.DMA((count, PIECES)),
            ],
        ),
        out_shape=jax.ShapeDtypeStruct(shape, late.dtype),
        compiler_params=pltpu.CompilerParams(vmem_limit_bytes=SMALL_VMEM),
        name="pick_states",
    )(table, *came, late)


def mamba_pre_kernel(
    heads,
    live_ref,
    first_ref,
    mix_ref,
    b_ref,
    c_ref,
    step_ref,
    decay_ref,
    skip_ref,
    spread_ref,
    split_ref,
    _pre_in,
    _z_in,
    _e_in,
    pre_ref,
    z_ref,
    e_ref,
    bs_ref,
    end_ref,
):
    block = pl.program_id(1)
    request = first_ref[0] + pl.program_id(0)
    copies = SPAN // heads
    row = lax.broadcasted_iota(jnp.int32, (SPAN, SPAN), 0)
    lane = lax.broadcasted_iota(jnp.int32, (SPAN, SPAN), 1)
    lower = row >= lane
    left = lane < MHDIM

    def three_way(value):
        high = value.astype(jnp.bfloat16)
        rest = value - high.astype(jnp.float32)
        middle = rest.astype(jnp.bfloat16)
        low = (rest - middle.astype(jnp.float32)).astype(jnp.bfloat16)
        high, middle, low = (v.astype(jnp.float32) for v in (high, middle, low))
        kept = jnp.where(
            lane < heads,
            high,
            jnp.where(lane < 2 * heads, middle, jnp.where(lane < 3 * heads, low, 0.0)),
        )
        return kept.astype(jnp.bfloat16)

    @pl.when((block == 0) | (live_ref[request] > SPAN))
    def _():
        raw = step_ref[...]
        rate_row = jnp.maximum(raw, 0.0) + jnp.log1p(jnp.exp(-jnp.abs(raw)))
        upper = jnp.where(row <= lane, 1.0, 0.0)
        cum_row = lax.dot_general(
            -rate_row * decay_ref[...],
            upper,
            (((1,), (0,)), ((), ())),
            precision=lax.Precision.HIGHEST,
            preferred_element_type=jnp.float32,
        )
        cum = jnp.concatenate([cum_row] * copies, axis=0).T
        rate_col = jnp.concatenate([rate_row] * copies, axis=0).T

        both = mm(split_ref[...], mix_ref[...].reshape(2 * SPAN, heads * MHDIM))
        z_ref[...] = both[SPAN:].astype(jnp.bfloat16)
        x = both[:SPAN]
        x_half = x.astype(jnp.bfloat16)
        b = b_ref[...]
        c = c_ref[...]
        cross = mm(c, b, NT)

        def weights(h):
            fall = cum[:, h : h + 1] - cum_row[h : h + 1, :]
            fade = jnp.exp(jnp.where(lower, fall, NEG_FILL))
            return (cross * fade * rate_row[h : h + 1, :]).astype(jnp.bfloat16)

        for pair in range(heads // 2):
            cols = slice(pair * 2 * MHDIM, (pair + 1) * 2 * MHDIM)
            xp = x_half[:, cols]
            zero = jnp.zeros_like(xp)
            stacked = jnp.concatenate([jnp.where(left, xp, zero), jnp.where(left, zero, xp)], axis=0)
            w = jnp.concatenate([weights(2 * pair), weights(2 * pair + 1)], axis=1)
            pre_ref[:, cols] = mm(w, stacked) + skip_ref[:, cols] * x[:, cols]

        @pl.when(block == 0)
        def _():
            end = cum[SPAN - 1 : SPAN, :]
            tail = jnp.exp(end - cum) * rate_col
            scaled = (mm(three_way(tail), spread_ref[...]) * x).astype(jnp.bfloat16)
            bs_ref[...] = mm(scaled, b, TN).astype(jnp.bfloat16)
            end_ref[...] = jnp.broadcast_to(end, end_ref.shape)
            e_ref[...] = three_way(jnp.exp(cum))

        @pl.when(block == 1)
        def _():
            e_half = three_way(jnp.exp(cum))
            carried = mm(c, bs_ref[...], NT)
            pre_ref[...] += mm(e_half, spread_ref[...]) * carried
            e_ref[...] = three_way(jnp.exp(cum + end_ref[0:1, :]))


def mamba_pre(heads, first, count, live, here, mixed, b_rows, c_rows, step_row, decay, skip, spread, split, carry):
    width = heads * MHDIM
    rows = b_rows.shape[0]

    def at(r, k, *_):
        return ((first + r) * 2 + k, 0)

    def fixed(r, k, *_):
        return (0, 0)

    blocks = count * 2
    outs = [
        jax.ShapeDtypeStruct((rows, width), jnp.float32),
        jax.ShapeDtypeStruct((rows, width), jnp.bfloat16),
        jax.ShapeDtypeStruct((rows, 128), jnp.bfloat16),
    ]
    if carry is None:
        carry = tuple(jnp.zeros((16, 128), jnp.float32) for _ in outs)
        aliases = {}
    else:
        aliases = {10: 0, 11: 1, 12: 2}
    return pl.pallas_call(
        functools.partial(mamba_pre_kernel, heads),
        grid_spec=pltpu.PrefetchScalarGridSpec(
            num_scalar_prefetch=2,
            grid=(count, 2),
            in_specs=[
                pl.BlockSpec((SPAN, 2, width), lambda r, k, *_: ((first + r) * 2 + k, 0, 0)),
                pl.BlockSpec((SPAN, STATE), at),
                pl.BlockSpec((SPAN, STATE), at),
                pl.BlockSpec((heads, SPAN), lambda r, k, *_: (0, (first + r) * 2 + k)),
                pl.BlockSpec((heads, SPAN), fixed),
                pl.BlockSpec((1, width), fixed),
                pl.BlockSpec((128, width), fixed),
                pl.BlockSpec((2 * SPAN, 2 * SPAN), fixed),
                ANYWHERE,
                ANYWHERE,
                ANYWHERE,
            ],
            out_specs=[
                pl.BlockSpec((SPAN, width), at),
                pl.BlockSpec((SPAN, width), at),
                pl.BlockSpec((SPAN, 128), at),
            ],
            scratch_shapes=[
                pltpu.VMEM((width, STATE), jnp.bfloat16),
                pltpu.VMEM((8, 128), jnp.float32),
            ],
        ),
        out_shape=outs,
        input_output_aliases=aliases,
        compiler_params=pltpu.CompilerParams(vmem_limit_bytes=VMEM),
        cost_estimate=pl.CostEstimate(
            flops=blocks * heads * 40 * SPAN * SPAN * MHDIM,
            bytes_accessed=blocks * SPAN * width * 10,
            transcendentals=blocks * heads * SPAN * SPAN,
        ),
        name="mamba_pre",
    )(live, here + first, mixed, b_rows, c_rows, step_row, decay, skip, spread, split, *carry)


def mamba_post_kernel(
    heads,
    whole_group,
    count,
    cap,
    states,
    fixed,
    late,
    here_ref,
    table_ref,
    live_ref,
    *rest,
):
    outs = 1 if whole_group else 2
    pool_ref, near_ref, *came_refs, late_ref, other_ref = rest[: fixed + 4]
    came_refs = each_step(came_refs)
    c_ref, pre_ref, z_ref, e_ref, spread_ref, gain_ref, *rest = rest[fixed + 4 :]
    out_refs = rest[outs : 2 * outs]
    stage_refs = rest[2 * outs : 3 * outs]
    state_ref, sem, out_sem = rest[-3:]
    i = pl.program_id(0)
    width = heads * MHDIM
    owner = here_ref[0]
    here_now = table_ref[2 * cap + 1]
    active = count - here_now if late else here_now

    def put(i, r):
        rows = pl.ds(pl.multiple_of(r * SUF, SUF), SUF)
        return [
            pltpu.make_async_copy(stage.at[i % 2], out.at[rows], out_sem.at[k, i % 2])
            for k, (stage, out) in enumerate(zip(stage_refs, out_refs))
        ]

    def fetch(i):
        r = post_request(cap, count, late, i, table_ref)
        code = table_ref[2 * cap + 3 + count + r]
        slot = i % 2
        start_from(
            code, states, owner, pool_ref, near_ref, came_refs, late_ref, state_ref.at[slot], sem.at[slot]
        )
        if late:

            @pl.when(code < 0)
            def _():
                for k in range(PIECES):
                    pltpu.make_async_copy(
                        piece_of(other_ref.at[r], k), piece_of(state_ref.at[slot], k), sem.at[slot, k]
                    ).start()

    @pl.when((i == 0) & (i < active))
    def _():
        fetch(i)

    @pl.when(i + 1 < active)
    def _():
        fetch(i + 1)

    @pl.when(i < active)
    def _():
        r = post_request(cap, count, late, i, table_ref)
        finish(pool_ref.at[0], state_ref.at[i % 2], sem.at[i % 2])
        carried = mm(c_ref[...], state_ref[i % 2], NT)
        summed = pre_ref[...] + mm(e_ref[...], spread_ref[...]) * carried
        z = z_ref[...].astype(jnp.float32)
        gated = summed * (z / (1.0 + jnp.exp(-z)))
        square = jnp.sum(gated * gated, axis=1, keepdims=True)

        @pl.when(i >= 2)
        def _():
            for copy in put(i, 0):
                copy.wait()

        if whole_group:
            norm = lax.rsqrt(square / width + EPSILON)
            live = lax.broadcasted_iota(jnp.int32, (SUF, 1), 0) < live_ref[owner * count + r]
            stage_refs[0][i % 2] = jnp.where(live, gated * norm * gain_ref[...], 0.0).astype(jnp.bfloat16)
        else:
            stage_refs[0][i % 2] = gated
            stage_refs[1][i % 2] = jnp.broadcast_to(square, (SUF, 128))
        for copy in put(i, r):
            copy.start()

        @pl.when(i == active - 1)
        def _():
            for copy in put(i, 0):
                copy.wait()

            @pl.when(i >= 1)
            def _():
                for copy in put(i - 1, 0):
                    copy.wait()


def post_request(cap, count, late, i, table_ref):
    here_now = table_ref[2 * cap + 1]
    if late:
        spot = here_now + jnp.minimum(i, jnp.maximum(count - here_now - 1, 0))
    else:
        spot = jnp.minimum(i, jnp.maximum(here_now - 1, 0))
    return table_ref[2 * cap + 2 + jnp.minimum(spot, count - 1)]


def mamba_post(
    heads, whole_group, cap, states, here, table, live, pool, near, came, late_room, other, c_rows, pre, z, e3, spread, gain, carry
):
    width = heads * MHDIM
    rows = c_rows.shape[0]
    count = rows // SUF
    late = carry is not None
    held = len(came)

    def at(i, here_ref, table_ref, *_):
        return (post_request(cap, count, late, i, table_ref), 0)

    def fixed(i, *_):
        return (0, 0)

    out_shape = [jax.ShapeDtypeStruct((rows, width), jnp.bfloat16 if whole_group else jnp.float32)]
    if not whole_group:
        out_shape.append(jax.ShapeDtypeStruct((rows, 128), jnp.float32))
    aliases = {}
    if late:
        aliases = {3 + held + 10 + k: k for k in range(len(out_shape))}
    else:
        carry = [jnp.zeros((16, 128), jnp.float32)] * len(out_shape)
        other = late_room
    return pl.pallas_call(
        functools.partial(mamba_post_kernel, heads, whole_group, count, cap, states, held, late),
        grid_spec=pltpu.PrefetchScalarGridSpec(
            num_scalar_prefetch=3,
            grid=(count,),
            in_specs=[IN_HBM] * (held + 4)
            + [
                pl.BlockSpec((SUF, STATE), at),
                pl.BlockSpec((SUF, width), at),
                pl.BlockSpec((SUF, width), at),
                pl.BlockSpec((SUF, 128), at),
                pl.BlockSpec((128, width), fixed),
                pl.BlockSpec((1, width), fixed),
            ]
            + [ANYWHERE] * len(out_shape),
            out_specs=[IN_HBM] * len(out_shape),
            scratch_shapes=[pltpu.VMEM((2, SUF) + out.shape[1:], out.dtype) for out in out_shape]
            + [
                pltpu.VMEM((2, width, STATE), jnp.bfloat16),
                pltpu.SemaphoreType.DMA((2, PIECES)),
                pltpu.SemaphoreType.DMA((len(out_shape), 2)),
            ],
        ),
        out_shape=out_shape,
        input_output_aliases=aliases,
        compiler_params=pltpu.CompilerParams(vmem_limit_bytes=VMEM),
        cost_estimate=pl.CostEstimate(
            flops=2 * rows * width * STATE,
            bytes_accessed=rows * width * 6,
            transcendentals=rows * width,
        ),
        name="mamba_post",
    )(here, table, live, pool, near, *came, late_room, other, c_rows, pre, z, e3, spread, gain, *carry)


def attend_kernel(
    qheads,
    chips,
    first_ref,
    pages_ref,
    prefix_ref,
    live_ref,
    q_ref,
    ks_ref,
    vs_ref,
    *rest,
):
    parts = rest[: 4 * chips - 2]
    out_ref, kv_ref, s_ref, top_ref, total_ref, mixed_ref, sem = rest[4 * chips - 1 :]
    request = first_ref[0]
    owner = first_ref[1]
    scale = math.log2(math.e) / math.sqrt(HD)
    pairs = prefix_ref[request] // (2 * PAGE)
    half = pl.program_id(0)
    start = half * SPAN
    live = live_ref[request]

    def columns(h):
        return slice(h * HD, (h + 1) * HD)

    @pl.when(half == 0)
    def _():
        def begin(p, carry):
            page = pages_ref[request * MAXP + p]
            giver = page // PAGES_DEV
            core = owner % 2
            away = giver // 2 - owner // 2
            ahead = jnp.where(core == 0, -away, away)
            which = jnp.where(ahead >= 0, ahead, chips - 1 - ahead)
            carrier = jnp.where(ahead >= 0, core, 1 - core)
            which = 2 * which + ((giver % 2) ^ carrier)
            spot = page % PAGES_DEV

            def fetch(low, high):
                if high - low == 1:
                    pltpu.make_async_copy(parts[low].at[spot], kv_ref.at[p + 2], sem).start()
                    return
                middle = (low + high) // 2

                @pl.when(which < middle)
                def _():
                    fetch(low, middle)

                @pl.when(which >= middle)
                def _():
                    fetch(middle, high)

            fetch(0, len(parts))
            return carry

        def end(p, carry):
            pltpu.make_async_copy(parts[0].at[0], kv_ref.at[p + 2], sem).wait()
            return carry

        lax.fori_loop(0, 2 * pairs, begin, 0)
        for page in range(2):
            at = slice(page * PAGE, (page + 1) * PAGE)
            kv_ref[page, 0] = ks_ref[at, :]
            kv_ref[page, 1] = vs_ref[at, :]
        lax.fori_loop(0, 2 * pairs, end, 0)

    @pl.when(start < live)
    def _():
        odd = pairs % 2

        def block(first, pages, kv):
            return kv_ref[pl.ds(first, pages), kv].reshape(pages * PAGE, HD)

        def place(i):
            return 2 + 2 * odd + 4 * i

        def fold(s, act):
            return functools.reduce(act, [s[:, k : k + HD] for k in range(0, s.shape[1], HD)])

        def first_scores(pages):
            keys = block(0, pages, 0)
            row = lax.broadcasted_iota(jnp.int32, (SPAN, pages * PAGE), 0) + start
            lane = lax.broadcasted_iota(jnp.int32, (SPAN, pages * PAGE), 1)
            allowed = (row >= lane) | (lane >= SUF)
            for h in range(qheads):
                s = jnp.where(allowed, mm(q_ref[:, columns(h)], keys, NT), NEG_FILL)
                s_ref[0, h, :, : pages * PAGE] = s
                top_ref[h] = fold(s, jnp.maximum)

        def scores(i, carry):
            keys = block(place(i), 4, 0)
            for h in range(qheads):
                s = mm(q_ref[:, columns(h)], keys, NT)
                s_ref[i + 1, h] = s
                top_ref[h] = jnp.maximum(top_ref[h], fold(s, jnp.maximum))
            return carry

        def weigh(h, s, values):
            top = jnp.concatenate([top_ref[h]] * (s.shape[1] // HD), axis=1)
            probs = jnp.exp2((s - top) * scale)
            return fold(probs, jnp.add), mm(probs.astype(jnp.bfloat16), values)

        def first_values(pages):
            rows = block(0, pages, 1)
            for h in range(qheads):
                total_ref[h], mixed_ref[h] = weigh(h, s_ref[0, h, :, : pages * PAGE], rows)

        def values(i, carry):
            rows = block(place(i), 4, 1)
            for h in range(qheads):
                total, mixed = weigh(h, s_ref[i + 1, h], rows)
                total_ref[h] += total
                mixed_ref[h] += mixed
            return carry

        def first_block(act):
            @pl.when(odd == 0)
            def _():
                act(2)

            @pl.when(odd == 1)
            def _():
                act(4)

        first_block(first_scores)
        lax.fori_loop(0, pairs // 2, scores, 0)
        for h in range(qheads):
            top_ref[h] = jnp.broadcast_to(jnp.max(top_ref[h], axis=1, keepdims=True), (SPAN, HD))
        first_block(first_values)
        lax.fori_loop(0, pairs // 2, values, 0)
        keep_row = lax.broadcasted_iota(jnp.int32, (SPAN, 1), 0) + start < live
        for h in range(qheads):
            total = jnp.sum(total_ref[h], axis=1, keepdims=True)
            out_ref[:, columns(h)] = jnp.where(keep_row, mixed_ref[h] / total, 0.0).astype(out_ref.dtype)

    @pl.when(start >= live)
    def _():
        out_ref[...] = jnp.zeros_like(out_ref)


def attention(qheads, first, here, pages, prefix, live, queries, keys, values, parts, carry):
    most = MAXP // 4 + 1
    width = qheads * HD
    if carry is None:
        carry = jnp.zeros((16, 128), jnp.bfloat16)
        aliases = {}
    else:
        aliases = {7 + len(parts): 0}

    def at(half, *_):
        return (first * 2 + half, 0)

    return pl.pallas_call(
        functools.partial(attend_kernel, qheads, (len(parts) + 2) // 4),
        grid_spec=pltpu.PrefetchScalarGridSpec(
            num_scalar_prefetch=4,
            grid=(2,),
            in_specs=[
                pl.BlockSpec((SPAN, width), at),
                pl.BlockSpec((SUF, HD), lambda *_: (first, 0)),
                pl.BlockSpec((SUF, HD), lambda *_: (first, 0)),
            ]
            + [IN_HBM] * len(parts)
            + [ANYWHERE],
            out_specs=pl.BlockSpec((SPAN, width), at),
            scratch_shapes=[
                pltpu.VMEM((MAXP + 2, 2, PAGE, HD), jnp.bfloat16),
                pltpu.VMEM((most, qheads, SPAN, 4 * PAGE), jnp.float32),
                pltpu.VMEM((qheads, SPAN, HD), jnp.float32),
                pltpu.VMEM((qheads, SPAN, HD), jnp.float32),
                pltpu.VMEM((qheads, SPAN, HD), jnp.float32),
                pltpu.SemaphoreType.DMA,
            ],
        ),
        out_shape=jax.ShapeDtypeStruct(queries.shape, jnp.bfloat16),
        input_output_aliases=aliases,
        compiler_params=pltpu.CompilerParams(vmem_limit_bytes=VMEM),
        cost_estimate=pl.CostEstimate(
            flops=qheads * SUF * (MAXP * PAGE + SUF) * HD * 4,
            bytes_accessed=SUF * qheads * HD * 4 + MAXP * PAGE * HD * 4,
            transcendentals=qheads * SUF * (MAXP * PAGE + SUF),
        ),
        name="attention",
    )(here, pages, prefix, live, queries, keys, values, *parts, carry)


def after(value, *others):
    return lax.optimization_barrier((value,) + others)[0]


def body(
    mixer_input,
    step_raw,
    decay_rate,
    skip_gain,
    state_proj,
    queries,
    suffix_kv,
    state_pool,
    page_pool,
    norm_gain,
    hit_owner,
    hit_slot,
    page_owner,
    page_slot,
    prefix_len,
    suffix_len,
):
    owners = lax.axis_size("owner")
    owner = lax.axis_index("owner").astype(jnp.int32)
    column = lax.axis_index("tensor")
    rows = mixer_input.shape[0]
    count = rows // SUF
    heads = decay_rate.shape[0]
    width = heads * MHDIM
    qheads = queries.shape[1] // HD
    per_group = SSM_HEAD_TOTAL // GROUPS
    group = column * heads // per_group
    kv_index = column * qheads // (QHEADS // KVHEADS)
    whole_group = heads == per_group
    chips = owners // 2
    per_chip = 2 * SLOTS_DEV
    states = owners * SLOTS_DEV
    here = owner.reshape(1)
    first = (owner * count).reshape(1)
    swap = [(o, o ^ 1) for o in range(owners)]

    def line(hop):
        up = [(o, o + 2) for o in range(0, owners - 2, 2) if o // 2 >= hop - 1]
        return up + [(o, o - 2) for o in range(3, owners, 2) if o // 2 <= chips - hop]

    def send(item, step):
        up = [(o, o + 2) for o in range(0, owners - 2, 2) if step >= HOP_STEPS * (o // 2)]
        down = [(o, o - 2) for o in range(3, owners, 2) if step >= HOP_STEPS * (chips - 1 - o // 2)]
        return lax.ppermute(item, "owner", up + down)

    def head_of(array, index, axis):
        return lax.dynamic_index_in_dim(array, index, axis, keepdims=False)

    pool = state_pool.reshape(SLOTS_DEV, width, STATE)
    near = lax.ppermute(pool, "owner", swap)
    own_pages = jnp.transpose(head_of(page_pool, kv_index, 3), (0, 2, 1, 3))
    near_pages = lax.ppermute(own_pages, "owner", swap)

    state_ids = (hit_owner[:, 0] * SLOTS_DEV + hit_slot).astype(jnp.int32)
    table, cap = route(after(state_ids, near_pages), owner, chips, per_chip, 2 * count)

    spread_np = np.zeros((128, width), np.float32)
    for h in range(heads):
        for k in range(3):
            spread_np[k * heads + h, h * MHDIM : (h + 1) * MHDIM] = 1.0
    spread = jnp.asarray(spread_np, jnp.bfloat16)
    split_np = np.zeros((2 * SPAN, 2 * SPAN), np.float32)
    for i in range(SPAN):
        split_np[i, 2 * i] = 1.0
        split_np[SPAN + i, 2 * i + 1] = 1.0
    split = jnp.asarray(split_np, jnp.bfloat16)
    skip = jnp.repeat(skip_gain, MHDIM)[None, :]
    decay = jnp.broadcast_to(decay_rate[:, None], (heads, SPAN))
    step_row = step_raw.T
    page_ids = (page_owner[:, :, 0] * PAGES_DEV + page_slot).astype(jnp.int32).reshape(-1)
    made = {}

    def shape_inputs(tie):
        maps = head_of(after(state_proj, tie), group, 2)
        made["b"], made["c"] = maps[:, 0], maps[:, 1]
        suffix = head_of(after(suffix_kv, tie), kv_index, 2)
        made["k"], made["v"] = suffix[:, 0], suffix[:, 1]
        return made["b"], made["k"]

    def pre_part(r):
        def run(tie):
            made["pre"] = mamba_pre(
                heads,
                r,
                2,
                suffix_len,
                after(first, tie),
                mixer_input,
                made["b"],
                made["c"],
                step_row,
                decay,
                skip,
                spread,
                split,
                made.get("pre"),
            )
            return (made["pre"][2],)

        return run

    def attention_part(r):
        def run(tie):
            place = jnp.concatenate([first + r, here])
            made["attn"] = attention(
                qheads,
                r,
                after(place, tie),
                page_ids,
                prefix_len,
                suffix_len,
                queries,
                made["k"],
                made["v"],
                made["parts"],
                made.get("attn"),
            )
            return (made["attn"],)

        return run

    def step_at(step):
        return jnp.full((1,), step, jnp.int32)

    beside = [shape_inputs] + [pre_part(r) for r in range(0, count, 2)]
    ours, theirs, came = [], [], []
    pieces = [own_pages, near_pages]
    for hop in range(1, chips):
        got = [lax.ppermute(piece, "owner", line(hop)) for piece in pieces]
        tie = pieces[1]
        if hop == 1:
            done = (table, near)
        else:
            step = HOP_STEPS * (hop - 2)
            tie = after(take(states, HOP_STEPS, here, table, step_at(step), pool, near, came), pieces[0])
            came.append(send(tie, step))
            done = ()
        if beside:
            done += beside.pop(0)(tie)
        pieces = [after(piece, *done) for piece in got]
        ours += pieces
        theirs += [lax.ppermute(piece, "owner", swap) for piece in pieces]
    made["parts"] = [own_pages, near_pages] + ours + theirs

    beside += [attention_part(r) for r in range(count)]
    started = HOP_STEPS * (chips - 2)
    fixed = started + FREE_STEPS
    flying = []
    for step in range(started, started + LAG):
        tie = take(states, 1, after(here, pieces[1]), table, step_at(step), pool, near, came)
        flying.append(send(tie, step))
    for step in range(started + LAG, fixed):
        done = ()
        if (step - started) % 2 == 0 and beside:
            done = beside.pop(0)(tie)
        came.append(after(flying.pop(0), *done))
        item = take(states, 1, here, table, step_at(step), pool, near, came)
        flying.append(send(item, step))
        tie = item
    done = ()
    while beside:
        done = beside.pop(0)(tie)
        tie = done[0]
    came.append(after(flying[0], *done))
    came.append(flying[1])

    def more(step, room):
        item = take(states, 1, here, table, step.reshape(1), pool, near, came, room)
        return keep(fixed, step.reshape(1), send(item, fixed), room)

    room = blank(here, (cap - fixed,) + pool.shape[1:], pool.dtype)
    room = lax.fori_loop(fixed, table[2 * cap], more, room)

    picked = pick(states, cap, count, table, came, room)
    other = lax.ppermute(picked, "owner", swap)
    result = None
    for place in (after(here, picked), here):
        result = mamba_post(
            heads,
            whole_group,
            cap,
            states,
            place,
            table,
            suffix_len,
            pool,
            near,
            came,
            room,
            other,
            made["c"],
            *made["pre"],
            spread,
            norm_gain[None, :],
            result,
        )
    if whole_group:
        return (result[0], made["attn"])
    gated, partial_sum = result
    partial_sum = partial_sum[:, 0]
    spread_sum = jnp.where(jnp.arange(GROUPS)[:, None] == group, partial_sum[None, :], 0.0)
    totals = lax.psum(spread_sum, "tensor")
    square = lax.dynamic_index_in_dim(totals, group, 0, keepdims=False) / (per_group * MHDIM)
    my_suffix = lax.dynamic_slice_in_dim(suffix_len, first[0], count, 0)
    active = (jnp.arange(SUF)[None, :] < my_suffix[:, None]).reshape(-1)
    scaled = gated * lax.rsqrt(square + EPSILON)[:, None] * norm_gain[None, :]
    return (jnp.where(active[:, None], scaled, 0.0).astype(jnp.bfloat16), made["attn"])


def solution(mesh):
    return jax.shard_map(
        body,
        mesh=mesh,
        in_specs=(
            P("owner", None, "tensor"),
            P("owner", "tensor"),
            P("tensor"),
            P("tensor"),
            P("owner", None, None, None),
            P("owner", "tensor"),
            P("owner", None, None, None),
            P("owner", "tensor"),
            P("owner", None, None, None, None),
            P("tensor"),
            P(),
            P(),
            P(),
            P(),
            P(),
            P(),
        ),
        out_specs=(P("owner", "tensor"), P("owner", "tensor")),
        check_vma=False,
    )
```
